128 devices in a mesh: owner: 16 (over z, y), sub: 8 (over x, core).
Axes of the slice: x: 4, y: 4, z: 4, core: 2. Of those that a mesh axis runs over, the one named last changes fastest.
Arguments:
- guess: float32 [1024, 32, 1024], P(('owner', 'sub')), may hold values from -6 to 6
- rhs: float32 [1024, 32, 1024], P(('owner', 'sub')), may hold values from -6 to 6
- coef: float32 [1024, 32, 1024], P(('owner', 'sub')), may hold values from 0.1 to 10
- occupied: int32 [1024], P(('owner', 'sub')), may hold values 0 or 1
- neighbours: int32 [1024, 4], P(('owner', 'sub')), may hold values from -1 to 1023, as said below
- swap_slot: int32 [128, 16], P(('owner', 'sub')), may hold values from -1 to 7, as said below
- send_list: int32 [128, 16], P(('owner', 'sub')), may hold values from -1 to 15, as said below
- recv_list: int32 [128, 16], P(('owner', 'sub')), may hold values from -1 to 15, as said below
Outputs:
- solution: float32 [1024, 32, 1024], P(('owner', 'sub'))
- coarse_residual: float32 [1024, 16, 256], P(('owner', 'sub'))
The draws below stay inside these ranges and needn't reach their ends.
Inputs may be any that keep to these rules, and one draw needn't show every extreme that they name: The x-minus and x-plus neighbours of a slot lie on the same device; the z-minus neighbour lies on the device with owner index one lower and the same sub index, the z-plus neighbour on the one with owner index one higher. Neighbourhood is mutual across opposite faces. An entry is >= 0 only where the owner indices differ in exactly one bit; entries are mutual (swap_slot[d, q] >= 0 exactly when the partner's entry for d's owner index is), and the slots of one row are distinct. `send_list`: at most 2 faces go from one device to one device of its segment; a device reaches it towards itself. Every face named is received by exactly one ghost, consistent with recv_list. `recv_list`: each ghost of a device is named at most once.
All inputs are finite; a program needn't handle non-finite values. No bound on the sum of `occupied` on one device may be relied on, other than what follows from the above.
Results may differ from the reference program's by a relative error of at most 0.0003.
Values sent between devices are 32-bit elements; how exact they have to be, the bound alone decides.
No kernel may reach another device: no remote copies, remote signals or barrier semaphores. Data moves between devices by JAX's collectives and lax.ppermute only.
A program may use at most 128 MiB of HBM per device.

```python
import math
import jax
import jax.numpy as jnp
from jax import lax

C = 32
SLOTS = 8
SWEEPS = 3
BLOCKS = 1024
N_OWNER = 16
N_SUB = 8


def random_order(key, rows, length):
    scores = jax.random.randint(key, (rows, length), 0, 1 << 20) * length + jnp.arange(length, dtype=jnp.int32)[None, :]
    return jnp.argsort(scores, axis=1).astype(jnp.int32)


def route_ranks(key):
    return random_order(key, N_OWNER * N_SUB, SLOTS)


def draw_send_list(key, part):
    ranks = route_ranks(key)
    device_count = N_OWNER * N_SUB
    depth = (SLOTS + N_SUB - 1) // N_SUB
    device = jnp.arange(device_count, dtype=jnp.int32)[:, None, None]
    own_sub = device % N_SUB
    peer_sub = jnp.arange(N_SUB, dtype=jnp.int32)[None, :, None]
    item_idx = jnp.arange(depth, dtype=jnp.int32)[None, None, :]
    forward = jnp.remainder(peer_sub - own_sub, N_SUB) + N_SUB * item_idx
    backward = jnp.remainder(own_sub - peer_sub, N_SUB) + N_SUB * item_idx
    plus_faces = jnp.where(forward < SLOTS, 2 * ranks[device, jnp.minimum(forward, SLOTS - 1)] + 1, -1)
    minus_faces = jnp.where(backward < SLOTS, 2 * ranks[device, jnp.minimum(backward, SLOTS - 1)], -1)
    return jnp.concatenate([plus_faces, minus_faces], axis=2).reshape(device_count, N_SUB * 2 * depth).astype(jnp.int32)


def draw_recv_list(key, part):
    ranks = route_ranks(key)
    device_count = N_OWNER * N_SUB
    depth = (SLOTS + N_SUB - 1) // N_SUB
    device = jnp.arange(device_count, dtype=jnp.int32)[:, None, None]
    own_sub = device % N_SUB
    peer_sub = jnp.arange(N_SUB, dtype=jnp.int32)[None, :, None]
    item_idx = jnp.arange(depth, dtype=jnp.int32)[None, None, :]
    forward = jnp.remainder(own_sub - peer_sub, N_SUB) + N_SUB * item_idx
    backward = jnp.remainder(peer_sub - own_sub, N_SUB) + N_SUB * item_idx
    minus_ghost = jnp.where(forward < SLOTS, 2 * ranks[device, jnp.minimum(forward, SLOTS - 1)], -1)
    plus_ghost = jnp.where(backward < SLOTS, 2 * ranks[device, jnp.minimum(backward, SLOTS - 1)] + 1, -1)
    return jnp.concatenate([minus_ghost, plus_ghost], axis=2).reshape(device_count, N_SUB * 2 * depth).astype(jnp.int32)


def draw_neighbours(key, part):
    key = jax.random.fold_in(key, 5)
    key_a, key_b = jax.random.split(key)
    device_count = N_OWNER * N_SUB
    device = jnp.arange(device_count, dtype=jnp.int32)[:, None]
    chain_order = random_order(key_a, device_count, SLOTS)
    chain_place = jnp.argsort(chain_order, axis=1).astype(jnp.int32)
    successor = chain_order[device, jnp.minimum(chain_place + 1, SLOTS - 1)]
    predecessor = chain_order[device, jnp.maximum(chain_place - 1, 0)]
    first_id = device * SLOTS
    x_plus = jnp.where(chain_place < SLOTS - 1, first_id + successor, -1)
    x_minus = jnp.where(chain_place > 0, first_id + predecessor, -1)
    upward = random_order(key_b, device_count, SLOTS)
    downward = jnp.argsort(upward, axis=1).astype(jnp.int32)
    owner_idx = device // N_SUB
    z_plus = jnp.where(owner_idx < N_OWNER - 1, (device + N_SUB) * SLOTS + upward, -1)
    below_dev = jnp.maximum(device - N_SUB, 0)
    slot_idx = jnp.arange(SLOTS, dtype=jnp.int32)[None, :]
    z_minus = jnp.where(owner_idx > 0, (device - N_SUB) * SLOTS + downward[below_dev, slot_idx], -1)
    return jnp.stack([x_minus, x_plus, z_minus, z_plus], axis=-1).reshape(device_count * SLOTS, 4).astype(jnp.int32)


def draw_swap_slot(key, part):
    key = jax.random.fold_in(key, 7)
    key_a, key_b = jax.random.split(key)
    device_count = N_OWNER * N_SUB
    bit_count = N_OWNER.bit_length() - 1
    slot_order = random_order(key_a, device_count, SLOTS)
    activity = jax.random.randint(key_b, (N_OWNER, N_SUB, bit_count), 0, 4)
    owner_idx = jnp.arange(N_OWNER, dtype=jnp.int32)[:, None, None]
    sub_idx = jnp.arange(N_SUB, dtype=jnp.int32)[None, :, None]
    peer_owner = jnp.arange(N_OWNER, dtype=jnp.int32)[None, None, :]
    distance = jnp.bitwise_xor(owner_idx, peer_owner)
    single = (distance > 0) & (jnp.bitwise_and(distance, distance - 1) == 0)
    bit_index = sum((level * (distance == 1 << level).astype(jnp.int32) for level in range(bit_count)))
    lower_owner = jnp.minimum(owner_idx, peer_owner)
    active_pair = activity[lower_owner, sub_idx, bit_index] > 0
    slot_pick = slot_order[owner_idx * N_SUB + sub_idx, bit_index]
    return jnp.where(single & active_pair, slot_pick, -1).reshape(device_count, N_OWNER).astype(jnp.int32)


def touch_ends(drawn, key, low, largest):
    index_at = [jax.random.randint(jax.random.fold_in(key, axis), (), 0, length) for axis, length in enumerate(drawn.shape)]
    longest = drawn.shape.index(max(drawn.shape))
    neighbour = index_at[:longest] + [(index_at[longest] + 1) % drawn.shape[longest]] + index_at[longest + 1:]
    return drawn.at[tuple(index_at)].set(low).at[tuple(neighbour)].set(largest)


def levels(key, shape, pieces, low, largest):
    factor_of = 1.0
    for dim, blocks in pieces:
        draws = jax.random.uniform(jax.random.fold_in(jax.random.fold_in(key, 6), dim), (blocks,), jnp.float32, low / len(pieces), largest / len(pieces))
        factor_of = factor_of * jnp.repeat(jnp.exp(draws), shape[dim] // blocks).reshape((-1,) + (1,) * (len(shape) - 1 - dim))
    return factor_of


def centred(stream_key, shape, scale, bound, pieces=(), kind=jnp.bfloat16):
    loudness = levels(stream_key, shape, pieces, -0.22, 0.18) if pieces else 1.0
    drawn = jax.random.normal(stream_key, shape, jnp.float32) * scale * loudness
    return jnp.minimum(jnp.maximum(drawn, -bound), bound).astype(kind)


def setup_inputs(seed: int = 0) -> dict:
    keys = jax.random.split(jax.random.key(seed), 9)
    return {
        "guess": centred(keys[0], (BLOCKS, C, C * C), 1.0, 6.0, ((0, 128),), jnp.float32),
        "rhs": centred(keys[1], (BLOCKS, C, C * C), 1.0, 6.0, ((0, 128),), jnp.float32),
        "coef": jnp.clip(jnp.exp(math.log(10.0) - 4.6051702 * jax.random.uniform(keys[2], (BLOCKS, C, C * C), jnp.float32) ** levels(keys[2], (BLOCKS, C, C * C), ((0, 128),), -0.2, 0.2)), 0.1, 10.0),
        "occupied": touch_ends((jax.random.randint(keys[3], (BLOCKS,), 0, 4) < 3).astype(jnp.int32), jax.random.fold_in(keys[3], 1), 0, 1),
        "neighbours": draw_neighbours(jax.random.fold_in(keys[8], 71), 0),
        "swap_slot": draw_swap_slot(jax.random.fold_in(keys[8], 71), 0),
        "send_list": draw_send_list(jax.random.fold_in(keys[8], 71), 0),
        "recv_list": draw_recv_list(jax.random.fold_in(keys[8], 71), 0),
    }


OMEGA = 0.8


def face_set(values):
    edge = values.shape[1]
    return (values[:, :, 0::edge], values[:, :, edge - 1::edge], values[:, :, :edge], values[:, :, -edge:], values[:, 0, :], values[:, -1, :])


def take_rows(source_rows, index):
    clamped = jnp.maximum(index, 0)
    present = (index >= 0).reshape(index.shape + (1,) * (source_rows.ndim - 1))
    return jnp.where(present, source_rows[clamped], jnp.zeros((), source_rows.dtype))


def shifted(values, ghost, direction):
    edge = values.shape[1]
    plane = values.shape[2]
    column = lax.broadcasted_iota(jnp.int32, (1, 1, plane), 2)
    layer = lax.broadcasted_iota(jnp.int32, (1, edge, 1), 1)
    if direction == 0:
        return jnp.where(column % edge == 0, jnp.repeat(ghost, edge, axis=2), jnp.roll(values, 1, axis=2))
    if direction == 1:
        return jnp.where(column % edge == edge - 1, jnp.repeat(ghost, edge, axis=2), jnp.roll(values, -1, axis=2))
    if direction == 2:
        return jnp.where(column // edge == 0, jnp.tile(ghost, (1, 1, edge)), jnp.roll(values, edge, axis=2))
    if direction == 3:
        return jnp.where(column // edge == edge - 1, jnp.tile(ghost, (1, 1, edge)), jnp.roll(values, -edge, axis=2))
    if direction == 4:
        return jnp.where(layer == 0, ghost[:, None, :], jnp.roll(values, 1, axis=1))
    return jnp.where(layer == edge - 1, ghost[:, None, :], jnp.roll(values, -1, axis=1))


def coef_fill(ghosts, conduct):
    return tuple(jnp.where(ghost > 0.0, ghost, own) for ghost, own in zip(ghosts, face_set(conduct)))


def face_terms(conduct, ghost_k):
    diagonal_sum = jnp.zeros_like(conduct)
    coefs = []
    for direction in range(6):
        face_coef = 0.5 * (conduct + shifted(conduct, ghost_k[direction], direction))
        diagonal_sum = diagonal_sum + face_coef
        coefs.append(face_coef)
    return tuple(coefs), diagonal_sum


def operator(solution, coefs, diagonal_sum, ghost_u):
    flux_sum = jnp.zeros_like(solution)
    for direction in range(6):
        flux_sum = flux_sum + coefs[direction] * shifted(solution, ghost_u[direction], direction)
    return diagonal_sum * solution - flux_sum


def restrict(residual_field):
    count, edge, plane = residual_field.shape
    half_edge = edge // 2
    grouped = residual_field.reshape(count, half_edge, 2, half_edge, 2, half_edge, 2)
    return jnp.mean(grouped, axis=(2, 4, 6)).reshape(count, half_edge, half_edge * half_edge)


def all_ghosts(values, neighbours, send_list, recv_list):
    parts = face_set(values)
    count, edge, plane = values.shape
    device_count = N_OWNER * N_SUB
    slot_count = count // device_count
    width = send_list.shape[1]
    depth = width // N_SUB
    face_rows = jnp.stack([parts[2].reshape(count, plane), parts[3].reshape(count, plane)], axis=1).reshape(device_count, 2 * slot_count, plane)
    receiver = jnp.arange(device_count, dtype=jnp.int32)[:, None]
    position = jnp.arange(width, dtype=jnp.int32)[None, :]
    source_dev = (receiver // N_SUB) * N_SUB + position // depth
    entry_idx = send_list[source_dev, (receiver % N_SUB) * depth + position % depth]
    arrived = jnp.where((entry_idx >= 0)[:, :, None], face_rows[source_dev, jnp.maximum(entry_idx, 0)], jnp.zeros((), values.dtype))
    target = jnp.where(recv_list < 0, 2 * slot_count, recv_list)
    placed = jnp.zeros((device_count, 2 * slot_count + 1, plane), values.dtype)
    placed = placed.at[jnp.broadcast_to(receiver, target.shape), target].set(arrived)
    side_ghost = placed[:, :2 * slot_count].reshape(count, 2, edge, edge)
    return (take_rows(parts[1], neighbours[:, 0]), take_rows(parts[0], neighbours[:, 1]), side_ghost[:, 0], side_ghost[:, 1], take_rows(parts[5], neighbours[:, 2]), take_rows(parts[4], neighbours[:, 3]))


def migrate(arrays, occupied, swap_slot):
    device_count = N_OWNER * N_SUB
    count = occupied.shape[0]
    slot_count = count // device_count
    device = jnp.arange(device_count, dtype=jnp.int32)[:, None]
    peer_owner = jnp.arange(N_OWNER, dtype=jnp.int32)[None, :]
    partner = peer_owner * N_SUB + device % N_SUB
    partner_slot = swap_slot[partner, jnp.broadcast_to(device // N_SUB, partner.shape)]
    target = jnp.where(swap_slot >= 0, device * slot_count + swap_slot, count)
    anchor = partner * slot_count + jnp.maximum(partner_slot, 0)
    source_of = jnp.arange(count, dtype=jnp.int32).at[target.reshape(-1)].set(anchor.reshape(-1), mode="drop")
    return tuple(values[source_of] for values in arrays), occupied[source_of]


def reference(guess, rhs, coef, occupied, neighbours, swap_slot, send_list, recv_list):
    moved, alive = migrate((guess, rhs, coef), occupied, swap_slot)
    alive_mask = alive.astype(jnp.float32).reshape(-1, 1, 1)
    solution = moved[0] * alive_mask
    forcing = moved[1] * alive_mask
    conduct = moved[2] * alive_mask
    ghost_k = coef_fill(all_ghosts(conduct, neighbours, send_list, recv_list), conduct)
    coefs, diagonal_sum = face_terms(conduct, ghost_k)
    for sweep in range(SWEEPS):
        applied = operator(solution, coefs, diagonal_sum, all_ghosts(solution, neighbours, send_list, recv_list))
        solution = solution + OMEGA * alive_mask * (forcing - applied) / (diagonal_sum + 1.0 - alive_mask)
    applied = operator(solution, coefs, diagonal_sum, all_ghosts(solution, neighbours, send_list, recv_list))
    return solution, restrict(alive_mask * (forcing - applied))
```

```python
import jax
import jax.numpy as jnp
from jax import lax
from jax.experimental import pallas as pl
from jax.experimental.pallas import tpu as pltpu
from jax.sharding import PartitionSpec as P

SWEEPS = 3
OMEGA = 0.8
SLOTS = 8
EDGE = 32
PLANE = EDGE * EDGE
ROWS = SLOTS * EDGE
LANES = 128
COLS = PLANE // LANES
FIELD = (ROWS, PLANE)
FACES = 2 * SLOTS
FACE = (8, LANES)
SMEM = pl.BlockSpec(memory_space=pltpu.SMEM)
VMEM = pl.BlockSpec(memory_space=pltpu.VMEM)


def f32(*shape):
    return jax.ShapeDtypeStruct(shape, jnp.float32)


def params(mib):
    return pltpu.CompilerParams(vmem_limit_bytes=mib << 20)


def cost(flops, bytes_accessed):
    return pl.CostEstimate(flops=flops, bytes_accessed=bytes_accessed, transcendentals=0)


def column(c):
    return slice(c * LANES, (c + 1) * LANES)


def block_rows(j):
    return pl.ds(pl.multiple_of(j * EDGE, EDGE), EDGE)


def scaled_neighbour(neighbours, j, side):
    entry = neighbours[j, side]
    return jnp.maximum(entry, 0) % SLOTS, (entry >= 0).astype(jnp.float32)


def pack_face(first, side):
    group = lax.broadcasted_iota(jnp.int32, FACE, 1) // EDGE
    face = None
    for g in range(4):
        turn = (EDGE * g + EDGE * side) % LANES
        part = first(g)
        part = pltpu.roll(part, turn, 1) if turn else part
        face = part if face is None else jnp.where(group == g, part, face)
    return face


def unpack_face(face, side):
    parts = []
    for g in range(4):
        turn = (-EDGE * g - EDGE * side) % LANES
        parts.append(pltpu.roll(face, turn, 1) if turn else face)
    return jnp.concatenate(parts, axis=0)


def pack_faces(field, packed):
    def one(j, carry):
        for side in range(2):
            cols = column(0) if side == 0 else column(COLS - 1)
            packed[2 * j + side] = pack_face(
                lambda g: field[pl.ds(pl.multiple_of(j * EDGE + 8 * g, 8), 8), cols], side
            )
        return carry

    lax.fori_loop(0, SLOTS, one, 0)


def send_faces(packed, send_list, out, offset, stride):
    for entry in range(FACES):
        face = send_list[0, entry]
        out[entry * stride + offset] = packed[jnp.maximum(face, 0)] * (face >= 0).astype(jnp.float32)


def receive_faces(arrived, recv_list, ghost, offset, stride):
    ghost[...] = jnp.zeros(ghost.shape, jnp.float32)
    for entry in range(FACES):
        face = recv_list[0, entry]
        ghost[jnp.where(face >= 0, face, FACES)] = arrived[entry * stride + offset]


def send_layers(field, parity, out_even, out_odd, offset):
    even = parity[0] == 0
    for j in range(SLOTS):
        for c in range(COLS):
            bottom = field[j * EDGE : j * EDGE + 1, column(c)]
            top = field[(j + 1) * EDGE - 1 : (j + 1) * EDGE, column(c)]
            out_even[offset + j, c : c + 1, :] = jnp.where(even, top, bottom)
            out_odd[offset + j, c : c + 1, :] = jnp.where(even, bottom, top)


def receive_layers(in_even, in_odd, parity, below, above, offset):
    from_even = in_even[offset : offset + SLOTS]
    from_odd = in_odd[offset : offset + SLOTS]
    even = parity[0] == 0
    above[...] = jnp.where(even, from_even, from_odd)
    below[...] = jnp.where(even, from_odd, from_even)


def six_neighbours(field, j, neighbours, ghost, below, above):
    lane = lax.broadcasted_iota(jnp.int32, (EDGE, LANES), 1)
    row = lax.broadcasted_iota(jnp.int32, (EDGE, LANES), 0)
    x = lane % EDGE
    xm, has_xm = scaled_neighbour(neighbours, j, 0)
    xp, has_xp = scaled_neighbour(neighbours, j, 1)
    zm, has_zm = scaled_neighbour(neighbours, j, 2)
    zp, has_zp = scaled_neighbour(neighbours, j, 3)
    under_face, over_face = below[zm] * has_zm, above[zp] * has_zp
    own, minus_rows, plus_rows = block_rows(j), block_rows(xm), block_rows(xp)
    values = [field[own, column(c)] for c in range(COLS)]
    forth = [pltpu.roll(v, EDGE, 1) for v in values]
    back = [pltpu.roll(v, LANES - EDGE, 1) for v in values]
    forth.insert(0, unpack_face(ghost[2 * j], 0))
    back.append(unpack_face(ghost[2 * j + 1], 1))
    for c in range(COLS):
        v = values[c]
        left = field[minus_rows, column(c)] * has_xm
        right = field[plus_rows, column(c)] * has_xp
        under = under_face[c : c + 1, :]
        over = over_face[c : c + 1, :]
        yield (
            c,
            v,
            (
                jnp.where(x == 0, pltpu.roll(left, LANES - EDGE + 1, 1), pltpu.roll(v, 1, 1)),
                jnp.where(x == EDGE - 1, pltpu.roll(right, EDGE - 1, 1), pltpu.roll(v, LANES - 1, 1)),
                jnp.where(lane < EDGE, forth[c], forth[c + 1]),
                jnp.where(lane >= LANES - EDGE, back[c + 1], back[c]),
                jnp.where(row == 0, under, pltpu.roll(v, 1, 0)),
                jnp.where(row == EDGE - 1, over, pltpu.roll(v, EDGE - 1, 0)),
            ),
        )


def swap_pack_kernel(bits, pairs, owner, occupied, *refs):
    outs = refs[3 * bits :]
    for bit in range(bits):
        slot = jnp.maximum(pairs[0, owner[0] ^ (1 << bit)], 0)
        alive = occupied[slot].astype(jnp.float32)
        for k in range(3):
            outs[bit][k * EDGE : (k + 1) * EDGE, :] = refs[3 * bit + k][...] * alive


def swap_pack(fields, occupied, pairs, owner, bits):
    def spec(bit):
        return pl.BlockSpec(
            (EDGE, PLANE),
            lambda i, pairs, owner, occupied: (jnp.maximum(pairs[0, owner[0] ^ (1 << bit)], 0), 0),
        )

    return pl.pallas_call(
        lambda *refs: swap_pack_kernel(bits, *refs),
        grid_spec=pltpu.PrefetchScalarGridSpec(
            num_scalar_prefetch=3,
            grid=(1,),
            in_specs=[spec(bit) for bit in range(bits) for k in range(3)],
            out_specs=[pl.BlockSpec((3 * EDGE, PLANE), lambda i, *refs: (0, 0)) for bit in range(bits)],
        ),
        out_shape=[f32(3 * EDGE, PLANE) for bit in range(bits)],
        compiler_params=params(16),
        cost_estimate=cost(1 << 19, 3 << 20),
        name="swap_pack",
    )(pairs, owner, occupied, *(fields * bits))


def merge_kernel(
    bits, pairs, owner, occupied, send_list, parity, guess, rhs, coef, *refs
):
    incoming = refs[:bits]
    v, f, c, ze, zo, ys, packed = refs[bits:]

    def one(j, carry):
        alive = occupied[j].astype(jnp.float32)
        rows = block_rows(j)
        for source, target in ((guess, v), (rhs, f), (coef, c)):
            target[rows, :] = source[rows, :] * alive
        return carry

    lax.fori_loop(0, SLOTS, one, 0)
    for bit in range(bits):
        slot = pairs[0, owner[0] ^ (1 << bit)]

        @pl.when(slot >= 0)
        def _(bit=bit, slot=slot):
            rows = block_rows(jnp.maximum(slot, 0))
            for k, target in enumerate((v, f, c)):
                target[rows, :] = incoming[bit][k * EDGE : (k + 1) * EDGE, :]

    for k, field in enumerate((v, c)):
        send_layers(field, parity, ze, zo, k * SLOTS)
        pack_faces(field, packed)
        send_faces(packed, send_list, ys, k, 2)


def merge(fields, incoming, occupied, pairs, owner, send_list, parity):
    bits = len(incoming)
    return pl.pallas_call(
        lambda *refs: merge_kernel(bits, *refs),
        in_specs=[SMEM] * 5 + [VMEM] * (3 + bits),
        out_specs=[VMEM] * 6,
        out_shape=[f32(*FIELD)] * 3 + [f32(2 * SLOTS, *FACE)] * 2 + [f32(2 * FACES, *FACE)],
        scratch_shapes=[pltpu.VMEM((FACES,) + FACE, jnp.float32)],
        compiler_params=params(24),
        cost_estimate=cost(1 << 20, 8 << 20),
        name="merge",
    )(pairs, owner, occupied, send_list, parity, *fields, *incoming)


def first_kernel(
    neighbours, send_list, recv_list, parity, v, f, c, ie, io, ya,
    wk, wf, dg, u, ze, zo, ys,
    below, above, ghost, below_c, above_c, ghost_c, packed,
):
    receive_layers(ie, io, parity, below, above, 0)
    receive_layers(ie, io, parity, below_c, above_c, SLOTS)
    receive_faces(ya, recv_list, ghost, 0, 2)
    receive_faces(ya, recv_list, ghost_c, 1, 2)

    def one(j, carry):
        rows = block_rows(j)
        for n, k, around in six_neighbours(c, j, neighbours, ghost_c, below_c, above_c):
            faces = [0.5 * (k + jnp.where(other > 0.0, other, k)) for other in around]
            total = faces[0]
            for face in faces[1:]:
                total = total + face
            alive = k > 0.0
            weight = jnp.where(alive, OMEGA / jnp.where(alive, total, 1.0), 0.0)
            for d in range(6):
                wk[d, rows, column(n)] = weight * faces[d]
            wf[rows, column(n)] = weight * f[rows, column(n)]
            dg[rows, column(n)] = jnp.where(alive, total * (1.0 / OMEGA), 0.0)
        return carry

    lax.fori_loop(0, SLOTS, one, 0)
    sweep_blocks(neighbours, v, wk, wf, u, ghost, below, above)
    send_all(u, send_list, parity, ze, zo, ys, packed)


def sweep_blocks(neighbours, v, wk, wf, u, ghost, below, above):
    def one(j, carry):
        rows = block_rows(j)
        for n, centre, around in six_neighbours(v, j, neighbours, ghost, below, above):
            total = wf[rows, column(n)] + (1.0 - OMEGA) * centre
            for d in range(6):
                total = total + wk[d, rows, column(n)] * around[d]
            u[rows, column(n)] = total
        return carry

    lax.fori_loop(0, SLOTS, one, 0)


def send_all(u, send_list, parity, ze, zo, ys, packed):
    send_layers(u, parity, ze, zo, 0)
    pack_faces(u, packed)
    send_faces(packed, send_list, ys, 0, 1)


LAYERS = pltpu.VMEM((SLOTS,) + FACE, jnp.float32)
GHOSTS = pltpu.VMEM((FACES + 1,) + FACE, jnp.float32)


def first(v, f, c, ie, io, ya, neighbours, send_list, recv_list, parity):
    return pl.pallas_call(
        first_kernel,
        in_specs=[SMEM] * 4 + [VMEM] * 6,
        out_specs=[VMEM] * 7,
        out_shape=[f32(6, *FIELD)] + [f32(*FIELD)] * 3 + [f32(SLOTS, *FACE)] * 2 + [f32(FACES, *FACE)],
        scratch_shapes=[LAYERS, LAYERS, GHOSTS, LAYERS, LAYERS, GHOSTS, pltpu.VMEM((FACES,) + FACE, jnp.float32)],
        compiler_params=params(24),
        cost_estimate=cost(1 << 24, 12 << 20),
        name="first",
    )(neighbours, send_list, recv_list, parity, v, f, c, ie, io, ya)


def sweep_kernel(
    neighbours, send_list, recv_list, parity, v, wk, wf, ie, io, ya,
    u, ze, zo, ys,
    below, above, ghost, packed,
):
    receive_layers(ie, io, parity, below, above, 0)
    receive_faces(ya, recv_list, ghost, 0, 1)
    sweep_blocks(neighbours, v, wk, wf, u, ghost, below, above)
    send_all(u, send_list, parity, ze, zo, ys, packed)


def sweep(v, wk, wf, ie, io, ya, neighbours, send_list, recv_list, parity):
    return pl.pallas_call(
        sweep_kernel,
        in_specs=[SMEM] * 4 + [VMEM] * 6,
        out_specs=[VMEM] * 4,
        out_shape=[f32(*FIELD)] + [f32(SLOTS, *FACE)] * 2 + [f32(FACES, *FACE)],
        scratch_shapes=[LAYERS, LAYERS, GHOSTS, pltpu.VMEM((FACES,) + FACE, jnp.float32)],
        compiler_params=params(24),
        cost_estimate=cost(1 << 22, 9 << 20),
        name="sweep",
    )(neighbours, send_list, recv_list, parity, v, wk, wf, ie, io, ya)


def last_kernel(
    neighbours, recv_list, parity, v, wk, wf, dg, ie, io, ya,
    coarse,
    below, above, ghost, residual,
):
    receive_layers(ie, io, parity, below, above, 0)
    receive_faces(ya, recv_list, ghost, 0, 1)

    def one(j, carry):
        rows = block_rows(j)
        for n, centre, around in six_neighbours(v, j, neighbours, ghost, below, above):
            total = wf[rows, column(n)] - OMEGA * centre
            for d in range(6):
                total = total + wk[d, rows, column(n)] * around[d]
            residual[n, rows, :] = total * dg[rows, column(n)]
        return carry

    lax.fori_loop(0, SLOTS, one, 0)
    lane = lax.broadcasted_iota(jnp.int32, (LANES, LANES), 0)
    target = lax.broadcasted_iota(jnp.int32, (LANES, LANES), 1)
    place = (lane // (2 * EDGE)) * (EDGE // 2) + (lane % EDGE) // 2
    half = ROWS // 2
    for part in range(2):
        total = jnp.zeros((half, LANES), jnp.float32)
        for n in range(4):
            column_sum = (
                residual[part * 4 + n, pl.ds(0, half, stride=2), :]
                + residual[part * 4 + n, pl.ds(1, half, stride=2), :]
            )
            gather = jnp.where(place + EDGE * n == target, 0.125, 0.0)
            total = total + jnp.dot(
                column_sum, gather, precision=lax.Precision.HIGHEST, preferred_element_type=jnp.float32
            )
        coarse[:, part * LANES : (part + 1) * LANES] = total


def last(v, wk, wf, dg, ie, io, ya, neighbours, recv_list, parity):
    return pl.pallas_call(
        last_kernel,
        in_specs=[SMEM] * 3 + [VMEM] * 7,
        out_specs=VMEM,
        out_shape=f32(ROWS // 2, PLANE // 4),
        scratch_shapes=[LAYERS, LAYERS, GHOSTS, pltpu.VMEM((COLS, ROWS, LANES), jnp.float32)],
        compiler_params=params(24),
        cost_estimate=cost(1 << 24, 10 << 20),
        name="last",
    )(neighbours, recv_list, parity, v, wk, wf, dg, ie, io, ya)


def pair_swap(values, stride):
    count = lax.axis_size("owner")
    return lax.ppermute(values, "owner", [(i, i ^ stride) for i in range(count)])


def odd_pair_swap(values):
    count = lax.axis_size("owner")
    return lax.ppermute(values, "owner", [(i, ((i - 1) ^ 1) + 1) for i in range(1, count - 1)])


def exchange(ze, zo, ys):
    arrived = lax.all_to_all(ys, "sub", split_axis=0, concat_axis=0, tiled=True)
    return pair_swap(ze, 1), odd_pair_swap(zo), arrived


def body(guess, rhs, coef, occupied, neighbours, swap_slot, send_list, recv_list):
    my_owner = lax.axis_index("owner").astype(jnp.int32)
    owner = my_owner.reshape(1)
    parity = (my_owner % 2).reshape(1)
    bits = lax.axis_size("owner").bit_length() - 1
    fields = tuple(values.reshape(FIELD) for values in (guess, rhs, coef))
    outgoing = swap_pack(fields, occupied, swap_slot, owner, bits)
    incoming = tuple(pair_swap(outgoing[bit], 1 << bit) for bit in range(bits))
    v, f, c, ze, zo, ys = merge(fields, incoming, occupied, swap_slot, owner, send_list, parity)
    ghosts = exchange(ze, zo, ys)
    wk, wf, dg, v, ze, zo, ys = first(v, f, c, *ghosts, neighbours, send_list, recv_list, parity)
    for _ in range(SWEEPS - 1):
        ghosts = exchange(ze, zo, ys)
        v, ze, zo, ys = sweep(v, wk, wf, *ghosts, neighbours, send_list, recv_list, parity)
    ghosts = exchange(ze, zo, ys)
    coarse = last(v, wk, wf, dg, *ghosts, neighbours, recv_list, parity)
    return v.reshape(SLOTS, EDGE, PLANE), coarse.reshape(SLOTS, EDGE // 2, PLANE // 4)


def solution(mesh):
    wide, flat, single = P(("owner", "sub"), None, None), P(("owner", "sub"), None), P(("owner", "sub"))
    return jax.shard_map(
        body,
        mesh=mesh,
        in_specs=(wide, wide, wide, single, flat, flat, flat, flat),
        out_specs=(wide, wide),
        check_vma=False,
    )
```

```python
import jax
import jax.numpy as jnp
from jax import lax
from jax.experimental import pallas as pl
from jax.experimental.pallas import tpu as pltpu
from jax.sharding import PartitionSpec as P

OMEGA = 0.8
SLOTS = 8
EDGE = 32
PLANE = EDGE * EDGE
ROWS = SLOTS * EDGE
LANES = 128
COLS = PLANE // LANES
FIELD = (ROWS, PLANE)
FACES = 2 * SLOTS
TILE = (8, LANES)
BITS = 4
V1, V2, C1, C2, F1 = range(5)
KINDS = 5
SEND = 4 * SLOTS
RECV = SEND + FACES
SMEM = pl.BlockSpec(memory_space=pltpu.SMEM)
VMEM = pl.BlockSpec(memory_space=pltpu.VMEM)
HBM = pl.BlockSpec(memory_space=pltpu.HBM)


def f32(*shape):
    return jax.ShapeDtypeStruct(shape, jnp.float32)


def tiles(count):
    return f32(count, *TILE)


def scratch(*shape):
    return pltpu.VMEM(shape, jnp.float32)


def params(mib):
    return pltpu.CompilerParams(vmem_limit_bytes=mib << 20)


def cost(flops, bytes_accessed):
    return pl.CostEstimate(flops=flops, bytes_accessed=bytes_accessed, transcendentals=0)


def column(c):
    return slice(c * LANES, (c + 1) * LANES)


def block_rows(j):
    return pl.ds(pl.multiple_of(j * EDGE, EDGE), EDGE)


def iotas(shape):
    rank = len(shape)
    sub = lax.broadcasted_iota(jnp.int32, shape, rank - 2)
    lane = lax.broadcasted_iota(jnp.int32, shape, rank - 1)
    return sub, lane


def slot_or(entry, none):
    return jnp.where(entry >= 0, jnp.maximum(entry, 0) % SLOTS, none)


def layer_tile(field, row, out, index):
    for c in range(COLS):
        out[index, c : c + 1, :] = field[row : row + 1, column(c)]


def face_tile(field, first_row, side):
    group = lax.broadcasted_iota(jnp.int32, TILE, 1) // EDGE
    cols = column(0) if side == 0 else column(COLS - 1)
    face = None
    for g in range(4):
        turn = (EDGE * g + EDGE * side) % LANES
        part = field[pl.ds(pl.multiple_of(first_row + 8 * g, 8), 8), cols]
        part = pltpu.roll(part, turn, 1) if turn else part
        face = part if face is None else jnp.where(group == g, part, face)
    return face


def unpack_face(face, side):
    parts = []
    for g in range(4):
        turn = (-EDGE * g - EDGE * side) % LANES
        parts.append(pltpu.roll(face, turn, 1) if turn else face)
    return jnp.concatenate(parts, axis=0)


def all_faces(field, out):
    def one(j, carry):
        for side in range(2):
            out[2 * j + side] = face_tile(field, j * EDGE, side)
        return carry

    lax.fori_loop(0, SLOTS, one, 0)


def pick_faces(faces, mine, out, offset, stride):
    for entry in range(FACES):
        face = mine[SEND + entry]
        out[(entry // 2) * stride + entry % 2 + offset] = faces[jnp.maximum(face, 0)] * (face >= 0).astype(
            jnp.float32
        )


def place_faces(arrived, mine, ghost, offset, stride):
    ghost[...] = jnp.zeros(ghost.shape, jnp.float32)
    for entry in range(FACES):
        face = mine[RECV + entry]
        ghost[jnp.where(face >= 0, face, FACES)] = arrived[(entry // 2) * stride + entry % 2 + offset]


class Lists:
    def __init__(self, even, from_even, from_odd, side):
        self.take_even = even if side else jnp.logical_not(even)
        self.from_even, self.from_odd = from_even, from_odd

    def at(self, i):
        return jnp.where(self.take_even, self.from_even[i], self.from_odd[i])

    def neighbour(self, slot, direction):
        return self.at(4 * slot + direction)

    def send(self, entry):
        return self.at(SEND + entry)

    def recv(self, entry):
        return self.at(RECV + entry)


def sheet_of(even, from_even, from_odd, kind, side):
    rows = slice(kind * SLOTS, (kind + 1) * SLOTS)
    pair = (from_even[rows], from_odd[rows])
    return jnp.where(even, *(pair if side else pair[::-1]))


def own_end(even, to_even, to_odd, kind, side):
    return sheet_of(even, to_even, to_odd, kind, side)


def fill_sheet(store, value):
    store[:SLOTS] = value
    store[SLOTS] = jnp.zeros(TILE, jnp.float32)


def pack_lines(sheets, lists, out, tile, stride):
    sub, lane = iotas(TILE)
    for peer in range(SLOTS):
        total = jnp.zeros(TILE, jnp.float32)
        row = 0
        for side in range(2):
            for i in range(2):
                face = lists[side].send(2 * peer + i)
                slot = jnp.where(face >= 0, jnp.maximum(face, 0) // 2, SLOTS)
                high = jnp.maximum(face, 0) % 2 == 1
                for store in sheets[side]:
                    line = store[slot]
                    low_line = line[0:1, :]
                    high_line = pltpu.roll(line, EDGE, 1)[7:8, :]
                    total = jnp.where(sub == row, jnp.where(high, high_line, low_line), total)
                    row += 1
        out[peer * stride + tile] = total


def place_lines(arrived, lists, edges, tile, stride):
    for pair in edges:
        for store in pair:
            store[...] = jnp.zeros(store.shape, jnp.float32)
    sub, lane = iotas(TILE)
    first = (sub == 0) & (lane < EDGE)
    final = (sub == 7) & (lane >= LANES - EDGE)
    for peer in range(SLOTS):
        got = arrived[peer * stride + tile]
        turned = pltpu.roll(got, LANES - EDGE, 1)
        row = 0
        for side in range(2):
            for i in range(2):
                ghost = lists[side].recv(2 * peer + i)
                slot = jnp.where(ghost >= 0, jnp.maximum(ghost, 0) // 2, SLOTS)
                high = jnp.maximum(ghost, 0) % 2 == 1
                for store in edges[side]:
                    low_part = jnp.where(first, got[row : row + 1, :], 0.0)
                    high_part = jnp.where(final, turned[row : row + 1, :], 0.0)
                    store[slot] = store[slot] + jnp.where(high, high_part, low_part)
                    row += 1


def sheet_around(store, inner, outer_tiles, edge, lists, side, gathered):
    shape = (SLOTS,) + TILE
    sub, lane = iotas(shape)
    x = lane % EDGE
    minus, plus, outer = gathered
    for slot in range(SLOTS):
        minus[slot] = store[slot_or(lists.neighbour(slot, 0), SLOTS)]
        plus[slot] = store[slot_or(lists.neighbour(slot, 1), SLOTS)]
        entry = lists.neighbour(slot, 2 if side else 3)
        outer[slot] = outer_tiles[slot_or(entry, 0)] * (entry >= 0).astype(jnp.float32)
    value = store[:SLOTS]
    edges = edge[:SLOTS]
    forth = pltpu.roll(value, EDGE, 2)
    back = pltpu.roll(value, LANES - EDGE, 2)
    before = jnp.where(lane < EDGE, pltpu.roll(forth, 1, 1), forth)
    after = jnp.where(lane >= LANES - EDGE, pltpu.roll(back, 7, 1), back)
    out = outer[...]
    return (
        jnp.where(x == 0, pltpu.roll(minus[...], LANES - EDGE + 1, 2), pltpu.roll(value, 1, 2)),
        jnp.where(x == EDGE - 1, pltpu.roll(plus[...], EDGE - 1, 2), pltpu.roll(value, LANES - 1, 2)),
        jnp.where((lane < EDGE) & (sub == 0), edges, before),
        jnp.where((lane >= LANES - EDGE) & (sub == 7), edges, after),
        out if side else inner,
        inner if side else out,
    )


def weights(k, around):
    faces = [0.5 * (k + jnp.where(other > 0.0, other, k)) for other in around]
    total = faces[0]
    for face in faces[1:]:
        total = total + face
    alive = k > 0.0
    weight = jnp.where(alive, OMEGA / jnp.where(alive, total, 1.0), 0.0)
    return [weight * face for face in faces], weight, jnp.where(alive, total * (1.0 / OMEGA), 0.0)


def six_neighbours(field, j, mine, ghost, below, above):
    _, lane = iotas((EDGE, LANES))
    x = lane % EDGE

    def scaled(side):
        entry = mine[4 * j + side]
        return slot_or(entry, 0), (entry >= 0).astype(jnp.float32)

    (xm, has_xm), (xp, has_xp), (zm, has_zm), (zp, has_zp) = [scaled(side) for side in range(4)]
    under_face, over_face = below[zm] * has_zm, above[zp] * has_zp
    own, minus_rows, plus_rows = block_rows(j), block_rows(xm), block_rows(xp)
    values = [field[own, column(c)] for c in range(COLS)]
    forth = [pltpu.roll(v, EDGE, 1) for v in values]
    back = [pltpu.roll(v, LANES - EDGE, 1) for v in values]
    forth.insert(0, unpack_face(ghost[2 * j], 0))
    back.append(unpack_face(ghost[2 * j + 1], 1))
    for c in range(COLS):
        v = values[c]
        left = field[minus_rows, column(c)] * has_xm
        right = field[plus_rows, column(c)] * has_xp
        yield (
            c,
            v,
            (
                jnp.where(x == 0, pltpu.roll(left, LANES - EDGE + 1, 1), pltpu.roll(v, 1, 1)),
                jnp.where(x == EDGE - 1, pltpu.roll(right, EDGE - 1, 1), pltpu.roll(v, LANES - 1, 1)),
                jnp.where(lane < EDGE, forth[c], forth[c + 1]),
                jnp.where(lane >= LANES - EDGE, back[c + 1], back[c]),
                jnp.concatenate([under_face[c : c + 1, :], v[: EDGE - 1]], axis=0),
                jnp.concatenate([v[1:], over_face[c : c + 1, :]], axis=0),
            ),
        )


def sweep_blocks(mine, v, wk, wf, u, ghost, below, above):
    def one(j, carry):
        rows = block_rows(j)
        for n, centre, around in six_neighbours(v, j, mine, ghost, below, above):
            total = wf[rows, column(n)] + (1.0 - OMEGA) * centre
            for d in range(6):
                total = total + wk[d, rows, column(n)] * around[d]
            u[rows, column(n)] = total
        return carry

    lax.fori_loop(0, SLOTS, one, 0)


def pair_slot(pairs, owner, bit):
    return pairs[0, owner[0] ^ (1 << bit)]


def early_tiles(v, f, c, row, out):
    for end in range(2):
        for kind, field, depth in ((V1, v, 0), (V2, v, 1), (C1, c, 0), (C2, c, 1), (F1, f, 0)):
            layer_tile(field, row + (depth if end else EDGE - 1 - depth), out, end * KINDS + kind)
    for k, field in enumerate((v, c)):
        for side in range(2):
            out[2 * KINDS + 2 * k + side] = face_tile(field, row, side)


def swap_pack_kernel(pairs, owner, occupied, guess, rhs, coef, *refs):
    early, bulk, sems = refs[:BITS], refs[BITS : 2 * BITS], refs[2 * BITS]
    slots = [jnp.maximum(pair_slot(pairs, owner, bit), 0) for bit in range(BITS)]

    def copies(bit):
        return [
            pltpu.make_async_copy(
                source.at[block_rows(slots[bit])], bulk[bit].at[pl.ds(k * EDGE, EDGE)], sems.at[bit, k]
            )
            for k, source in enumerate((guess, rhs, coef))
        ]

    for bit in range(BITS):
        for copy in copies(bit):
            copy.start()
    for bit in range(BITS):
        for copy in copies(bit):
            copy.wait()

        @pl.when(occupied[slots[bit]] == 0)
        def _(bit=bit):
            bulk[bit][...] = jnp.zeros((3 * EDGE, PLANE), jnp.float32)

        out = bulk[bit]
        early_tiles(
            out.at[pl.ds(0, EDGE)], out.at[pl.ds(EDGE, EDGE)], out.at[pl.ds(2 * EDGE, EDGE)], 0, early[bit]
        )


def swap_pack(fields, occupied, pairs, owner):
    outs = pl.pallas_call(
        swap_pack_kernel,
        in_specs=[SMEM] * 3 + [HBM] * 3,
        out_specs=[VMEM] * (2 * BITS),
        out_shape=[tiles(2 * KINDS + 4)] * BITS + [f32(3 * EDGE, PLANE)] * BITS,
        scratch_shapes=[pltpu.SemaphoreType.DMA((BITS, 3))],
        compiler_params=params(8),
        cost_estimate=cost(1 << 19, 3 << 20),
        name="swap_pack",
    )(pairs, owner, occupied, *fields)
    return outs[:BITS], outs[BITS:]


def local_kernel(occupied, guess, rhs, coef, top, bottom, faces, v, f, c, out, sems):
    copies = [
        pltpu.make_async_copy(source, target, sems.at[k])
        for k, (source, target) in enumerate(((guess, v), (rhs, f), (coef, c)))
    ]
    for copy in copies:
        copy.start()
    for copy in copies:
        copy.wait()
    for j in range(SLOTS):
        early_tiles(v, f, c, j * EDGE, out)
        alive = occupied[j].astype(jnp.float32)
        for kind in range(KINDS):
            top[kind * SLOTS + j] = out[kind] * alive
            bottom[kind * SLOTS + j] = out[KINDS + kind] * alive
        for k in range(2):
            for side in range(2):
                faces[k * FACES + 2 * j + side] = out[2 * KINDS + 2 * k + side] * alive


def local(fields, occupied):
    return pl.pallas_call(
        local_kernel,
        in_specs=[SMEM] + [HBM] * 3,
        out_specs=[VMEM] * 3,
        out_shape=[tiles(KINDS * SLOTS)] * 2 + [tiles(2 * FACES)],
        scratch_shapes=[scratch(*FIELD)] * 3 + [scratch(2 * KINDS + 4, *TILE), pltpu.SemaphoreType.DMA((3,))],
        compiler_params=params(8),
        cost_estimate=cost(1 << 20, 4 << 20),
        name="local",
    )(occupied, *fields)


def ends_kernel(pairs, owner, mine, parity, top, bottom, faces, *refs):
    early = refs[:BITS]
    ze, zo, ys, held = refs[BITS:]
    even = parity[0] == 0
    ze[...] = jnp.where(even, top[...], bottom[...])
    zo[...] = jnp.where(even, bottom[...], top[...])
    held[...] = faces[...]
    for bit in range(BITS):
        slot = pair_slot(pairs, owner, bit)

        @pl.when(slot >= 0)
        def _(bit=bit, slot=jnp.maximum(slot, 0)):
            fresh = early[bit]
            for kind in range(KINDS):
                high, low = fresh[kind], fresh[KINDS + kind]
                ze[kind * SLOTS + slot] = jnp.where(even, high, low)
                zo[kind * SLOTS + slot] = jnp.where(even, low, high)
            for k in range(2):
                for side in range(2):
                    held[k * FACES + 2 * slot + side] = fresh[2 * KINDS + 2 * k + side]

    for k in range(2):
        pick_faces(held.at[pl.ds(k * FACES, FACES)], mine, ys, 2 * k, 4)


def ends(top, bottom, faces, early, pairs, owner, mine, parity):
    return pl.pallas_call(
        ends_kernel,
        in_specs=[SMEM] * 4 + [VMEM] * (3 + BITS),
        out_specs=[VMEM] * 3,
        out_shape=[tiles(KINDS * SLOTS)] * 2 + [tiles(2 * FACES)],
        scratch_shapes=[scratch(2 * FACES, *TILE)],
        compiler_params=params(4),
        cost_estimate=cost(1 << 18, 1 << 20),
        name="ends",
    )(pairs, owner, mine, parity, top, bottom, faces, *early)


def first_kernel(
    pairs, owner, occupied, mine, parity, lists_e, lists_o, ie, io, ya, *refs
):
    bulk, fields = refs[:BITS], refs[BITS : BITS + 3]
    wk, wf, dg, u, ys, v, f, c, ghost, ghost_c, below, above, below_c, above_c, faces, sems = refs[BITS + 3 :]
    even = parity[0] == 0
    merged = (v, f, c)
    slots = [pair_slot(pairs, owner, bit) for bit in range(BITS)]
    for k in (2, 0, 1):
        for j in range(SLOTS):
            swapped = slots[0] == j
            for slot in slots[1:]:
                swapped = swapped | (slot == j)
            rows = pl.ds(j * EDGE, EDGE)

            @pl.when(jnp.logical_not(swapped))
            def _(k=k, rows=rows):
                pltpu.make_async_copy(fields[k].at[rows], merged[k].at[rows], sems.at[k]).start()

        for bit in range(BITS):

            @pl.when(slots[bit] >= 0)
            def _(k=k, bit=bit):
                pltpu.make_async_copy(
                    bulk[bit].at[pl.ds(k * EDGE, EDGE)],
                    merged[k].at[block_rows(jnp.maximum(slots[bit], 0))],
                    sems.at[k],
                ).start()

    sheets = ((below, below_c), (above, above_c))
    for side in range(2):
        for store, kind in zip(sheets[side], (V1, C1)):
            fill_sheet(store, sheet_of(even, ie, io, kind, side))
    place_faces(ya, mine, ghost, 0, 4)
    place_faces(ya, mine, ghost_c, 2, 4)
    lists = [Lists(even, lists_e, lists_o, side) for side in range(2)]
    pack_lines(sheets, lists, ys, 2, 3)

    def settle(k):
        pltpu.make_async_copy(fields[k], merged[k], sems.at[k]).wait()
        for j in range(SLOTS):
            swapped = slots[0] == j
            for slot in slots[1:]:
                swapped = swapped | (slot == j)

            @pl.when((occupied[j] == 0) & jnp.logical_not(swapped))
            def _(j=j):
                merged[k][j * EDGE : (j + 1) * EDGE, :] = jnp.zeros((EDGE, PLANE), jnp.float32)

    for k in (2, 0, 1):
        settle(k)

    def one(j, carry):
        rows = block_rows(j)
        for n, k, around in six_neighbours(c, j, mine, ghost_c, below_c, above_c):
            scaled, weight, inverse = weights(k, around)
            for d in range(6):
                wk[d, rows, column(n)] = scaled[d]
            wf[rows, column(n)] = weight * f[rows, column(n)]
            dg[rows, column(n)] = inverse
        return carry

    lax.fori_loop(0, SLOTS, one, 0)
    sweep_blocks(mine, v, wk, wf, u, ghost, below, above)
    all_faces(u, faces)
    pick_faces(faces, mine, ys, 0, 3)


SHEET = scratch(SLOTS + 1, *TILE)
GHOSTS = scratch(FACES + 1, *TILE)
GATHERED = [scratch(SLOTS, *TILE)] * 3


def first(pairs, owner, occupied, mine, parity, lists, ends_in, ya, bulk, fields):
    return pl.pallas_call(
        first_kernel,
        in_specs=[SMEM] * 7 + [VMEM] * 3 + [HBM] * (BITS + 3),
        out_specs=[VMEM] * 5,
        out_shape=[f32(6, *FIELD)] + [f32(*FIELD)] * 3 + [tiles(3 * SLOTS)],
        scratch_shapes=[scratch(*FIELD)] * 3
        + [GHOSTS] * 2
        + [SHEET] * 4
        + [scratch(FACES, *TILE), pltpu.SemaphoreType.DMA((3,))],
        compiler_params=params(20),
        cost_estimate=cost(1 << 24, 12 << 20),
        name="first",
    )(pairs, owner, occupied, mine, parity, *lists, *ends_in, ya, *bulk, *fields)


def second_kernel(
    mine, parity, lists_e, lists_o,
    v, wk, wf, ye, yo, ie, io, ya,
    u, ze, zo, ys, kept,
    ghost, below, above, below_c, above_c, edge_bv, edge_bc, edge_av, edge_ac, gm, gp, go, faces, ends_out,
):
    even = parity[0] == 0
    lists = [Lists(even, lists_e, lists_o, side) for side in range(2)]
    place_faces(ya, mine, ghost, 0, 3)
    edges = ((edge_bv, edge_bc), (edge_av, edge_ac))
    place_lines(ya, lists, edges, 2, 3)
    for side, (store, store_c) in enumerate(((below, below_c), (above, above_c))):
        fill_sheet(store, sheet_of(even, ie, io, V1, side))
        fill_sheet(store_c, sheet_of(even, ie, io, C1, side))
        k = store_c[:SLOTS]
        ends_out[...] = own_end(even, ye, yo, C1, side)
        inner = sheet_of(even, ie, io, C2, side)
        around = sheet_around(store_c, inner, ends_out, edges[side][1], lists[side], side, (gm, gp, go))
        scaled, weight, _ = weights(k, around)
        forced = weight * sheet_of(even, ie, io, F1, side)
        for d in range(6):
            kept[(side * 7 + d) * SLOTS : (side * 7 + d + 1) * SLOTS] = scaled[d]
        kept[(side * 7 + 6) * SLOTS : (side * 7 + 7) * SLOTS] = forced
        ends_out[...] = own_end(even, ye, yo, V1, side)
        inner = sheet_of(even, ie, io, V2, side)
        around = sheet_around(store, inner, ends_out, edges[side][0], lists[side], side, (gm, gp, go))
        total = forced + (1.0 - OMEGA) * store[:SLOTS]
        for d in range(6):
            total = total + scaled[d] * around[d]
        store[:SLOTS] = total
    sweep_blocks(mine, v, wk, wf, u, ghost, below, above)
    all_faces(u, faces)
    pick_faces(faces, mine, ys, 0, 2)
    for j in range(SLOTS):
        for depth in range(2):
            layer_tile(u, j * EDGE + EDGE - 1 - depth, ends_out, 0)
            layer_tile(u, j * EDGE + depth, ends_out, 1)
            ze[depth * SLOTS + j] = jnp.where(even, ends_out[0], ends_out[1])
            zo[depth * SLOTS + j] = jnp.where(even, ends_out[1], ends_out[0])


def second(v, wk, wf, sent, got, ya, mine, parity, lists):
    return pl.pallas_call(
        second_kernel,
        in_specs=[SMEM] * 4 + [VMEM] * 8,
        out_specs=[VMEM] * 5,
        out_shape=[f32(*FIELD), tiles(2 * SLOTS), tiles(2 * SLOTS), tiles(FACES), tiles(14 * SLOTS)],
        scratch_shapes=[GHOSTS] + [SHEET] * 8 + GATHERED + [scratch(FACES, *TILE), scratch(SLOTS, *TILE)],
        compiler_params=params(16),
        cost_estimate=cost(1 << 22, 9 << 20),
        name="second",
    )(mine, parity, *lists, v, wk, wf, *sent, *got, ya)


def third_kernel(
    mine, parity, lists_e, lists_o,
    v, wk, wf, ie, io, ya,
    u, ys,
    ghost, below, above, faces,
):
    even = parity[0] == 0
    lists = [Lists(even, lists_e, lists_o, side) for side in range(2)]
    place_faces(ya, mine, ghost, 0, 2)
    for side, store in enumerate((below, above)):
        fill_sheet(store, sheet_of(even, ie, io, V1, side))
    pack_lines(((below,), (above,)), lists, ys, 2, 3)
    sweep_blocks(mine, v, wk, wf, u, ghost, below, above)
    all_faces(u, faces)
    pick_faces(faces, mine, ys, 0, 3)


def third(v, wk, wf, got, ya, mine, parity, lists):
    return pl.pallas_call(
        third_kernel,
        in_specs=[SMEM] * 4 + [VMEM] * 6,
        out_specs=[VMEM] * 2,
        out_shape=[f32(*FIELD), tiles(3 * SLOTS)],
        scratch_shapes=[GHOSTS] + [SHEET] * 2 + [scratch(FACES, *TILE)],
        compiler_params=params(16),
        cost_estimate=cost(1 << 22, 9 << 20),
        name="third",
    )(mine, parity, *lists, v, wk, wf, *got, ya)


def last_kernel(
    mine, parity, lists_e, lists_o,
    v, wk, wf, dg, kept, ye, yo, ie, io, ya,
    out, coarse,
    ghost, below, above, edge_b, edge_a, gm, gp, go, ends_out, residual, sem,
):
    write = pltpu.make_async_copy(v, out, sem)
    write.start()
    even = parity[0] == 0
    lists = [Lists(even, lists_e, lists_o, side) for side in range(2)]
    place_faces(ya, mine, ghost, 0, 3)
    edges = ((edge_b,), (edge_a,))
    place_lines(ya, lists, edges, 2, 3)
    for side, store in enumerate((below, above)):
        fill_sheet(store, sheet_of(even, ie, io, V1, side))
        ends_out[...] = own_end(even, ye, yo, V1, side)
        inner = sheet_of(even, ie, io, V2, side)
        around = sheet_around(store, inner, ends_out, edges[side][0], lists[side], side, (gm, gp, go))
        total = kept[(side * 7 + 6) * SLOTS : (side * 7 + 7) * SLOTS] + (1.0 - OMEGA) * store[:SLOTS]
        for d in range(6):
            total = total + kept[(side * 7 + d) * SLOTS : (side * 7 + d + 1) * SLOTS] * around[d]
        store[:SLOTS] = total

    def one(j, carry):
        rows = block_rows(j)
        for n, centre, around in six_neighbours(v, j, mine, ghost, below, above):
            total = wf[rows, column(n)] - OMEGA * centre
            for d in range(6):
                total = total + wk[d, rows, column(n)] * around[d]
            residual[n, rows, :] = total * dg[rows, column(n)]
        return carry

    lax.fori_loop(0, SLOTS, one, 0)
    lane = lax.broadcasted_iota(jnp.int32, (LANES, LANES), 0)
    target = lax.broadcasted_iota(jnp.int32, (LANES, LANES), 1)
    place = (lane // (2 * EDGE)) * (EDGE // 2) + (lane % EDGE) // 2
    half = ROWS // 2
    for part in range(2):
        total = jnp.zeros((half, LANES), jnp.float32)
        for n in range(4):
            column_sum = (
                residual[part * 4 + n, pl.ds(0, half, stride=2), :]
                + residual[part * 4 + n, pl.ds(1, half, stride=2), :]
            )
            gather = jnp.where(place + EDGE * n == target, 0.125, 0.0)
            total = total + jnp.dot(
                column_sum, gather, precision=lax.Precision.HIGHEST, preferred_element_type=jnp.float32
            )
        coarse[:, part * LANES : (part + 1) * LANES] = total
    write.wait()


def last(v, wk, wf, dg, kept, sent, got, ya, mine, parity, lists):
    return pl.pallas_call(
        last_kernel,
        in_specs=[SMEM] * 4 + [VMEM] * 10,
        out_specs=[HBM, VMEM],
        out_shape=[f32(*FIELD), f32(ROWS // 2, PLANE // 4)],
        scratch_shapes=[GHOSTS] + [SHEET] * 4 + GATHERED + [scratch(SLOTS, *TILE), scratch(COLS, ROWS, LANES), pltpu.SemaphoreType.DMA],
        compiler_params=params(16),
        cost_estimate=cost(1 << 24, 10 << 20),
        name="last",
    )(mine, parity, *lists, v, wk, wf, dg, kept, *sent, *got, ya)


def pair_swap(values, stride):
    count = lax.axis_size("owner")
    return lax.ppermute(values, "owner", [(i, i ^ stride) for i in range(count)])


def odd_pair_swap(values):
    count = lax.axis_size("owner")
    return lax.ppermute(values, "owner", [(i, ((i - 1) ^ 1) + 1) for i in range(1, count - 1)])


def in_hbm(values):
    return pltpu.with_memory_space_constraint(values, pltpu.HBM)


def segment_swap(ys):
    return lax.all_to_all(ys, "sub", split_axis=0, concat_axis=0, tiled=True)


def body(guess, rhs, coef, occupied, neighbours, swap_slot, send_list, recv_list):
    my_owner = lax.axis_index("owner").astype(jnp.int32)
    owner = my_owner.reshape(1)
    parity = (my_owner % 2).reshape(1)
    fields = tuple(values.reshape(FIELD) for values in (guess, rhs, coef))
    fields = tuple(in_hbm(x) for x in fields)
    occupied, swap_slot = in_hbm(occupied), in_hbm(swap_slot)
    early, bulk = swap_pack(fields, occupied, swap_slot, owner)
    early = [pair_swap(early[bit], 1 << bit) for bit in range(BITS)]
    early, bulk = lax.optimization_barrier((early, bulk))
    bulk = [pair_swap(bulk[bit], 1 << bit) for bit in range(BITS)]
    mine = jnp.concatenate([neighbours.reshape(-1), send_list.reshape(-1), recv_list.reshape(-1)])
    lists = (pair_swap(mine, 1), odd_pair_swap(mine))
    top, bottom, faces = local(fields, occupied)
    ze, zo, ys = ends(top, bottom, faces, early, swap_slot, owner, mine, parity)
    sent, got, ya = (ze, zo), (pair_swap(ze, 1), odd_pair_swap(zo)), segment_swap(ys)
    wk, wf, dg, v, ys = first(
        swap_slot, owner, occupied, mine, parity, lists, got, ya, bulk, fields
    )
    v, ze, zo, ys, kept = second(
        v, wk, wf, sent, got, segment_swap(ys), mine, parity, lists
    )
    sent, got = (ze, zo), (pair_swap(ze, 1), odd_pair_swap(zo))
    v, ys = third(v, wk, wf, got, segment_swap(ys), mine, parity, lists)
    v, coarse = last(v, wk, wf, dg, kept, sent, got, segment_swap(ys), mine, parity, lists)
    return v.reshape(SLOTS, EDGE, PLANE), coarse.reshape(SLOTS, EDGE // 2, PLANE // 4)


def solution(mesh):
    wide, flat, single = P(("owner", "sub"), None, None), P(("owner", "sub"), None), P(("owner", "sub"))
    return jax.shard_map(
        body,
        mesh=mesh,
        in_specs=(wide, wide, wide, single, flat, flat, flat, flat),
        out_specs=(wide, wide),
        check_vma=False,
    )
```

```python
import jax
import jax.numpy as jnp
from jax import lax
from jax.experimental import pallas as pl
from jax.experimental.pallas import tpu as pltpu
from jax.sharding import PartitionSpec as P

OMEGA = 0.8
SLOTS = 8
EDGE = 32
PLANE = EDGE * EDGE
ROWS = SLOTS * EDGE
LANES = 128
COLS = PLANE // LANES
FIELD = (ROWS, PLANE)
TURNED = (ROWS + EDGE, PLANE)
FACES = 2 * SLOTS
TILE = (8, LANES)
BITS = 4
V1, V2, C1, C2, F1 = range(5)
KINDS = 5
SEND = 4 * SLOTS
RECV = SEND + FACES
LISTS = RECV + FACES
SMEM = pl.BlockSpec(memory_space=pltpu.SMEM)
VMEM = pl.BlockSpec(memory_space=pltpu.VMEM)
HBM = pl.BlockSpec(memory_space=pltpu.HBM)


def f32(*shape):
    return jax.ShapeDtypeStruct(shape, jnp.float32)


def tiles(count):
    return f32(count, *TILE)


def scratch(*shape):
    return pltpu.VMEM(shape, jnp.float32)


def params(mib):
    return pltpu.CompilerParams(vmem_limit_bytes=mib << 20)


def cost(flops, bytes_accessed):
    return pl.CostEstimate(flops=flops, bytes_accessed=bytes_accessed, transcendentals=0)


def column(c):
    return slice(c * LANES, (c + 1) * LANES)


def block_rows(j):
    return pl.ds(pl.multiple_of(j * EDGE, EDGE), EDGE)


def iotas(shape):
    rank = len(shape)
    sub = lax.broadcasted_iota(jnp.int32, shape, rank - 2)
    lane = lax.broadcasted_iota(jnp.int32, shape, rank - 1)
    return sub, lane


def slot_or(entry, none):
    return jnp.where(entry >= 0, jnp.maximum(entry, 0) % SLOTS, none)


def layer_tile(field, row, out, index):
    for c in range(COLS):
        out[index, c : c + 1, :] = field[row : row + 1, column(c)]


def face_of(cells, side, forth=None, back=None):
    group = lax.broadcasted_iota(jnp.int32, TILE, 1) // EDGE
    turned = {0: cells, EDGE: forth, LANES - EDGE: back}
    face = None
    for g in range(4):
        turn = (EDGE * g + EDGE * side) % LANES
        rows = slice(8 * g, 8 * g + 8)
        done = turned.get(turn)
        part = pltpu.roll(cells[rows], turn, 1) if done is None else done[rows]
        face = part if face is None else jnp.where(group == g, part, face)
    return face


def face_tile(field, first_row, side):
    return face_of(field[first_row : first_row + EDGE, column(COLS - 1 if side else 0)], side)


def unpack_face(face, side):
    parts = []
    for g in range(4):
        turn = (-EDGE * g - EDGE * side) % LANES
        parts.append(pltpu.roll(face, turn, 1) if turn else face)
    return jnp.concatenate(parts, axis=0)


def pick_faces(faces, mine, out, offset, stride):
    for entry in range(FACES):
        face = mine[SEND + entry]
        out[(entry // 2) * stride + entry % 2 + offset] = faces[jnp.maximum(face, 0)] * (face >= 0).astype(
            jnp.float32
        )


def place_faces(arrived, mine, ghost, offset, stride):
    ghost[...] = jnp.zeros(ghost.shape, jnp.float32)
    for entry in range(FACES):
        face = mine[RECV + entry]
        ghost[jnp.where(face >= 0, face, FACES)] = arrived[(entry // 2) * stride + entry % 2 + offset]


class Lists:
    def __init__(self, lists, side):
        self.lists, self.side = lists, side

    def at(self, i):
        return self.lists[self.side, i]

    def neighbour(self, slot, direction):
        return self.at(4 * slot + direction)

    def send(self, entry):
        return self.at(SEND + entry)

    def recv(self, entry):
        return self.at(RECV + entry)


def lists_tile(mine):
    sub, lane = iotas(TILE)
    tile = jnp.zeros(TILE, jnp.float32)
    for i in range(LISTS):
        tile = jnp.where(lane == i, mine[i].astype(jnp.float32), tile)
    return jnp.where(sub == 0, tile, 0.0)


def list_copies(ie, io, held, sems):
    return [
        pltpu.make_async_copy(source.at[KINDS * SLOTS], held.at[k], sems.at[k]) for k, source in enumerate((ie, io))
    ]


def read_lists(even, held, lists):
    for side in range(2):
        source = jnp.where(even, 1 - side, side)
        for i in range(LISTS):
            lists[side, i] = held[source, 0, i].astype(jnp.int32)
    return [Lists(lists, side) for side in range(2)]


def sheet_of(even, from_even, from_odd, kind, side):
    rows = slice(kind * SLOTS, (kind + 1) * SLOTS)
    pair = (from_even[rows], from_odd[rows])
    return jnp.where(even, *(pair if side else pair[::-1]))


def own_end(even, to_even, to_odd, kind, side):
    return sheet_of(even, to_even, to_odd, kind, side)


def fill_sheet(store, value):
    store[:SLOTS] = value
    store[SLOTS] = jnp.zeros(TILE, jnp.float32)


def pack_lines(sheets, lists, out, tile, stride):
    sub, lane = iotas(TILE)
    for peer in range(SLOTS):
        total = jnp.zeros(TILE, jnp.float32)
        row = 0
        for side in range(2):
            for i in range(2):
                face = lists[side].send(2 * peer + i)
                slot = jnp.where(face >= 0, jnp.maximum(face, 0) // 2, SLOTS)
                high = jnp.maximum(face, 0) % 2 == 1
                for store in sheets[side]:
                    line = store[slot]
                    low_line = line[0:1, :]
                    high_line = pltpu.roll(line, EDGE, 1)[7:8, :]
                    total = jnp.where(sub == row, jnp.where(high, high_line, low_line), total)
                    row += 1
        out[peer * stride + tile] = total


def place_lines(arrived, lists, edges, tile, stride):
    for pair in edges:
        for store in pair:
            store[...] = jnp.zeros(store.shape, jnp.float32)
    sub, lane = iotas(TILE)
    first = (sub == 0) & (lane < EDGE)
    final = (sub == 7) & (lane >= LANES - EDGE)
    for peer in range(SLOTS):
        got = arrived[peer * stride + tile]
        turned = pltpu.roll(got, LANES - EDGE, 1)
        row = 0
        for side in range(2):
            for i in range(2):
                ghost = lists[side].recv(2 * peer + i)
                slot = jnp.where(ghost >= 0, jnp.maximum(ghost, 0) // 2, SLOTS)
                high = jnp.maximum(ghost, 0) % 2 == 1
                for store in edges[side]:
                    low_part = jnp.where(first, got[row : row + 1, :], 0.0)
                    high_part = jnp.where(final, turned[row : row + 1, :], 0.0)
                    store[slot] = store[slot] + jnp.where(high, high_part, low_part)
                    row += 1


def sheet_around(store, inner, outer_tiles, edge, lists, side, gathered):
    shape = (SLOTS,) + TILE
    sub, lane = iotas(shape)
    x = lane % EDGE
    minus, plus, outer = gathered
    for slot in range(SLOTS):
        minus[slot] = store[slot_or(lists.neighbour(slot, 0), SLOTS)]
        plus[slot] = store[slot_or(lists.neighbour(slot, 1), SLOTS)]
        entry = lists.neighbour(slot, 2 if side else 3)
        outer[slot] = outer_tiles[slot_or(entry, 0)] * (entry >= 0).astype(jnp.float32)
    value = store[:SLOTS]
    edges = edge[:SLOTS]
    forth = pltpu.roll(value, EDGE, 2)
    back = pltpu.roll(value, LANES - EDGE, 2)
    before = jnp.where(lane < EDGE, pltpu.roll(forth, 1, 1), forth)
    after = jnp.where(lane >= LANES - EDGE, pltpu.roll(back, 7, 1), back)
    out = outer[...]
    return (
        jnp.where(x == 0, pltpu.roll(minus[...], LANES - EDGE + 1, 2), pltpu.roll(value, 1, 2)),
        jnp.where(x == EDGE - 1, pltpu.roll(plus[...], EDGE - 1, 2), pltpu.roll(value, LANES - 1, 2)),
        jnp.where((lane < EDGE) & (sub == 0), edges, before),
        jnp.where((lane >= LANES - EDGE) & (sub == 7), edges, after),
        out if side else inner,
        inner if side else out,
    )


def weights(k, around):
    faces = [0.5 * (k + jnp.where(other > 0.0, other, k)) for other in around]
    total = faces[0]
    for face in faces[1:]:
        total = total + face
    alive = k > 0.0
    weight = jnp.where(alive, OMEGA / jnp.where(alive, total, 1.0), 0.0)
    return [weight * face for face in faces], weight, jnp.where(alive, total * (1.0 / OMEGA), 0.0)


def six_turned(field, forth, back, j, mine, ghost, below, above):
    _, lane = iotas((EDGE, LANES))
    x = lane % EDGE
    xm, xp, zm, zp = [slot_or(mine[4 * j + side], SLOTS) for side in range(4)]
    under_face, over_face = below[zm], above[zp]
    own, minus_rows, plus_rows = block_rows(j), block_rows(xm), block_rows(xp)
    for c in range(COLS):
        v = field[own, column(c)]
        before = forth[own, column(c - 1)] if c else unpack_face(ghost[2 * j], 0)
        after = back[own, column(c + 1)] if c < COLS - 1 else unpack_face(ghost[2 * j + 1], 1)
        yield (
            c,
            v,
            (
                pltpu.roll(jnp.where(x == EDGE - 1, back[minus_rows, column(c)], v), 1, 1),
                pltpu.roll(jnp.where(x == 0, forth[plus_rows, column(c)], v), LANES - 1, 1),
                jnp.where(lane < EDGE, before, forth[own, column(c)]),
                jnp.where(lane >= LANES - EDGE, after, back[own, column(c)]),
                jnp.concatenate([under_face[c : c + 1, :], v[: EDGE - 1]], axis=0),
                jnp.concatenate([v[1:], over_face[c : c + 1, :]], axis=0),
            ),
        )


def store_swept(total, n, j, u, forth, back, faces):
    rows = block_rows(j)
    ahead, behind = pltpu.roll(total, EDGE, 1), pltpu.roll(total, LANES - EDGE, 1)
    u[rows, column(n)] = total
    forth[rows, column(n)] = ahead
    back[rows, column(n)] = behind
    if n in (0, COLS - 1):
        side = n // (COLS - 1)
        faces[2 * j + side] = face_of(total, side, ahead, behind)


def turn_block(field, j, forth, back):
    rows = block_rows(j)
    for c in range(COLS):
        cells = field[rows, column(c)]
        forth[rows, column(c)] = pltpu.roll(cells, EDGE, 1)
        back[rows, column(c)] = pltpu.roll(cells, LANES - EDGE, 1)


def end_turned(forth, back):
    for turned in (forth, back):
        turned[ROWS:, :] = jnp.zeros((EDGE, PLANE), jnp.float32)


def sweep_blocks(turned, mine, ghost, below, above, wk, wf, u, forth, back, faces):
    def one(j, carry):
        rows = block_rows(j)
        for n, centre, around in six_turned(*turned, j, mine, ghost, below, above):
            total = wf[rows, column(n)] + (1.0 - OMEGA) * centre
            for d in range(6):
                total = total + wk[d, rows, column(n)] * around[d]
            store_swept(total, n, j, u, forth, back, faces)
        return carry

    lax.fori_loop(0, SLOTS, one, 0)
    end_turned(forth, back)


def pair_slot(pairs, owner, bit):
    return pairs[0, owner[0] ^ (1 << bit)]


def block_tiles(v, f, c, row, out):
    for end in range(2):
        for kind, field, depth in ((V1, v, 0), (V2, v, 1), (C1, c, 0), (C2, c, 1), (F1, f, 0)):
            layer_tile(field, row + (depth if end else EDGE - 1 - depth), out, end * KINDS + kind)
    for k, field in enumerate((v, c)):
        for side in range(2):
            out[2 * KINDS + 2 * k + side] = face_tile(field, row, side)


def swap_pack_kernel(bits, pairs, owner, occupied, guess, rhs, coef, *refs):
    bulk, sems = refs[: len(bits)], refs[len(bits)]
    slots = [jnp.maximum(pair_slot(pairs, owner, bit), 0) for bit in bits]

    def copies(n):
        return [
            pltpu.make_async_copy(
                source.at[block_rows(slots[n])], bulk[n].at[pl.ds(k * EDGE, EDGE)], sems.at[n, k]
            )
            for k, source in enumerate((guess, rhs, coef))
        ]

    for n in range(len(bits)):
        for copy in copies(n):
            copy.start()
    for n in range(len(bits)):
        for copy in copies(n):
            copy.wait()

        @pl.when(occupied[slots[n]] == 0)
        def _(n=n):
            bulk[n][...] = jnp.zeros((3 * EDGE, PLANE), jnp.float32)


def swap_pack(fields, occupied, pairs, owner, bits):
    return pl.pallas_call(
        lambda *refs: swap_pack_kernel(bits, *refs),
        in_specs=[SMEM] * 3 + [HBM] * 3,
        out_specs=[VMEM] * len(bits),
        out_shape=[f32(3 * EDGE, PLANE)] * len(bits),
        scratch_shapes=[pltpu.SemaphoreType.DMA((len(bits), 3))],
        compiler_params=params(8),
        cost_estimate=cost(1 << 19, len(bits) * (768 << 10)),
        name="swap_pack",
    )(pairs, owner, occupied, *fields)


def local_kernel(
    occupied, neighbours, send_list, recv_list, guess, rhs, coef, top, bottom, faces, mine, v, f, c, forth_v, back_v, forth_c, back_c, sems
):
    copies = [
        pltpu.make_async_copy(source, target, sems.at[k])
        for k, (source, target) in enumerate(((guess, v), (coef, c), (rhs, f)))
    ]
    for copy in copies:
        copy.start()
    for slot in range(SLOTS):
        for side in range(4):
            mine[4 * slot + side] = neighbours[slot, side]
    for entry in range(FACES):
        mine[SEND + entry] = send_list[0, entry]
        mine[RECV + entry] = recv_list[0, entry]
    for k, (field, kinds) in enumerate(((v, (V1, V2)), (c, (C1, C2)), (f, (F1,)))):
        copies[k].wait()
        for j in range(SLOTS):

            @pl.when(occupied[j] == 0)
            def _(field=field, j=j):
                field[j * EDGE : (j + 1) * EDGE, :] = jnp.zeros((EDGE, PLANE), jnp.float32)

        for j in range(SLOTS):
            for depth, kind in enumerate(kinds):
                for end, out in enumerate((top, bottom)):
                    row = j * EDGE + (depth if end else EDGE - 1 - depth)
                    layer_tile(field, row, out, kind * SLOTS + j)
            if len(kinds) == 2:
                for side in range(2):
                    faces[k * FACES + 2 * j + side] = face_tile(field, j * EDGE, side)
    for field, forth, back in ((v, forth_v, back_v), (c, forth_c, back_c)):

        def one(j, carry, field=field, forth=forth, back=back):
            turn_block(field, j, forth, back)
            return carry

        lax.fori_loop(0, SLOTS, one, 0)
        end_turned(forth, back)


def local(fields, occupied, neighbours, send_list, recv_list):
    return pl.pallas_call(
        local_kernel,
        in_specs=[SMEM] * 4 + [HBM] * 3,
        out_specs=[VMEM] * 3 + [SMEM] + [VMEM] * 7,
        out_shape=[tiles(KINDS * SLOTS)] * 2
        + [tiles(2 * FACES), jax.ShapeDtypeStruct((LISTS,), jnp.int32)]
        + [f32(*FIELD)] * 3
        + [f32(*TURNED)] * 4,
        scratch_shapes=[pltpu.SemaphoreType.DMA((3,))],
        compiler_params=params(8),
        cost_estimate=cost(1 << 20, 4 << 20),
        name="local",
    )(occupied, neighbours, send_list, recv_list, *fields)


def ends_kernel(pairs, owner, mine, parity, top, bottom, faces, *refs):
    bulk = refs[:BITS]
    ze, zo, ys, held, fresh = refs[BITS:]
    even = parity[0] == 0
    ze[: KINDS * SLOTS] = jnp.where(even, top[...], bottom[...])
    zo[: KINDS * SLOTS] = jnp.where(even, bottom[...], top[...])
    ze[KINDS * SLOTS] = zo[KINDS * SLOTS] = lists_tile(mine)
    held[...] = faces[...]
    for bit in range(BITS):
        slot = pair_slot(pairs, owner, bit)

        @pl.when(slot >= 0)
        def _(bit=bit, slot=jnp.maximum(slot, 0)):
            block_tiles(*(bulk[bit].at[pl.ds(k * EDGE, EDGE)] for k in range(3)), 0, fresh)
            for kind in range(KINDS):
                high, low = fresh[kind], fresh[KINDS + kind]
                ze[kind * SLOTS + slot] = jnp.where(even, high, low)
                zo[kind * SLOTS + slot] = jnp.where(even, low, high)
            for k in range(2):
                for side in range(2):
                    held[k * FACES + 2 * slot + side] = fresh[2 * KINDS + 2 * k + side]

    for k in range(2):
        pick_faces(held.at[pl.ds(k * FACES, FACES)], mine, ys, 2 * k, 4)

def ends(top, bottom, faces, bulk, pairs, owner, mine, parity):
    return pl.pallas_call(
        ends_kernel,
        in_specs=[SMEM] * 4 + [VMEM] * (3 + BITS),
        out_specs=[VMEM] * 3,
        out_shape=[tiles(KINDS * SLOTS + 1)] * 2 + [tiles(2 * FACES)],
        scratch_shapes=[scratch(2 * FACES, *TILE), scratch(2 * KINDS + 4, *TILE)],
        compiler_params=params(8),
        cost_estimate=cost(1 << 18, 1 << 20),
        name="ends",
    )(pairs, owner, mine, parity, top, bottom, faces, *bulk)


def first_kernel(pairs, owner, mine, parity, ie, io, ya, *refs):
    bulk, refs = refs[:BITS], refs[BITS + len(MERGED) :]
    v, f, c, forth_v, back_v, forth_c, back_c = refs[: len(MERGED)]
    wk, wf, dg, u, forth, back, ys, lists_out = refs[len(MERGED) : len(MERGED) + 8]
    ghost, ghost_c, below, above, below_c, above_c, faces, held, list_sems, sems = refs[len(MERGED) + 8 :]
    even = parity[0] == 0
    slots = [pair_slot(pairs, owner, bit) for bit in range(BITS)]

    def merges(k):
        for bit in range(BITS):
            copy = pltpu.make_async_copy(
                bulk[bit].at[pl.ds(k * EDGE, EDGE)],
                (v, f, c)[k].at[block_rows(jnp.maximum(slots[bit], 0))],
                sems.at[bit, k],
            )
            yield slots[bit], copy

    def start(k):
        for slot, copy in merges(k):

            @pl.when(slot >= 0)
            def _(copy=copy):
                copy.start()

    def settle(k, field=None, forth=None, back=None):
        for slot, copy in merges(k):

            @pl.when(slot >= 0)
            def _(slot=jnp.maximum(slot, 0), copy=copy):
                copy.wait()
                if field is not None:
                    turn_block(field, slot, forth, back)

    copies = list_copies(ie, io, held, list_sems)
    for copy in copies:
        copy.start()
    for k in (2, 1, 0):
        start(k)
    sheets = ((below, below_c), (above, above_c))
    for side in range(2):
        for store, kind in zip(sheets[side], (V1, C1)):
            fill_sheet(store, sheet_of(even, ie, io, kind, side))
    place_faces(ya, mine, ghost, 0, 4)
    place_faces(ya, mine, ghost_c, 2, 4)
    for copy in copies:
        copy.wait()
    lists = read_lists(even, held, lists_out)
    pack_lines(sheets, lists, ys, 2, 3)
    settle(2, c, forth_c, back_c)
    settle(1)

    def one(j, carry):
        rows = block_rows(j)
        for n, k, around in six_turned(c, forth_c, back_c, j, mine, ghost_c, below_c, above_c):
            scaled, weight, inverse = weights(k, around)
            for d in range(6):
                wk[d, rows, column(n)] = scaled[d]
            wf[rows, column(n)] = weight * f[rows, column(n)]
            dg[rows, column(n)] = inverse
        return carry

    lax.fori_loop(0, SLOTS, one, 0)
    settle(0, v, forth_v, back_v)
    sweep_blocks((v, forth_v, back_v), mine, ghost, below, above, wk, wf, u, forth, back, faces)
    pick_faces(faces, mine, ys, 0, 3)


SHEET = scratch(SLOTS + 1, *TILE)
GHOSTS = scratch(FACES + 1, *TILE)
GATHERED = [scratch(SLOTS, *TILE)] * 3


MERGED = [f32(*FIELD)] * 3 + [f32(*TURNED)] * 4


def first(merged, bulk, ends_in, ya, pairs, owner, mine, parity):
    outs = pl.pallas_call(
        first_kernel,
        in_specs=[SMEM] * 4 + [VMEM] * (3 + BITS + len(MERGED)),
        out_specs=[VMEM] * (len(MERGED) + 7) + [SMEM],
        out_shape=MERGED
        + [f32(6, *FIELD)]
        + [f32(*FIELD)] * 3
        + [f32(*TURNED)] * 2
        + [tiles(3 * SLOTS), jax.ShapeDtypeStruct((2, LISTS), jnp.int32)],
        input_output_aliases={7 + BITS + k: k for k in range(len(MERGED))},
        scratch_shapes=[GHOSTS] * 2
        + [SHEET] * 4
        + [scratch(FACES, *TILE), pltpu.SMEM((2,) + TILE, jnp.float32), pltpu.SemaphoreType.DMA((2,))]
        + [pltpu.SemaphoreType.DMA((BITS, 3))],
        compiler_params=params(20),
        cost_estimate=cost(1 << 24, 12 << 20),
        name="first",
    )(pairs, owner, mine, parity, *ends_in, ya, *bulk, *merged)
    return outs[len(MERGED) :]


def second_kernel(
    mine, parity, lists_in,
    v, forth_in, back_in, wk, wf, ye, yo, ie, io, ya,
    u, forth, back, ze, zo, ys, kept,
    ghost, below, above, below_c, above_c, edge_bv, edge_bc, edge_av, edge_ac, gm, gp, go, faces, ends_out,
):
    even = parity[0] == 0
    lists = [Lists(lists_in, side) for side in range(2)]
    place_faces(ya, mine, ghost, 0, 3)
    edges = ((edge_bv, edge_bc), (edge_av, edge_ac))
    place_lines(ya, lists, edges, 2, 3)
    for side, (store, store_c) in enumerate(((below, below_c), (above, above_c))):
        fill_sheet(store, sheet_of(even, ie, io, V1, side))
        fill_sheet(store_c, sheet_of(even, ie, io, C1, side))
        k = store_c[:SLOTS]
        ends_out[...] = own_end(even, ye, yo, C1, side)
        inner = sheet_of(even, ie, io, C2, side)
        around = sheet_around(store_c, inner, ends_out, edges[side][1], lists[side], side, (gm, gp, go))
        scaled, weight, _ = weights(k, around)
        forced = weight * sheet_of(even, ie, io, F1, side)
        for d in range(6):
            kept[(side * 7 + d) * SLOTS : (side * 7 + d + 1) * SLOTS] = scaled[d]
        kept[(side * 7 + 6) * SLOTS : (side * 7 + 7) * SLOTS] = forced
        ends_out[...] = own_end(even, ye, yo, V1, side)
        inner = sheet_of(even, ie, io, V2, side)
        around = sheet_around(store, inner, ends_out, edges[side][0], lists[side], side, (gm, gp, go))
        total = forced + (1.0 - OMEGA) * store[:SLOTS]
        for d in range(6):
            total = total + scaled[d] * around[d]
        store[:SLOTS] = total
    sweep_blocks((v, forth_in, back_in), mine, ghost, below, above, wk, wf, u, forth, back, faces)
    pick_faces(faces, mine, ys, 0, 2)
    for j in range(SLOTS):
        for depth in range(2):
            layer_tile(u, j * EDGE + EDGE - 1 - depth, ends_out, 0)
            layer_tile(u, j * EDGE + depth, ends_out, 1)
            ze[depth * SLOTS + j] = jnp.where(even, ends_out[0], ends_out[1])
            zo[depth * SLOTS + j] = jnp.where(even, ends_out[1], ends_out[0])


def second(turned, wk, wf, sent, got, ya, mine, parity, lists):
    return pl.pallas_call(
        second_kernel,
        in_specs=[SMEM] * 3 + [VMEM] * 10,
        out_specs=[VMEM] * 7,
        out_shape=[f32(*FIELD), f32(*TURNED), f32(*TURNED), tiles(2 * SLOTS), tiles(2 * SLOTS), tiles(FACES), tiles(14 * SLOTS)],
        scratch_shapes=[GHOSTS] + [SHEET] * 8 + GATHERED + [scratch(FACES, *TILE), scratch(SLOTS, *TILE)],
        compiler_params=params(16),
        cost_estimate=cost(1 << 22, 9 << 20),
        name="second",
    )(mine, parity, lists, *turned, wk, wf, *sent, *got, ya)


def third_kernel(
    mine, parity, lists_in,
    v, forth_in, back_in, wk, wf, ie, io, ya,
    u, forth, back, ys,
    ghost, below, above, faces,
):
    even = parity[0] == 0
    lists = [Lists(lists_in, side) for side in range(2)]
    place_faces(ya, mine, ghost, 0, 2)
    for side, store in enumerate((below, above)):
        fill_sheet(store, sheet_of(even, ie, io, V1, side))
    pack_lines(((below,), (above,)), lists, ys, 2, 3)
    sweep_blocks((v, forth_in, back_in), mine, ghost, below, above, wk, wf, u, forth, back, faces)
    pick_faces(faces, mine, ys, 0, 3)


def third(turned, wk, wf, got, ya, mine, parity, lists):
    return pl.pallas_call(
        third_kernel,
        in_specs=[SMEM] * 3 + [VMEM] * 8,
        out_specs=[VMEM] * 4,
        out_shape=[f32(*FIELD), f32(*TURNED), f32(*TURNED), tiles(3 * SLOTS)],
        scratch_shapes=[GHOSTS] + [SHEET] * 2 + [scratch(FACES, *TILE)],
        compiler_params=params(16),
        cost_estimate=cost(1 << 22, 9 << 20),
        name="third",
    )(mine, parity, lists, *turned, wk, wf, *got, ya)


def last_kernel(
    mine, parity, lists_in,
    v, forth_in, back_in, wk, wf, dg, kept, ye, yo, ie, io, ya,
    out, coarse,
    ghost, below, above, edge_b, edge_a, gm, gp, go, ends_out, residual, sem,
):
    write = pltpu.make_async_copy(v, out, sem)
    write.start()
    even = parity[0] == 0
    lists = [Lists(lists_in, side) for side in range(2)]
    place_faces(ya, mine, ghost, 0, 3)
    edges = ((edge_b,), (edge_a,))
    place_lines(ya, lists, edges, 2, 3)
    for side, store in enumerate((below, above)):
        fill_sheet(store, sheet_of(even, ie, io, V1, side))
        ends_out[...] = own_end(even, ye, yo, V1, side)
        inner = sheet_of(even, ie, io, V2, side)
        around = sheet_around(store, inner, ends_out, edges[side][0], lists[side], side, (gm, gp, go))
        total = kept[(side * 7 + 6) * SLOTS : (side * 7 + 7) * SLOTS] + (1.0 - OMEGA) * store[:SLOTS]
        for d in range(6):
            total = total + kept[(side * 7 + d) * SLOTS : (side * 7 + d + 1) * SLOTS] * around[d]
        store[:SLOTS] = total

    def one(j, carry):
        rows = block_rows(j)
        for n, centre, around in six_turned(v, forth_in, back_in, j, mine, ghost, below, above):
            total = wf[rows, column(n)] - OMEGA * centre
            for d in range(6):
                total = total + wk[d, rows, column(n)] * around[d]
            residual[n, rows, :] = total * dg[rows, column(n)]
        return carry

    lax.fori_loop(0, SLOTS, one, 0)
    lane = lax.broadcasted_iota(jnp.int32, (LANES, LANES), 0)
    target = lax.broadcasted_iota(jnp.int32, (LANES, LANES), 1)
    place = (lane // (2 * EDGE)) * (EDGE // 2) + (lane % EDGE) // 2
    half = ROWS // 2
    for part in range(2):
        total = jnp.zeros((half, LANES), jnp.float32)
        for n in range(4):
            column_sum = (
                residual[part * 4 + n, pl.ds(0, half, stride=2), :]
                + residual[part * 4 + n, pl.ds(1, half, stride=2), :]
            )
            gather = jnp.where(place + EDGE * n == target, 0.125, 0.0)
            total = total + jnp.dot(
                column_sum, gather, precision=lax.Precision.HIGHEST, preferred_element_type=jnp.float32
            )
        coarse[:, part * LANES : (part + 1) * LANES] = total
    write.wait()


def last(turned, wk, wf, dg, kept, sent, got, ya, mine, parity, lists):
    return pl.pallas_call(
        last_kernel,
        in_specs=[SMEM] * 3 + [VMEM] * 12,
        out_specs=[HBM, VMEM],
        out_shape=[f32(*FIELD), f32(ROWS // 2, PLANE // 4)],
        scratch_shapes=[GHOSTS] + [SHEET] * 4 + GATHERED + [scratch(SLOTS, *TILE), scratch(COLS, ROWS, LANES), pltpu.SemaphoreType.DMA]
       ,
        compiler_params=params(16),
        cost_estimate=cost(1 << 24, 10 << 20),
        name="last",
    )(mine, parity, lists, *turned, wk, wf, dg, kept, *sent, *got, ya)


def pair_swap(values, stride):
    count = lax.axis_size("owner")
    return lax.ppermute(values, "owner", [(i, i ^ stride) for i in range(count)])


def odd_pair_swap(values):
    count = lax.axis_size("owner")
    return lax.ppermute(values, "owner", [(i, ((i - 1) ^ 1) + 1) for i in range(1, count - 1)])


def in_hbm(values):
    return pltpu.with_memory_space_constraint(values, pltpu.HBM)


def segment_swap(ys):
    return lax.all_to_all(ys, "sub", split_axis=0, concat_axis=0, tiled=True)


def body(guess, rhs, coef, occupied, neighbours, swap_slot, send_list, recv_list):
    my_owner = lax.axis_index("owner").astype(jnp.int32)
    owner = my_owner.reshape(1)
    parity = (my_owner % 2).reshape(1)
    fields = tuple(values.reshape(FIELD) for values in (guess, rhs, coef))
    fields = tuple(in_hbm(x) for x in fields)
    occupied, swap_slot = in_hbm(occupied), in_hbm(swap_slot)
    bulk = [None] * BITS
    for bits in ((0, 2, 1, 3),):
        for bit, block in zip(bits, swap_pack(fields, occupied, swap_slot, owner, bits)):
            bulk[bit] = pair_swap(block, 1 << bit)
    top, bottom, faces, mine, *merged = local(fields, occupied, neighbours, in_hbm(send_list), in_hbm(recv_list))
    ze, zo, ys = ends(top, bottom, faces, bulk, swap_slot, owner, mine, parity)
    sent, got, ya = (ze, zo), (pair_swap(ze, 1), odd_pair_swap(zo)), segment_swap(ys)
    wk, wf, dg, v, forth, back, ys, lists = first(merged, bulk, got, ya, swap_slot, owner, mine, parity)
    turned = v, forth, back
    *turned, ze, zo, ys, kept = second(turned, wk, wf, sent, got, segment_swap(ys), mine, parity, lists)
    sent, got = (ze, zo), (pair_swap(ze, 1), odd_pair_swap(zo))
    *turned, ys = third(turned, wk, wf, got, segment_swap(ys), mine, parity, lists)
    v, coarse = last(turned, wk, wf, dg, kept, sent, got, segment_swap(ys), mine, parity, lists)
    return v.reshape(SLOTS, EDGE, PLANE), coarse.reshape(SLOTS, EDGE // 2, PLANE // 4)


def solution(mesh):
    wide, flat, single = P(("owner", "sub"), None, None), P(("owner", "sub"), None), P(("owner", "sub"))
    return jax.shard_map(
        body,
        mesh=mesh,
        in_specs=(wide, wide, wide, single, flat, flat, flat, flat),
        out_specs=(wide, wide),
        check_vma=False,
    )
```

```python
import jax
import jax.numpy as jnp
from jax import lax
from jax.experimental import pallas as pl
from jax.experimental.pallas import tpu as pltpu
from jax.sharding import PartitionSpec as P

OMEGA = 0.8
SLOTS = 8
EDGE = 32
PLANE = EDGE * EDGE
ROWS = SLOTS * EDGE
LANES = 128
COLS = PLANE // LANES
FIELD = (ROWS, PLANE)
TURNED = (ROWS + EDGE, PLANE)
FACES = 2 * SLOTS
TILE = (8, LANES)
BITS = 4
ORDER = (0, 2, 1, 3)
V1, V2, C1, C2, F1 = range(5)
KINDS = 5
SEND = 4 * SLOTS
RECV = SEND + FACES
LISTS = RECV + FACES
SMEM = pl.BlockSpec(memory_space=pltpu.SMEM)
VMEM = pl.BlockSpec(memory_space=pltpu.VMEM)
HBM = pl.BlockSpec(memory_space=pltpu.HBM)


def f32(*shape):
    return jax.ShapeDtypeStruct(shape, jnp.float32)


def tiles(count):
    return f32(count, *TILE)


def scratch(*shape):
    return pltpu.VMEM(shape, jnp.float32)


def params(mib):
    return pltpu.CompilerParams(vmem_limit_bytes=mib << 20)


def cost(flops, bytes_accessed):
    return pl.CostEstimate(flops=flops, bytes_accessed=bytes_accessed, transcendentals=0)


def column(c):
    return slice(c * LANES, (c + 1) * LANES)


def block_rows(j):
    return pl.ds(pl.multiple_of(j * EDGE, EDGE), EDGE)


def iotas(shape):
    rank = len(shape)
    sub = lax.broadcasted_iota(jnp.int32, shape, rank - 2)
    lane = lax.broadcasted_iota(jnp.int32, shape, rank - 1)
    return sub, lane


def slot_or(entry, none):
    return jnp.where(entry >= 0, jnp.maximum(entry, 0) % SLOTS, none)


def layer_tile(field, row, out, index):
    for c in range(COLS):
        out[index, c : c + 1, :] = field[row : row + 1, column(c)]


def face_of(cells, side, forth=None, back=None):
    group = lax.broadcasted_iota(jnp.int32, TILE, 1) // EDGE
    turned = {0: cells, EDGE: forth, LANES - EDGE: back}
    face = None
    for g in range(4):
        turn = (EDGE * g + EDGE * side) % LANES
        rows = slice(8 * g, 8 * g + 8)
        done = turned.get(turn)
        part = pltpu.roll(cells[rows], turn, 1) if done is None else done[rows]
        face = part if face is None else jnp.where(group == g, part, face)
    return face


def face_tile(field, first_row, side):
    return face_of(field[first_row : first_row + EDGE, column(COLS - 1 if side else 0)], side)


def unpack_face(face, side):
    parts = []
    for g in range(4):
        turn = (-EDGE * g - EDGE * side) % LANES
        parts.append(pltpu.roll(face, turn, 1) if turn else face)
    return jnp.concatenate(parts, axis=0)


def pick_faces(faces, mine, out, offset, stride):
    for entry in range(FACES):
        face = mine[SEND + entry]
        out[(entry // 2) * stride + entry % 2 + offset] = faces[jnp.maximum(face, 0)] * (face >= 0).astype(
            jnp.float32
        )


def place_faces(arrived, mine, ghost, offset, stride):
    ghost[...] = jnp.zeros(ghost.shape, jnp.float32)
    for entry in range(FACES):
        face = mine[RECV + entry]
        ghost[jnp.where(face >= 0, face, FACES)] = arrived[(entry // 2) * stride + entry % 2 + offset]


class Lists:
    def __init__(self, lists, side):
        self.lists, self.side = lists, side

    def at(self, i):
        return self.lists[self.side, i]

    def neighbour(self, slot, direction):
        return self.at(4 * slot + direction)

    def send(self, entry):
        return self.at(SEND + entry)

    def recv(self, entry):
        return self.at(RECV + entry)


def lists_tile(mine):
    sub, lane = iotas(TILE)
    tile = jnp.zeros(TILE, jnp.float32)
    for i in range(LISTS):
        tile = jnp.where(lane == i, mine[i].astype(jnp.float32), tile)
    return jnp.where(sub == 0, tile, 0.0)


def list_copies(ie, io, held, sems):
    return [
        pltpu.make_async_copy(source.at[KINDS * SLOTS], held.at[k], sems.at[k]) for k, source in enumerate((ie, io))
    ]


def read_lists(even, held, lists):
    for side in range(2):
        source = jnp.where(even, 1 - side, side)
        for i in range(LISTS):
            lists[side, i] = held[source, 0, i].astype(jnp.int32)
    return [Lists(lists, side) for side in range(2)]


def sheet_of(even, from_even, from_odd, kind, side):
    rows = slice(kind * SLOTS, (kind + 1) * SLOTS)
    pair = (from_even[rows], from_odd[rows])
    return jnp.where(even, *(pair if side else pair[::-1]))


def own_end(even, to_even, to_odd, kind, side):
    return sheet_of(even, to_even, to_odd, kind, side)


def fill_sheet(store, value):
    store[:SLOTS] = value
    store[SLOTS] = jnp.zeros(TILE, jnp.float32)


def pack_lines(sheets, lists, out, tile, stride):
    sub, lane = iotas(TILE)
    for peer in range(SLOTS):
        total = jnp.zeros(TILE, jnp.float32)
        row = 0
        for side in range(2):
            for i in range(2):
                face = lists[side].send(2 * peer + i)
                slot = jnp.where(face >= 0, jnp.maximum(face, 0) // 2, SLOTS)
                high = jnp.maximum(face, 0) % 2 == 1
                for store in sheets[side]:
                    line = store[slot]
                    low_line = line[0:1, :]
                    high_line = pltpu.roll(line, EDGE, 1)[7:8, :]
                    total = jnp.where(sub == row, jnp.where(high, high_line, low_line), total)
                    row += 1
        out[peer * stride + tile] = total


def place_lines(arrived, lists, edges, tile, stride):
    for pair in edges:
        for store in pair:
            store[...] = jnp.zeros(store.shape, jnp.float32)
    sub, lane = iotas(TILE)
    first = (sub == 0) & (lane < EDGE)
    final = (sub == 7) & (lane >= LANES - EDGE)
    for peer in range(SLOTS):
        got = arrived[peer * stride + tile]
        turned = pltpu.roll(got, LANES - EDGE, 1)
        row = 0
        for side in range(2):
            for i in range(2):
                ghost = lists[side].recv(2 * peer + i)
                slot = jnp.where(ghost >= 0, jnp.maximum(ghost, 0) // 2, SLOTS)
                high = jnp.maximum(ghost, 0) % 2 == 1
                for store in edges[side]:
                    low_part = jnp.where(first, got[row : row + 1, :], 0.0)
                    high_part = jnp.where(final, turned[row : row + 1, :], 0.0)
                    store[slot] = store[slot] + jnp.where(high, high_part, low_part)
                    row += 1


def sheet_around(store, inner, outer_tiles, edge, lists, side, gathered):
    shape = (SLOTS,) + TILE
    sub, lane = iotas(shape)
    x = lane % EDGE
    minus, plus, outer = gathered
    for slot in range(SLOTS):
        minus[slot] = store[slot_or(lists.neighbour(slot, 0), SLOTS)]
        plus[slot] = store[slot_or(lists.neighbour(slot, 1), SLOTS)]
        entry = lists.neighbour(slot, 2 if side else 3)
        outer[slot] = outer_tiles[slot_or(entry, 0)] * (entry >= 0).astype(jnp.float32)
    value = store[:SLOTS]
    edges = edge[:SLOTS]
    forth = pltpu.roll(value, EDGE, 2)
    back = pltpu.roll(value, LANES - EDGE, 2)
    before = jnp.where(lane < EDGE, pltpu.roll(forth, 1, 1), forth)
    after = jnp.where(lane >= LANES - EDGE, pltpu.roll(back, 7, 1), back)
    out = outer[...]
    return (
        jnp.where(x == 0, pltpu.roll(minus[...], LANES - EDGE + 1, 2), pltpu.roll(value, 1, 2)),
        jnp.where(x == EDGE - 1, pltpu.roll(plus[...], EDGE - 1, 2), pltpu.roll(value, LANES - 1, 2)),
        jnp.where((lane < EDGE) & (sub == 0), edges, before),
        jnp.where((lane >= LANES - EDGE) & (sub == 7), edges, after),
        out if side else inner,
        inner if side else out,
    )


def weights(k, around):
    faces = [k + jnp.where(other > 0.0, other, k) for other in around]
    total = (faces[0] + faces[1]) + (faces[2] + faces[3]) + (faces[4] + faces[5])
    alive = k > 0.0
    factor = jnp.where(alive, OMEGA / total, 0.0)
    return [factor * face for face in faces], 2.0 * factor, jnp.where(alive, total * (0.5 / OMEGA), 0.0)


def six_turned(field, forth, back, j, mine, ghost, below, above):
    _, lane = iotas((EDGE, LANES))
    x = lane % EDGE
    xm, xp, zm, zp = [slot_or(mine[4 * j + side], SLOTS) for side in range(4)]
    under_face, over_face = below[zm], above[zp]
    own, minus_rows, plus_rows = block_rows(j), block_rows(xm), block_rows(xp)
    for c in range(COLS):
        v = field[own, column(c)]
        before = forth[own, column(c - 1)] if c else unpack_face(ghost[2 * j], 0)
        after = back[own, column(c + 1)] if c < COLS - 1 else unpack_face(ghost[2 * j + 1], 1)
        yield (
            c,
            v,
            (
                pltpu.roll(jnp.where(x == EDGE - 1, back[minus_rows, column(c)], v), 1, 1),
                pltpu.roll(jnp.where(x == 0, forth[plus_rows, column(c)], v), LANES - 1, 1),
                jnp.where(lane < EDGE, before, forth[own, column(c)]),
                jnp.where(lane >= LANES - EDGE, after, back[own, column(c)]),
                jnp.concatenate([under_face[c : c + 1, :], v[: EDGE - 1]], axis=0),
                jnp.concatenate([v[1:], over_face[c : c + 1, :]], axis=0),
            ),
        )


def store_swept(total, n, j, u, forth, back, faces):
    rows = block_rows(j)
    ahead, behind = pltpu.roll(total, EDGE, 1), pltpu.roll(total, LANES - EDGE, 1)
    u[rows, column(n)] = total
    forth[rows, column(n)] = ahead
    back[rows, column(n)] = behind
    if n in (0, COLS - 1):
        side = n // (COLS - 1)
        faces[2 * j + side] = face_of(total, side, ahead, behind)


def turn_block(field, j, forth, back):
    rows = block_rows(j)
    for c in range(COLS):
        cells = field[rows, column(c)]
        forth[rows, column(c)] = pltpu.roll(cells, EDGE, 1)
        back[rows, column(c)] = pltpu.roll(cells, LANES - EDGE, 1)


def end_turned(forth, back):
    for turned in (forth, back):
        turned[ROWS:, :] = jnp.zeros((EDGE, PLANE), jnp.float32)


def sweep_blocks(turned, mine, ghost, below, above, wk, wf, u, forth, back, faces):
    def one(j, carry):
        rows = block_rows(j)
        for n, centre, around in six_turned(*turned, j, mine, ghost, below, above):
            total = wf[rows, column(n)] + (1.0 - OMEGA) * centre
            for d in range(6):
                total = total + wk[d, rows, column(n)] * around[d]
            store_swept(total, n, j, u, forth, back, faces)
        return carry

    lax.fori_loop(0, SLOTS, one, 0)
    end_turned(forth, back)


def pair_slot(pairs, owner, bit):
    return pairs[0, owner[0] ^ (1 << bit)]


def block_tiles(v, f, c, row, out):
    for end in range(2):
        for kind, field, depth in ((V1, v, 0), (V2, v, 1), (C1, c, 0), (C2, c, 1), (F1, f, 0)):
            layer_tile(field, row + (depth if end else EDGE - 1 - depth), out, end * KINDS + kind)
    for k, field in enumerate((v, c)):
        for side in range(2):
            out[2 * KINDS + 2 * k + side] = face_tile(field, row, side)


def swap_pack_kernel(bits, pairs, owner, occupied, guess, rhs, coef, *refs):
    bulk, sems = refs[: len(bits)], refs[len(bits)]
    slots = [jnp.maximum(pair_slot(pairs, owner, bit), 0) for bit in bits]

    def copies(n):
        return [
            pltpu.make_async_copy(
                source.at[block_rows(slots[n])], bulk[n].at[pl.ds(k * EDGE, EDGE)], sems.at[n, k]
            )
            for k, source in enumerate((guess, rhs, coef))
        ]

    for n in range(len(bits)):
        for copy in copies(n):
            copy.start()
    for n in range(len(bits)):
        for copy in copies(n):
            copy.wait()

        @pl.when(occupied[slots[n]] == 0)
        def _(n=n):
            bulk[n][...] = jnp.zeros((3 * EDGE, PLANE), jnp.float32)


def swap_pack(fields, occupied, pairs, owner, bits):
    return pl.pallas_call(
        lambda *refs: swap_pack_kernel(bits, *refs),
        in_specs=[SMEM] * 3 + [HBM] * 3,
        out_specs=[VMEM] * len(bits),
        out_shape=[f32(3 * EDGE, PLANE)] * len(bits),
        scratch_shapes=[pltpu.SemaphoreType.DMA((len(bits), 3))],
        compiler_params=params(8),
        cost_estimate=cost(1 << 19, len(bits) * (768 << 10)),
        name="swap_pack",
    )(pairs, owner, occupied, *fields)


def local_kernel(
    occupied, neighbours, send_list, recv_list, guess, rhs, coef, top, bottom, faces, mine, v, f, c, forth_v, back_v, forth_c, back_c, sems
):
    copies = [
        pltpu.make_async_copy(source, target, sems.at[k])
        for k, (source, target) in enumerate(((guess, v), (coef, c), (rhs, f)))
    ]
    for copy in copies:
        copy.start()
    for slot in range(SLOTS):
        for side in range(4):
            mine[4 * slot + side] = neighbours[slot, side]
    for entry in range(FACES):
        mine[SEND + entry] = send_list[0, entry]
        mine[RECV + entry] = recv_list[0, entry]
    for k, (field, kinds) in enumerate(((v, (V1, V2)), (c, (C1, C2)), (f, (F1,)))):
        copies[k].wait()
        for j in range(SLOTS):

            @pl.when(occupied[j] == 0)
            def _(field=field, j=j):
                field[j * EDGE : (j + 1) * EDGE, :] = jnp.zeros((EDGE, PLANE), jnp.float32)

        for j in range(SLOTS):
            for depth, kind in enumerate(kinds):
                for end, out in enumerate((top, bottom)):
                    row = j * EDGE + (depth if end else EDGE - 1 - depth)
                    layer_tile(field, row, out, kind * SLOTS + j)
            if len(kinds) == 2:
                for side in range(2):
                    faces[k * FACES + 2 * j + side] = face_tile(field, j * EDGE, side)
    for field, forth, back in ((v, forth_v, back_v), (c, forth_c, back_c)):

        def one(j, carry, field=field, forth=forth, back=back):
            turn_block(field, j, forth, back)
            return carry

        lax.fori_loop(0, SLOTS, one, 0)
        end_turned(forth, back)


def local(fields, occupied, neighbours, send_list, recv_list):
    return pl.pallas_call(
        local_kernel,
        in_specs=[SMEM] * 4 + [HBM] * 3,
        out_specs=[VMEM] * 3 + [SMEM] + [VMEM] * 7,
        out_shape=[tiles(KINDS * SLOTS)] * 2
        + [tiles(2 * FACES), jax.ShapeDtypeStruct((LISTS,), jnp.int32)]
        + [f32(*FIELD)] * 3
        + [f32(*TURNED)] * 4,
        scratch_shapes=[pltpu.SemaphoreType.DMA((3,))],
        compiler_params=params(8),
        cost_estimate=cost(1 << 20, 4 << 20),
        name="local",
    )(occupied, neighbours, send_list, recv_list, *fields)


def ends_kernel(pairs, owner, mine, parity, top, bottom, faces, *refs):
    bulk = dict(zip(ORDER, refs))
    ze, zo, ys, held, fresh = refs[BITS:]
    even = parity[0] == 0
    ze[: KINDS * SLOTS] = jnp.where(even, top[...], bottom[...])
    zo[: KINDS * SLOTS] = jnp.where(even, bottom[...], top[...])
    ze[KINDS * SLOTS] = zo[KINDS * SLOTS] = lists_tile(mine)
    held[...] = faces[...]
    for bit in range(BITS):
        slot = pair_slot(pairs, owner, bit)

        @pl.when(slot >= 0)
        def _(bit=bit, slot=jnp.maximum(slot, 0)):
            block_tiles(*(bulk[bit].at[pl.ds(k * EDGE, EDGE)] for k in range(3)), 0, fresh)
            for kind in range(KINDS):
                high, low = fresh[kind], fresh[KINDS + kind]
                ze[kind * SLOTS + slot] = jnp.where(even, high, low)
                zo[kind * SLOTS + slot] = jnp.where(even, low, high)
            for k in range(2):
                for side in range(2):
                    held[k * FACES + 2 * slot + side] = fresh[2 * KINDS + 2 * k + side]

    for k in range(2):
        pick_faces(held.at[pl.ds(k * FACES, FACES)], mine, ys, 2 * k, 4)

def ends(top, bottom, faces, bulk, pairs, owner, mine, parity):
    return pl.pallas_call(
        ends_kernel,
        in_specs=[SMEM] * 4 + [VMEM] * (3 + BITS),
        out_specs=[VMEM] * 3,
        out_shape=[tiles(KINDS * SLOTS + 1)] * 2 + [tiles(2 * FACES)],
        scratch_shapes=[scratch(2 * FACES, *TILE), scratch(2 * KINDS + 4, *TILE)],
        compiler_params=params(8),
        cost_estimate=cost(1 << 18, 1 << 20),
        name="ends",
    )(pairs, owner, mine, parity, top, bottom, faces, *bulk)


def first_kernel(pairs, owner, mine, parity, ie, io, ya, *refs):
    bulk, refs = dict(zip(ORDER, refs)), refs[BITS + len(MERGED) :]
    v, f, c, forth_v, back_v, forth_c, back_c = refs[: len(MERGED)]
    wk, wf, dg, u, forth, back, ys, lists_out = refs[len(MERGED) : len(MERGED) + 8]
    ghost, ghost_c, below, above, below_c, above_c, faces, held, list_sems, sems = refs[len(MERGED) + 8 :]
    even = parity[0] == 0
    slots = [pair_slot(pairs, owner, bit) for bit in range(BITS)]

    def merges(k):
        for bit in range(BITS):
            copy = pltpu.make_async_copy(
                bulk[bit].at[pl.ds(k * EDGE, EDGE)],
                (v, f, c)[k].at[block_rows(jnp.maximum(slots[bit], 0))],
                sems.at[bit, k],
            )
            yield slots[bit], copy

    def start(k):
        for slot, copy in merges(k):

            @pl.when(slot >= 0)
            def _(copy=copy):
                copy.start()

    def settle(k, field=None, forth=None, back=None):
        for slot, copy in merges(k):

            @pl.when(slot >= 0)
            def _(slot=jnp.maximum(slot, 0), copy=copy):
                copy.wait()
                if field is not None:
                    turn_block(field, slot, forth, back)

    copies = list_copies(ie, io, held, list_sems)
    for copy in copies:
        copy.start()
    for k in (2, 1, 0):
        start(k)
    sheets = ((below, below_c), (above, above_c))
    for side in range(2):
        for store, kind in zip(sheets[side], (V1, C1)):
            fill_sheet(store, sheet_of(even, ie, io, kind, side))
    place_faces(ya, mine, ghost, 0, 4)
    place_faces(ya, mine, ghost_c, 2, 4)
    for copy in copies:
        copy.wait()
    lists = read_lists(even, held, lists_out)
    pack_lines(sheets, lists, ys, 2, 3)
    settle(2, c, forth_c, back_c)
    settle(1)
    settle(0, v, forth_v, back_v)

    def one(j, carry):
        rows = block_rows(j)
        conduct = six_turned(c, forth_c, back_c, j, mine, ghost_c, below_c, above_c)
        iterate = six_turned(v, forth_v, back_v, j, mine, ghost, below, above)
        for (n, k, around_k), (_, centre, around) in zip(conduct, iterate):
            scaled, weight, inverse = weights(k, around_k)
            forced = weight * f[rows, column(n)]
            wf[rows, column(n)] = forced
            dg[rows, column(n)] = inverse
            total = forced + (1.0 - OMEGA) * centre
            for d in range(6):
                wk[d, rows, column(n)] = scaled[d]
                total = total + scaled[d] * around[d]
            store_swept(total, n, j, u, forth, back, faces)
        return carry

    lax.fori_loop(0, SLOTS, one, 0)
    end_turned(forth, back)
    pick_faces(faces, mine, ys, 0, 3)


SHEET = scratch(SLOTS + 1, *TILE)
GHOSTS = scratch(FACES + 1, *TILE)
GATHERED = [scratch(SLOTS, *TILE)] * 3


MERGED = [f32(*FIELD)] * 3 + [f32(*TURNED)] * 4


def first(merged, bulk, ends_in, ya, pairs, owner, mine, parity):
    outs = pl.pallas_call(
        first_kernel,
        in_specs=[SMEM] * 4 + [VMEM] * (3 + BITS + len(MERGED)),
        out_specs=[VMEM] * (len(MERGED) + 7) + [SMEM],
        out_shape=MERGED
        + [f32(6, *FIELD)]
        + [f32(*FIELD)] * 3
        + [f32(*TURNED)] * 2
        + [tiles(3 * SLOTS), jax.ShapeDtypeStruct((2, LISTS), jnp.int32)],
        input_output_aliases={7 + BITS + k: k for k in range(len(MERGED))},
        scratch_shapes=[GHOSTS] * 2
        + [SHEET] * 4
        + [scratch(FACES, *TILE), pltpu.SMEM((2,) + TILE, jnp.float32), pltpu.SemaphoreType.DMA((2,))]
        + [pltpu.SemaphoreType.DMA((BITS, 3))],
        compiler_params=params(20),
        cost_estimate=cost(1 << 24, 12 << 20),
        name="first",
    )(pairs, owner, mine, parity, *ends_in, ya, *bulk, *merged)
    return outs[len(MERGED) :]


def second_kernel(
    mine, parity, lists_in,
    v, forth_in, back_in, wk, wf, ye, yo, ie, io, ya,
    u, forth, back, ze, zo, ys, kept,
    ghost, below, above, below_c, above_c, edge_bv, edge_bc, edge_av, edge_ac, gm, gp, go, faces, ends_out,
):
    even = parity[0] == 0
    lists = [Lists(lists_in, side) for side in range(2)]
    place_faces(ya, mine, ghost, 0, 3)
    edges = ((edge_bv, edge_bc), (edge_av, edge_ac))
    place_lines(ya, lists, edges, 2, 3)
    for side, (store, store_c) in enumerate(((below, below_c), (above, above_c))):
        fill_sheet(store, sheet_of(even, ie, io, V1, side))
        fill_sheet(store_c, sheet_of(even, ie, io, C1, side))
        k = store_c[:SLOTS]
        ends_out[...] = own_end(even, ye, yo, C1, side)
        inner = sheet_of(even, ie, io, C2, side)
        around = sheet_around(store_c, inner, ends_out, edges[side][1], lists[side], side, (gm, gp, go))
        scaled, weight, _ = weights(k, around)
        forced = weight * sheet_of(even, ie, io, F1, side)
        for d in range(6):
            kept[(side * 7 + d) * SLOTS : (side * 7 + d + 1) * SLOTS] = scaled[d]
        kept[(side * 7 + 6) * SLOTS : (side * 7 + 7) * SLOTS] = forced
        ends_out[...] = own_end(even, ye, yo, V1, side)
        inner = sheet_of(even, ie, io, V2, side)
        around = sheet_around(store, inner, ends_out, edges[side][0], lists[side], side, (gm, gp, go))
        total = forced + (1.0 - OMEGA) * store[:SLOTS]
        for d in range(6):
            total = total + scaled[d] * around[d]
        store[:SLOTS] = total
    sweep_blocks((v, forth_in, back_in), mine, ghost, below, above, wk, wf, u, forth, back, faces)
    pick_faces(faces, mine, ys, 0, 2)
    for j in range(SLOTS):
        for depth in range(2):
            layer_tile(u, j * EDGE + EDGE - 1 - depth, ends_out, 0)
            layer_tile(u, j * EDGE + depth, ends_out, 1)
            ze[depth * SLOTS + j] = jnp.where(even, ends_out[0], ends_out[1])
            zo[depth * SLOTS + j] = jnp.where(even, ends_out[1], ends_out[0])


def second(turned, wk, wf, sent, got, ya, mine, parity, lists):
    return pl.pallas_call(
        second_kernel,
        in_specs=[SMEM] * 3 + [VMEM] * 10,
        out_specs=[VMEM] * 7,
        out_shape=[f32(*FIELD), f32(*TURNED), f32(*TURNED), tiles(2 * SLOTS), tiles(2 * SLOTS), tiles(FACES), tiles(14 * SLOTS)],
        scratch_shapes=[GHOSTS] + [SHEET] * 8 + GATHERED + [scratch(FACES, *TILE), scratch(SLOTS, *TILE)],
        compiler_params=params(16),
        cost_estimate=cost(1 << 22, 9 << 20),
        name="second",
    )(mine, parity, lists, *turned, wk, wf, *sent, *got, ya)


def third_kernel(
    mine, parity, lists_in,
    v, forth_in, back_in, wk, wf, ie, io, ya,
    u, forth, back, ys,
    ghost, below, above, faces,
):
    even = parity[0] == 0
    lists = [Lists(lists_in, side) for side in range(2)]
    place_faces(ya, mine, ghost, 0, 2)
    for side, store in enumerate((below, above)):
        fill_sheet(store, sheet_of(even, ie, io, V1, side))
    pack_lines(((below,), (above,)), lists, ys, 2, 3)
    sweep_blocks((v, forth_in, back_in), mine, ghost, below, above, wk, wf, u, forth, back, faces)
    pick_faces(faces, mine, ys, 0, 3)


def third(turned, wk, wf, got, ya, mine, parity, lists):
    return pl.pallas_call(
        third_kernel,
        in_specs=[SMEM] * 3 + [VMEM] * 8,
        out_specs=[VMEM] * 4,
        out_shape=[f32(*FIELD), f32(*TURNED), f32(*TURNED), tiles(3 * SLOTS)],
        scratch_shapes=[GHOSTS] + [SHEET] * 2 + [scratch(FACES, *TILE)],
        compiler_params=params(16),
        cost_estimate=cost(1 << 22, 9 << 20),
        name="third",
    )(mine, parity, lists, *turned, wk, wf, *got, ya)


def last_kernel(
    mine, parity, lists_in,
    v, forth_in, back_in, wk, wf, dg, kept, ye, yo, ie, io, ya,
    out, coarse,
    ghost, below, above, edge_b, edge_a, gm, gp, go, ends_out, residual, sem,
):
    write = pltpu.make_async_copy(v, out, sem)
    write.start()
    even = parity[0] == 0
    lists = [Lists(lists_in, side) for side in range(2)]
    place_faces(ya, mine, ghost, 0, 3)
    edges = ((edge_b,), (edge_a,))
    place_lines(ya, lists, edges, 2, 3)
    for side, store in enumerate((below, above)):
        fill_sheet(store, sheet_of(even, ie, io, V1, side))
        ends_out[...] = own_end(even, ye, yo, V1, side)
        inner = sheet_of(even, ie, io, V2, side)
        around = sheet_around(store, inner, ends_out, edges[side][0], lists[side], side, (gm, gp, go))
        total = kept[(side * 7 + 6) * SLOTS : (side * 7 + 7) * SLOTS] + (1.0 - OMEGA) * store[:SLOTS]
        for d in range(6):
            total = total + kept[(side * 7 + d) * SLOTS : (side * 7 + d + 1) * SLOTS] * around[d]
        store[:SLOTS] = total

    def one(j, carry):
        rows = block_rows(j)
        for n, centre, around in six_turned(v, forth_in, back_in, j, mine, ghost, below, above):
            total = wf[rows, column(n)] - OMEGA * centre
            for d in range(6):
                total = total + wk[d, rows, column(n)] * around[d]
            residual[n, rows, :] = total * dg[rows, column(n)]
        return carry

    lax.fori_loop(0, SLOTS, one, 0)
    lane = lax.broadcasted_iota(jnp.int32, (LANES, LANES), 0)
    target = lax.broadcasted_iota(jnp.int32, (LANES, LANES), 1)
    place = (lane // (2 * EDGE)) * (EDGE // 2) + (lane % EDGE) // 2
    half = ROWS // 2
    for part in range(2):
        total = jnp.zeros((half, LANES), jnp.float32)
        for n in range(4):
            column_sum = (
                residual[part * 4 + n, pl.ds(0, half, stride=2), :]
                + residual[part * 4 + n, pl.ds(1, half, stride=2), :]
            )
            gather = jnp.where(place + EDGE * n == target, 0.125, 0.0)
            total = total + jnp.dot(
                column_sum, gather, precision=lax.Precision.HIGHEST, preferred_element_type=jnp.float32
            )
        coarse[:, part * LANES : (part + 1) * LANES] = total
    write.wait()


def last(turned, wk, wf, dg, kept, sent, got, ya, mine, parity, lists):
    return pl.pallas_call(
        last_kernel,
        in_specs=[SMEM] * 3 + [VMEM] * 12,
        out_specs=[HBM, VMEM],
        out_shape=[f32(*FIELD), f32(ROWS // 2, PLANE // 4)],
        scratch_shapes=[GHOSTS] + [SHEET] * 4 + GATHERED + [scratch(SLOTS, *TILE), scratch(COLS, ROWS, LANES), pltpu.SemaphoreType.DMA]
       ,
        compiler_params=params(16),
        cost_estimate=cost(1 << 24, 10 << 20),
        name="last",
    )(mine, parity, lists, *turned, wk, wf, dg, kept, *sent, *got, ya)


def pair_swap(values, stride):
    count = lax.axis_size("owner")
    return lax.ppermute(values, "owner", [(i, i ^ stride) for i in range(count)])


def odd_pair_swap(values):
    count = lax.axis_size("owner")
    return lax.ppermute(values, "owner", [(i, ((i - 1) ^ 1) + 1) for i in range(1, count - 1)])


def in_hbm(values):
    return pltpu.with_memory_space_constraint(values, pltpu.HBM)


def segment_swap(ys):
    return lax.all_to_all(ys, "sub", split_axis=0, concat_axis=0, tiled=True)


def body(guess, rhs, coef, occupied, neighbours, swap_slot, send_list, recv_list):
    my_owner = lax.axis_index("owner").astype(jnp.int32)
    owner = my_owner.reshape(1)
    parity = (my_owner % 2).reshape(1)
    fields = tuple(values.reshape(FIELD) for values in (guess, rhs, coef))
    fields = tuple(in_hbm(x) for x in fields)
    occupied, swap_slot = in_hbm(occupied), in_hbm(swap_slot)
    bulk = swap_pack(fields, occupied, swap_slot, owner, ORDER)
    bulk = [pair_swap(block, 1 << bit) for bit, block in zip(ORDER, bulk)]
    top, bottom, faces, mine, *merged = local(fields, occupied, neighbours, in_hbm(send_list), in_hbm(recv_list))
    ze, zo, ys = ends(top, bottom, faces, bulk, swap_slot, owner, mine, parity)
    sent, got, ya = (ze, zo), (pair_swap(ze, 1), odd_pair_swap(zo)), segment_swap(ys)
    wk, wf, dg, v, forth, back, ys, lists = first(merged, bulk, got, ya, swap_slot, owner, mine, parity)
    turned = v, forth, back
    *turned, ze, zo, ys, kept = second(turned, wk, wf, sent, got, segment_swap(ys), mine, parity, lists)
    sent, got = (ze, zo), (pair_swap(ze, 1), odd_pair_swap(zo))
    *turned, ys = third(turned, wk, wf, got, segment_swap(ys), mine, parity, lists)
    v, coarse = last(turned, wk, wf, dg, kept, sent, got, segment_swap(ys), mine, parity, lists)
    return v.reshape(SLOTS, EDGE, PLANE), coarse.reshape(SLOTS, EDGE // 2, PLANE // 4)


def solution(mesh):
    wide, flat, single = P(("owner", "sub"), None, None), P(("owner", "sub"), None), P(("owner", "sub"))
    return jax.shard_map(
        body,
        mesh=mesh,
        in_specs=(wide, wide, wide, single, flat, flat, flat, flat),
        out_specs=(wide, wide),
        check_vma=False,
    )
```

```python
import jax
import jax.numpy as jnp
from jax import lax
from jax.experimental import pallas as pl
from jax.experimental.pallas import tpu as pltpu
from jax.sharding import PartitionSpec as P

OMEGA = 0.8
SLOTS = 8
EDGE = 32
PLANE = EDGE * EDGE
ROWS = SLOTS * EDGE
LANES = 128
COLS = PLANE // LANES
FIELD = (ROWS, PLANE)
TURNED = (ROWS + EDGE, PLANE)
FACES = 2 * SLOTS
TILE = (8, LANES)
BITS = 4
ORDER = (2, 0, 3, 1)
V, C, F = 0, 4, 8
KINDS = 11
DEPTHS = (3, 2, 1)
SEND = 4 * SLOTS
RECV = SEND + FACES
LISTS = RECV + FACES
SMEM = pl.BlockSpec(memory_space=pltpu.SMEM)
VMEM = pl.BlockSpec(memory_space=pltpu.VMEM)
HBM = pl.BlockSpec(memory_space=pltpu.HBM)


def f32(*shape):
    return jax.ShapeDtypeStruct(shape, jnp.float32)


def tiles(count):
    return f32(count, *TILE)


def scratch(*shape):
    return pltpu.VMEM(shape, jnp.float32)


def params(mib):
    return pltpu.CompilerParams(vmem_limit_bytes=mib << 20)


def cost(flops, bytes_accessed):
    return pl.CostEstimate(flops=flops, bytes_accessed=bytes_accessed, transcendentals=0)


def column(c):
    return slice(c * LANES, (c + 1) * LANES)


def block_rows(j):
    return pl.ds(pl.multiple_of(j * EDGE, EDGE), EDGE)


def iotas(shape):
    rank = len(shape)
    sub = lax.broadcasted_iota(jnp.int32, shape, rank - 2)
    lane = lax.broadcasted_iota(jnp.int32, shape, rank - 1)
    return sub, lane


def slot_or(entry, none):
    return jnp.where(entry >= 0, jnp.maximum(entry, 0) % SLOTS, none)


def layer_tile(field, row, out, index):
    for c in range(COLS):
        out[index, c : c + 1, :] = field[row : row + 1, column(c)]


def face_of(cells, side, forth=None, back=None):
    group = lax.broadcasted_iota(jnp.int32, TILE, 1) // EDGE
    turned = {0: cells, EDGE: forth, LANES - EDGE: back}
    face = None
    for g in range(4):
        turn = (EDGE * g + EDGE * side) % LANES
        rows = slice(8 * g, 8 * g + 8)
        done = turned.get(turn)
        part = pltpu.roll(cells[rows], turn, 1) if done is None else done[rows]
        face = part if face is None else jnp.where(group == g, part, face)
    return face


def face_tile(field, first_row, side):
    return face_of(field[first_row : first_row + EDGE, column(COLS - 1 if side else 0)], side)


def unpack_face(face, side):
    parts = []
    for g in range(4):
        turn = (-EDGE * g - EDGE * side) % LANES
        parts.append(pltpu.roll(face, turn, 1) if turn else face)
    return jnp.concatenate(parts, axis=0)


def pick_faces(faces, mine, out, offset, stride):
    for entry in range(FACES):
        face = mine[SEND + entry]
        out[(entry // 2) * stride + entry % 2 + offset] = faces[jnp.maximum(face, 0)] * (face >= 0).astype(
            jnp.float32
        )


def place_faces(arrived, mine, ghost, offset, stride):
    ghost[...] = jnp.zeros(ghost.shape, jnp.float32)
    for entry in range(FACES):
        face = mine[RECV + entry]
        ghost[jnp.where(face >= 0, face, FACES)] = arrived[(entry // 2) * stride + entry % 2 + offset]


class Lists:
    def __init__(self, lists, side):
        self.lists, self.side = lists, side

    def at(self, i):
        return self.lists[self.side, i]

    def neighbour(self, slot, direction):
        return self.at(4 * slot + direction)

    def send(self, entry):
        return self.at(SEND + entry)

    def recv(self, entry):
        return self.at(RECV + entry)


def lists_tile(mine):
    sub, lane = iotas(TILE)
    tile = jnp.zeros(TILE, jnp.float32)
    for i in range(LISTS):
        tile = jnp.where(lane == i, mine[i].astype(jnp.float32), tile)
    return jnp.where(sub == 0, tile, 0.0)


def list_copies(ie, io, held, sems):
    return [
        pltpu.make_async_copy(source.at[KINDS * SLOTS], held.at[k], sems.at[k]) for k, source in enumerate((ie, io))
    ]


def read_lists(even, held, lists):
    for side in range(2):
        source = jnp.where(even, 1 - side, side)
        for i in range(LISTS):
            lists[side, i] = held[source, 0, i].astype(jnp.int32)
    return [Lists(lists, side) for side in range(2)]


def sheet_of(even, from_even, from_odd, kind, side):
    rows = slice(kind * SLOTS, (kind + 1) * SLOTS)
    pair = (from_even[rows], from_odd[rows])
    return jnp.where(even, *(pair if side else pair[::-1]))


def own_end(even, to_even, to_odd, kind, side):
    return sheet_of(even, to_even, to_odd, kind, side)


def fill_sheet(store, value):
    store[:SLOTS] = value
    store[SLOTS] = jnp.zeros(TILE, jnp.float32)


def pack_lines(sheets, lists, out, tile, stride):
    sub, lane = iotas(TILE)
    for peer in range(SLOTS):
        totals = []
        row = 0
        for side in range(2):
            for i in range(2):
                face = lists[side].send(2 * peer + i)
                slot = jnp.where(face >= 0, jnp.maximum(face, 0) // 2, SLOTS)
                high = jnp.maximum(face, 0) % 2 == 1
                for store in sheets[side]:
                    line = store[slot]
                    low_line = line[0:1, :]
                    high_line = pltpu.roll(line, EDGE, 1)[7:8, :]
                    if row % 8 == 0:
                        totals.append(jnp.zeros(TILE, jnp.float32))
                    totals[-1] = jnp.where(sub == row % 8, jnp.where(high, high_line, low_line), totals[-1])
                    row += 1
        total = totals[0]
        for group, part in enumerate(totals[1:], 1):
            total = jnp.where(lane // EDGE == group, pltpu.roll(part, EDGE * group, 1), total)
        out[peer * stride + tile] = total


def place_lines(arrived, lists, edges, tile, stride):
    for stores in edges:
        for store in stores:
            store[...] = jnp.zeros(store.shape, jnp.float32)
    sub, lane = iotas(TILE)
    first = (sub == 0) & (lane < EDGE)
    final = (sub == 7) & (lane >= LANES - EDGE)
    groups = (4 * len(edges[0]) + 7) // 8
    for peer in range(SLOTS):
        got = arrived[peer * stride + tile]
        turned = [got] + [pltpu.roll(got, LANES - EDGE * g, 1) for g in range(1, groups + 1)]
        row = 0
        for side in range(2):
            for i in range(2):
                ghost = lists[side].recv(2 * peer + i)
                slot = jnp.where(ghost >= 0, jnp.maximum(ghost, 0) // 2, SLOTS)
                high = jnp.maximum(ghost, 0) % 2 == 1
                for store in edges[side]:
                    group, at = row // 8, row % 8
                    low_part = jnp.where(first, turned[group][at : at + 1, :], 0.0)
                    high_part = jnp.where(final, turned[group + 1][at : at + 1, :], 0.0)
                    store[slot] = store[slot] + jnp.where(high, high_part, low_part)
                    row += 1


def beyond(ends, lists, side, gathered):
    for slot in range(SLOTS):
        entry = lists.neighbour(slot, 2 if side else 3)
        gathered[slot] = ends[slot_or(entry, 0)] * (entry >= 0).astype(jnp.float32)
    return gathered[...]


def sheet_around(store, inner, outer, edge, lists, side, gathered):
    shape = (SLOTS,) + TILE
    sub, lane = iotas(shape)
    x = lane % EDGE
    minus, plus = gathered
    for slot in range(SLOTS):
        minus[slot] = store[slot_or(lists.neighbour(slot, 0), SLOTS)]
        plus[slot] = store[slot_or(lists.neighbour(slot, 1), SLOTS)]
    value = store[:SLOTS]
    edges = edge[:SLOTS]
    forth = pltpu.roll(value, EDGE, 2)
    back = pltpu.roll(value, LANES - EDGE, 2)
    before = jnp.where(lane < EDGE, pltpu.roll(forth, 1, 1), forth)
    after = jnp.where(lane >= LANES - EDGE, pltpu.roll(back, 7, 1), back)
    return (
        jnp.where(x == 0, pltpu.roll(minus[...], LANES - EDGE + 1, 2), pltpu.roll(value, 1, 2)),
        jnp.where(x == EDGE - 1, pltpu.roll(plus[...], EDGE - 1, 2), pltpu.roll(value, LANES - 1, 2)),
        jnp.where((lane < EDGE) & (sub == 0), edges, before),
        jnp.where((lane >= LANES - EDGE) & (sub == 7), edges, after),
        outer if side else inner,
        inner if side else outer,
    )


def layers(ref, index):
    return ref[index * SLOTS : (index + 1) * SLOTS]


def keep_layers(ref, index, value):
    ref[index * SLOTS : (index + 1) * SLOTS] = value


def swept(value, forced, scaled, around):
    total = forced + (1.0 - OMEGA) * value
    for d in range(6):
        total = total + scaled[d] * around[d]
    return total


def kept_index(side, depth):
    return 7 * (2 * side + depth)


def sweep_sheets(sheets, ends, kept, depths, stores, edges, lists, gathered):
    minus, plus, touching = gathered
    for side in range(2):
        old = [layers(sheets, side * (depths + 1) + depth) for depth in range(depths + 1)]
        for depth in range(depths):
            fill_sheet(stores[side][depth], old[depth])
        outer = beyond(ends.at[pl.ds(side * SLOTS, SLOTS)], lists[side], side, touching)
        fresh = []
        for depth in range(depths):
            around = sheet_around(
                stores[side][depth], old[depth + 1], outer, edges[side][depth], lists[side], side, (minus, plus)
            )
            at = kept_index(side, depth)
            scaled = [layers(kept, at + d) for d in range(6)]
            fresh.append(swept(old[depth], layers(kept, at + 6), scaled, around))
            outer = old[depth]
        for depth in range(depths):
            fill_sheet(stores[side][depth], fresh[depth])


def own_ends(v, out):
    for j in range(SLOTS):
        layer_tile(v, j * EDGE, out, j)
        layer_tile(v, j * EDGE + EDGE - 1, out, SLOTS + j)


def weights(k, around):
    faces = [k + jnp.where(other > 0.0, other, k) for other in around]
    total = (faces[0] + faces[1]) + (faces[2] + faces[3]) + (faces[4] + faces[5])
    alive = k > 0.0
    factor = jnp.where(alive, OMEGA / total, 0.0)
    return [factor * face for face in faces], 2.0 * factor, jnp.where(alive, total * (0.5 / OMEGA), 0.0)


def six_turned(field, forth, back, j, mine, ghost, below, above):
    _, lane = iotas((EDGE, LANES))
    x = lane % EDGE
    xm, xp, zm, zp = [slot_or(mine[4 * j + side], SLOTS) for side in range(4)]
    under_face, over_face = below[zm], above[zp]
    own, minus_rows, plus_rows = block_rows(j), block_rows(xm), block_rows(xp)
    for c in range(COLS):
        v = field[own, column(c)]
        before = forth[own, column(c - 1)] if c else unpack_face(ghost[2 * j], 0)
        after = back[own, column(c + 1)] if c < COLS - 1 else unpack_face(ghost[2 * j + 1], 1)
        yield (
            c,
            v,
            (
                pltpu.roll(jnp.where(x == EDGE - 1, back[minus_rows, column(c)], v), 1, 1),
                pltpu.roll(jnp.where(x == 0, forth[plus_rows, column(c)], v), LANES - 1, 1),
                jnp.where(lane < EDGE, before, forth[own, column(c)]),
                jnp.where(lane >= LANES - EDGE, after, back[own, column(c)]),
                jnp.concatenate([under_face[c : c + 1, :], v[: EDGE - 1]], axis=0),
                jnp.concatenate([v[1:], over_face[c : c + 1, :]], axis=0),
            ),
        )


def store_swept(total, n, j, u, forth, back, faces):
    rows = block_rows(j)
    ahead, behind = pltpu.roll(total, EDGE, 1), pltpu.roll(total, LANES - EDGE, 1)
    u[rows, column(n)] = total
    forth[rows, column(n)] = ahead
    back[rows, column(n)] = behind
    if n in (0, COLS - 1):
        side = n // (COLS - 1)
        faces[2 * j + side] = face_of(total, side, ahead, behind)


def turn_block(field, j, forth, back):
    rows = block_rows(j)
    for c in range(COLS):
        cells = field[rows, column(c)]
        forth[rows, column(c)] = pltpu.roll(cells, EDGE, 1)
        back[rows, column(c)] = pltpu.roll(cells, LANES - EDGE, 1)


def end_turned(forth, back):
    for turned in (forth, back):
        turned[ROWS:, :] = jnp.zeros((EDGE, PLANE), jnp.float32)


def sweep_blocks(turned, mine, ghost, below, above, wk, wf, u, forth, back, faces):
    def one(j, carry):
        rows = block_rows(j)
        for n, centre, around in six_turned(*turned, j, mine, ghost, below, above):
            total = wf[rows, column(n)] + (1.0 - OMEGA) * centre
            for d in range(6):
                total = total + wk[d, rows, column(n)] * around[d]
            store_swept(total, n, j, u, forth, back, faces)
        return carry

    lax.fori_loop(0, SLOTS, one, 0)
    end_turned(forth, back)


def pair_slot(pairs, owner, bit):
    return pairs[0, owner[0] ^ (1 << bit)]


def block_tiles(v, f, c, row, out):
    for end in range(2):
        for kind, field, count in ((V, v, 4), (C, c, 4), (F, f, 3)):
            for depth in range(count):
                layer_tile(field, row + (depth if end else EDGE - 1 - depth), out, end * KINDS + kind + depth)
    for k, field in enumerate((v, c)):
        for side in range(2):
            out[2 * KINDS + 2 * k + side] = face_tile(field, row, side)


def swap_pack_kernel(bits, pairs, owner, occupied, guess, rhs, coef, *refs):
    bulk, sems = refs[: len(bits)], refs[len(bits)]
    slots = [jnp.maximum(pair_slot(pairs, owner, bit), 0) for bit in bits]

    def copies(n):
        return [
            pltpu.make_async_copy(
                source.at[block_rows(slots[n])], bulk[n].at[pl.ds(k * EDGE, EDGE)], sems.at[n, k]
            )
            for k, source in enumerate((guess, rhs, coef))
        ]

    for n in range(len(bits)):
        for copy in copies(n):
            copy.start()
    for n in range(len(bits)):
        for copy in copies(n):
            copy.wait()

        @pl.when(occupied[slots[n]] == 0)
        def _(n=n):
            bulk[n][...] = jnp.zeros((3 * EDGE, PLANE), jnp.float32)


def swap_pack(fields, occupied, pairs, owner, bits):
    return pl.pallas_call(
        lambda *refs: swap_pack_kernel(bits, *refs),
        in_specs=[SMEM] * 3 + [HBM] * 3,
        out_specs=[VMEM] * len(bits),
        out_shape=[f32(3 * EDGE, PLANE)] * len(bits),
        scratch_shapes=[pltpu.SemaphoreType.DMA((len(bits), 3))],
        compiler_params=params(8),
        cost_estimate=cost(1 << 19, len(bits) * (768 << 10)),
        name="swap_pack",
    )(pairs, owner, occupied, *fields)


def local_kernel(
    occupied, neighbours, send_list, recv_list, guess, rhs, coef, top, bottom, faces, mine, v, f, c, forth_v, back_v, forth_c, back_c, sems
):
    copies = [
        pltpu.make_async_copy(source, target, sems.at[k])
        for k, (source, target) in enumerate(((guess, v), (coef, c), (rhs, f)))
    ]
    for copy in copies:
        copy.start()
    for slot in range(SLOTS):
        for side in range(4):
            mine[4 * slot + side] = neighbours[slot, side]
    for entry in range(FACES):
        mine[SEND + entry] = send_list[0, entry]
        mine[RECV + entry] = recv_list[0, entry]
    for k, (field, kinds) in enumerate(((v, range(V, C)), (c, range(C, F)), (f, range(F, KINDS)))):
        copies[k].wait()
        for j in range(SLOTS):

            @pl.when(occupied[j] == 0)
            def _(field=field, j=j):
                field[j * EDGE : (j + 1) * EDGE, :] = jnp.zeros((EDGE, PLANE), jnp.float32)

        for j in range(SLOTS):
            for depth, kind in enumerate(kinds):
                for end, out in enumerate((top, bottom)):
                    row = j * EDGE + (depth if end else EDGE - 1 - depth)
                    layer_tile(field, row, out, kind * SLOTS + j)
            if k < 2:
                for side in range(2):
                    faces[k * FACES + 2 * j + side] = face_tile(field, j * EDGE, side)
    for field, forth, back in ((v, forth_v, back_v), (c, forth_c, back_c)):

        def one(j, carry, field=field, forth=forth, back=back):
            turn_block(field, j, forth, back)
            return carry

        lax.fori_loop(0, SLOTS, one, 0)
        end_turned(forth, back)


def local(fields, occupied, neighbours, send_list, recv_list):
    return pl.pallas_call(
        local_kernel,
        in_specs=[SMEM] * 4 + [HBM] * 3,
        out_specs=[VMEM] * 3 + [SMEM] + [VMEM] * 7,
        out_shape=[tiles(KINDS * SLOTS)] * 2
        + [tiles(2 * FACES), jax.ShapeDtypeStruct((LISTS,), jnp.int32)]
        + [f32(*FIELD)] * 3
        + [f32(*TURNED)] * 4,
        scratch_shapes=[pltpu.SemaphoreType.DMA((3,))],
        compiler_params=params(8),
        cost_estimate=cost(1 << 20, 4 << 20),
        name="local",
    )(occupied, neighbours, send_list, recv_list, *fields)


def ends_kernel(pairs, owner, mine, parity, top, bottom, faces, *refs):
    bulk = dict(zip(ORDER, refs))
    ze, zo, ys, held, fresh = refs[BITS:]
    even = parity[0] == 0
    ze[: KINDS * SLOTS] = jnp.where(even, top[...], bottom[...])
    zo[: KINDS * SLOTS] = jnp.where(even, bottom[...], top[...])
    ze[KINDS * SLOTS] = zo[KINDS * SLOTS] = lists_tile(mine)
    held[...] = faces[...]
    for bit in range(BITS):
        slot = pair_slot(pairs, owner, bit)

        @pl.when(slot >= 0)
        def _(bit=bit, slot=jnp.maximum(slot, 0)):
            block_tiles(*(bulk[bit].at[pl.ds(k * EDGE, EDGE)] for k in range(3)), 0, fresh)
            for kind in range(KINDS):
                high, low = fresh[kind], fresh[KINDS + kind]
                ze[kind * SLOTS + slot] = jnp.where(even, high, low)
                zo[kind * SLOTS + slot] = jnp.where(even, low, high)
            for k in range(2):
                for side in range(2):
                    held[k * FACES + 2 * slot + side] = fresh[2 * KINDS + 2 * k + side]

    for k in range(2):
        pick_faces(held.at[pl.ds(k * FACES, FACES)], mine, ys, 2 * k, 4)

def ends(top, bottom, faces, bulk, pairs, owner, mine, parity):
    return pl.pallas_call(
        ends_kernel,
        in_specs=[SMEM] * 4 + [VMEM] * (3 + BITS),
        out_specs=[VMEM] * 3,
        out_shape=[tiles(KINDS * SLOTS + 1)] * 2 + [tiles(2 * FACES)],
        scratch_shapes=[scratch(2 * FACES, *TILE), scratch(2 * KINDS + 4, *TILE)],
        compiler_params=params(8),
        cost_estimate=cost(1 << 18, 1 << 20),
        name="ends",
    )(pairs, owner, mine, parity, top, bottom, faces, *bulk)


def first_kernel(pairs, owner, mine, parity, ie, io, ya, *refs):
    bulk, refs = dict(zip(ORDER, refs)), refs[BITS + len(MERGED) :]
    v, f, c, forth_v, back_v, forth_c, back_c = refs[: len(MERGED)]
    wk, wf, dg, u, forth, back, ys, lists_out = refs[len(MERGED) : len(MERGED) + 8]
    ghost, ghost_c, faces, held, list_sems, sems, *sheet_refs = refs[len(MERGED) + 8 :]
    even = parity[0] == 0
    slots = [pair_slot(pairs, owner, bit) for bit in range(BITS)]

    def merges(k):
        for bit in range(BITS):
            copy = pltpu.make_async_copy(
                bulk[bit].at[pl.ds(k * EDGE, EDGE)],
                (v, f, c)[k].at[block_rows(jnp.maximum(slots[bit], 0))],
                sems.at[bit, k],
            )
            yield slots[bit], copy

    def start(k):
        for slot, copy in merges(k):

            @pl.when(slot >= 0)
            def _(copy=copy):
                copy.start()

    def settle(k, field=None, forth=None, back=None):
        for slot, copy in merges(k):

            @pl.when(slot >= 0)
            def _(slot=jnp.maximum(slot, 0), copy=copy):
                copy.wait()
                if field is not None:
                    turn_block(field, slot, forth, back)

    copies = list_copies(ie, io, held, list_sems)
    for copy in copies:
        copy.start()
    for k in (2, 1, 0):
        start(k)
    sheets = sheet_refs[:6], sheet_refs[6:]
    for side in range(2):
        for store, kind in zip(sheets[side], (V, V + 1, V + 2, C, C + 1, C + 2)):
            fill_sheet(store, sheet_of(even, ie, io, kind, side))
    (below, _, _, below_c, _, _), (above, _, _, above_c, _, _) = sheets
    place_faces(ya, mine, ghost, 0, 4)
    place_faces(ya, mine, ghost_c, 2, 4)
    for copy in copies:
        copy.wait()
    lists = read_lists(even, held, lists_out)
    pack_lines(sheets, lists, ys, 2, 3)
    settle(2, c, forth_c, back_c)
    settle(1)
    settle(0, v, forth_v, back_v)

    def one(j, carry):
        rows = block_rows(j)
        conduct = six_turned(c, forth_c, back_c, j, mine, ghost_c, below_c, above_c)
        iterate = six_turned(v, forth_v, back_v, j, mine, ghost, below, above)
        for (n, k, around_k), (_, centre, around) in zip(conduct, iterate):
            scaled, weight, inverse = weights(k, around_k)
            forced = weight * f[rows, column(n)]
            wf[rows, column(n)] = forced
            dg[rows, column(n)] = inverse
            total = forced + (1.0 - OMEGA) * centre
            for d in range(6):
                wk[d, rows, column(n)] = scaled[d]
                total = total + scaled[d] * around[d]
            store_swept(total, n, j, u, forth, back, faces)
        return carry

    lax.fori_loop(0, SLOTS, one, 0)
    end_turned(forth, back)
    pick_faces(faces, mine, ys, 0, 3)


SHEET = scratch(SLOTS + 1, *TILE)
GHOSTS = scratch(FACES + 1, *TILE)
GATHERED = [scratch(SLOTS, *TILE)] * 3


MERGED = [f32(*FIELD)] * 3 + [f32(*TURNED)] * 4


def first(merged, bulk, ends_in, ya, pairs, owner, mine, parity):
    outs = pl.pallas_call(
        first_kernel,
        in_specs=[SMEM] * 4 + [VMEM] * (3 + BITS + len(MERGED)),
        out_specs=[VMEM] * (len(MERGED) + 7) + [SMEM],
        out_shape=MERGED
        + [f32(6, *FIELD)]
        + [f32(*FIELD)] * 3
        + [f32(*TURNED)] * 2
        + [tiles(3 * SLOTS), jax.ShapeDtypeStruct((2, LISTS), jnp.int32)],
        input_output_aliases={7 + BITS + k: k for k in range(len(MERGED))},
        scratch_shapes=[GHOSTS] * 2
        + [scratch(FACES, *TILE), pltpu.SMEM((2,) + TILE, jnp.float32), pltpu.SemaphoreType.DMA((2,))]
        + [pltpu.SemaphoreType.DMA((BITS, 3))]
        + [SHEET] * 12,
        compiler_params=params(20),
        cost_estimate=cost(1 << 24, 12 << 20),
        name="first",
    )(pairs, owner, mine, parity, *ends_in, ya, *bulk, *merged)
    return outs[len(MERGED) :]


def second_kernel(
    mine, parity, lists_in,
    v, forth_in, back_in, wk, wf, ye, yo, ie, io, ya,
    u, forth, back, ys, kept, sheets, ends,
    ghost, faces, ends_out, minus, plus, touching, *sheet_refs,
):
    even = parity[0] == 0
    lists = [Lists(lists_in, side) for side in range(2)]
    place_faces(ya, mine, ghost, 0, 3)
    own_ends(v, ends)
    depths = DEPTHS[0]
    stores, edges = (sheet_refs[:6], sheet_refs[6:12]), (sheet_refs[12:18], sheet_refs[18:])
    place_lines(ya, lists, edges, 2, 3)
    for side in range(2):
        iterate = [sheet_of(even, ie, io, V + depth, side) for depth in range(depths + 1)]
        conduct = [sheet_of(even, ie, io, C + depth, side) for depth in range(depths + 1)]
        for depth in range(depths):
            fill_sheet(stores[side][depth], iterate[depth])
            fill_sheet(stores[side][3 + depth], conduct[depth])
        ends_out[...] = own_end(even, ye, yo, V, side)
        outer = beyond(ends_out, lists[side], side, touching)
        ends_out[...] = own_end(even, ye, yo, C, side)
        outer_c = beyond(ends_out, lists[side], side, touching)
        fresh = []
        for depth in range(depths):
            around_c = sheet_around(
                stores[side][3 + depth], conduct[depth + 1], outer_c, edges[side][3 + depth], lists[side], side,
                (minus, plus),
            )
            scaled, weight, _ = weights(conduct[depth], around_c)
            forced = weight * sheet_of(even, ie, io, F + depth, side)
            if depth < DEPTHS[1]:
                for d in range(6):
                    keep_layers(kept, kept_index(side, depth) + d, scaled[d])
                keep_layers(kept, kept_index(side, depth) + 6, forced)
            around = sheet_around(
                stores[side][depth], iterate[depth + 1], outer, edges[side][depth], lists[side], side, (minus, plus)
            )
            fresh.append(swept(iterate[depth], forced, scaled, around))
            outer, outer_c = iterate[depth], conduct[depth]
        for depth in range(depths):
            fill_sheet(stores[side][depth], fresh[depth])
            keep_layers(sheets, side * depths + depth, fresh[depth])
    pack_lines([stores[side][: DEPTHS[1]] for side in range(2)], lists, ys, 2, 3)
    below, above = stores[0][0], stores[1][0]
    sweep_blocks((v, forth_in, back_in), mine, ghost, below, above, wk, wf, u, forth, back, faces)
    pick_faces(faces, mine, ys, 0, 3)


def second(turned, wk, wf, sent, got, ya, mine, parity, lists):
    return pl.pallas_call(
        second_kernel,
        in_specs=[SMEM] * 3 + [VMEM] * 10,
        out_specs=[VMEM] * 7,
        out_shape=[f32(*FIELD), f32(*TURNED), f32(*TURNED), tiles(3 * SLOTS)]
        + [tiles(28 * SLOTS), tiles(2 * DEPTHS[0] * SLOTS), tiles(2 * SLOTS)],
        scratch_shapes=[GHOSTS, scratch(FACES, *TILE), scratch(SLOTS, *TILE)] + GATHERED + [SHEET] * 24,
        compiler_params=params(16),
        cost_estimate=cost(1 << 22, 9 << 20),
        name="second",
    )(mine, parity, lists, *turned, wk, wf, *sent, *got, ya)


def third_kernel(
    mine, lists_in,
    v, forth_in, back_in, wk, wf, kept, sheets_in, ends_in, ya,
    u, forth, back, ys, sheets, ends,
    ghost, faces, minus, plus, touching, *sheet_refs,
):
    lists = [Lists(lists_in, side) for side in range(2)]
    place_faces(ya, mine, ghost, 0, 3)
    own_ends(v, ends)
    depths = DEPTHS[1]
    stores, edges = (sheet_refs[:2], sheet_refs[2:4]), (sheet_refs[4:6], sheet_refs[6:])
    place_lines(ya, lists, edges, 2, 3)
    sweep_sheets(sheets_in, ends_in, kept, depths, stores, edges, lists, (minus, plus, touching))
    for side in range(2):
        for depth in range(depths):
            keep_layers(sheets, side * depths + depth, stores[side][depth][:SLOTS])
    pack_lines([stores[side][: DEPTHS[2]] for side in range(2)], lists, ys, 2, 3)
    below, above = stores[0][0], stores[1][0]
    sweep_blocks((v, forth_in, back_in), mine, ghost, below, above, wk, wf, u, forth, back, faces)
    pick_faces(faces, mine, ys, 0, 3)


def third(turned, wk, wf, kept, sheets, ends, ya, mine, lists):
    return pl.pallas_call(
        third_kernel,
        in_specs=[SMEM] * 2 + [VMEM] * 9,
        out_specs=[VMEM] * 6,
        out_shape=[f32(*FIELD), f32(*TURNED), f32(*TURNED), tiles(3 * SLOTS)]
        + [tiles(2 * DEPTHS[1] * SLOTS), tiles(2 * SLOTS)],
        scratch_shapes=[GHOSTS, scratch(FACES, *TILE)] + GATHERED + [SHEET] * 8,
        compiler_params=params(16),
        cost_estimate=cost(1 << 22, 9 << 20),
        name="third",
    )(mine, lists, *turned, wk, wf, kept, sheets, ends, ya)


def last_kernel(
    mine, lists_in,
    v, forth_in, back_in, wk, wf, dg, kept, sheets_in, ends_in, ya,
    out, coarse,
    ghost, below, above, edge_b, edge_a, minus, plus, touching, residual, sem,
):
    write = pltpu.make_async_copy(v, out, sem)
    write.start()
    lists = [Lists(lists_in, side) for side in range(2)]
    place_faces(ya, mine, ghost, 0, 3)
    edges = ((edge_b,), (edge_a,))
    place_lines(ya, lists, edges, 2, 3)
    sweep_sheets(
        sheets_in, ends_in, kept, DEPTHS[2], ((below,), (above,)), edges, lists, (minus, plus, touching)
    )

    def one(j, carry):
        rows = block_rows(j)
        for n, centre, around in six_turned(v, forth_in, back_in, j, mine, ghost, below, above):
            total = wf[rows, column(n)] - OMEGA * centre
            for d in range(6):
                total = total + wk[d, rows, column(n)] * around[d]
            residual[n, rows, :] = total * dg[rows, column(n)]
        return carry

    lax.fori_loop(0, SLOTS, one, 0)
    lane = lax.broadcasted_iota(jnp.int32, (LANES, LANES), 0)
    target = lax.broadcasted_iota(jnp.int32, (LANES, LANES), 1)
    place = (lane // (2 * EDGE)) * (EDGE // 2) + (lane % EDGE) // 2
    half = ROWS // 2
    for part in range(2):
        total = jnp.zeros((half, LANES), jnp.float32)
        for n in range(4):
            column_sum = (
                residual[part * 4 + n, pl.ds(0, half, stride=2), :]
                + residual[part * 4 + n, pl.ds(1, half, stride=2), :]
            )
            gather = jnp.where(place + EDGE * n == target, 0.125, 0.0)
            total = total + jnp.dot(
                column_sum, gather, precision=lax.Precision.HIGHEST, preferred_element_type=jnp.float32
            )
        coarse[:, part * LANES : (part + 1) * LANES] = total
    write.wait()


def last(turned, wk, wf, dg, kept, sheets, ends, ya, mine, lists):
    return pl.pallas_call(
        last_kernel,
        in_specs=[SMEM] * 2 + [VMEM] * 10,
        out_specs=[HBM, VMEM],
        out_shape=[f32(*FIELD), f32(ROWS // 2, PLANE // 4)],
        scratch_shapes=[GHOSTS]
        + [SHEET] * 4
        + GATHERED
        + [scratch(COLS, ROWS, LANES), pltpu.SemaphoreType.DMA],
        compiler_params=params(16),
        cost_estimate=cost(1 << 24, 10 << 20),
        name="last",
    )(mine, lists, *turned, wk, wf, dg, kept, sheets, ends, ya)


def pair_swap(values, stride):
    count = lax.axis_size("owner")
    return lax.ppermute(values, "owner", [(i, i ^ stride) for i in range(count)])


def odd_pair_swap(values):
    count = lax.axis_size("owner")
    return lax.ppermute(values, "owner", [(i, ((i - 1) ^ 1) + 1) for i in range(1, count - 1)])


def in_hbm(values):
    return pltpu.with_memory_space_constraint(values, pltpu.HBM)


def segment_swap(ys):
    return lax.all_to_all(ys, "sub", split_axis=0, concat_axis=0, tiled=True)


def body(guess, rhs, coef, occupied, neighbours, swap_slot, send_list, recv_list):
    my_owner = lax.axis_index("owner").astype(jnp.int32)
    owner = my_owner.reshape(1)
    parity = (my_owner % 2).reshape(1)
    fields = tuple(values.reshape(FIELD) for values in (guess, rhs, coef))
    fields = tuple(in_hbm(x) for x in fields)
    occupied, swap_slot = in_hbm(occupied), in_hbm(swap_slot)
    bulk = swap_pack(fields, occupied, swap_slot, owner, ORDER)
    bulk = [pair_swap(block, 1 << bit) for bit, block in zip(ORDER, bulk)]
    top, bottom, faces, mine, *merged = local(fields, occupied, neighbours, in_hbm(send_list), in_hbm(recv_list))
    ze, zo, ys = ends(top, bottom, faces, bulk, swap_slot, owner, mine, parity)
    sent, got, ya = (ze, zo), (pair_swap(ze, 1), odd_pair_swap(zo)), segment_swap(ys)
    wk, wf, dg, v, forth, back, ys, lists = first(merged, bulk, got, ya, swap_slot, owner, mine, parity)
    turned = v, forth, back
    *turned, ys, kept, sheets, ends_of = second(turned, wk, wf, sent, got, segment_swap(ys), mine, parity, lists)
    *turned, ys, sheets, ends_of = third(turned, wk, wf, kept, sheets, ends_of, segment_swap(ys), mine, lists)
    v, coarse = last(turned, wk, wf, dg, kept, sheets, ends_of, segment_swap(ys), mine, lists)
    return v.reshape(SLOTS, EDGE, PLANE), coarse.reshape(SLOTS, EDGE // 2, PLANE // 4)


def solution(mesh):
    wide, flat, single = P(("owner", "sub"), None, None), P(("owner", "sub"), None), P(("owner", "sub"))
    return jax.shard_map(
        body,
        mesh=mesh,
        in_specs=(wide, wide, wide, single, flat, flat, flat, flat),
        out_specs=(wide, wide),
        check_vma=False,
    )
```

```python
import jax
import jax.numpy as jnp
from jax import lax
from jax.experimental import pallas as pl
from jax.experimental.pallas import tpu as pltpu
from jax.sharding import PartitionSpec as P

OMEGA = 0.8
SLOTS = 8
EDGE = 32
PLANE = EDGE * EDGE
ROWS = SLOTS * EDGE
LANES = 128
COLS = PLANE // LANES
FIELD = (ROWS, PLANE)
TURNED = (ROWS + EDGE, PLANE)
FACES = 2 * SLOTS
TILE = (8, LANES)
BITS = 4
GROUP = 8
ORDER = (2, 0, 3, 1)
SOON, LATE = ORDER[:2], ORDER[2:]
V, C, F = 0, 4, 8
KINDS = 11
DEPTHS = (3, 2, 1)
SEND = 4 * SLOTS
RECV = SEND + FACES
LISTS = RECV + FACES
SMEM = pl.BlockSpec(memory_space=pltpu.SMEM)
VMEM = pl.BlockSpec(memory_space=pltpu.VMEM)
HBM = pl.BlockSpec(memory_space=pltpu.HBM)


def f32(*shape):
    return jax.ShapeDtypeStruct(shape, jnp.float32)


def tiles(count):
    return f32(count, *TILE)


def scratch(*shape):
    return pltpu.VMEM(shape, jnp.float32)


def params(mib):
    return pltpu.CompilerParams(vmem_limit_bytes=mib << 20)


def cost(flops, bytes_accessed):
    return pl.CostEstimate(flops=flops, bytes_accessed=bytes_accessed, transcendentals=0)


def column(c):
    return slice(c * LANES, (c + 1) * LANES)


def block_rows(j):
    return pl.ds(pl.multiple_of(j * EDGE, EDGE), EDGE)


def iotas(shape):
    rank = len(shape)
    sub = lax.broadcasted_iota(jnp.int32, shape, rank - 2)
    lane = lax.broadcasted_iota(jnp.int32, shape, rank - 1)
    return sub, lane


def slot_or(entry, none):
    return jnp.where(entry >= 0, jnp.maximum(entry, 0) % SLOTS, none)


def layer_tile(field, row, out, index):
    for c in range(COLS):
        out[index, c : c + 1, :] = field[row : row + 1, column(c)]


def face_of(cells, side, forth=None, back=None):
    group = lax.broadcasted_iota(jnp.int32, TILE, 1) // EDGE
    turned = {0: cells, EDGE: forth, LANES - EDGE: back}
    face = None
    for g in range(4):
        turn = (EDGE * g + EDGE * side) % LANES
        rows = slice(8 * g, 8 * g + 8)
        done = turned.get(turn)
        part = pltpu.roll(cells[rows], turn, 1) if done is None else done[rows]
        face = part if face is None else jnp.where(group == g, part, face)
    return face


def face_tile(field, first_row, side):
    return face_of(field[first_row : first_row + EDGE, column(COLS - 1 if side else 0)], side)


def unpack_face(face, side):
    parts = []
    for g in range(4):
        turn = (-EDGE * g - EDGE * side) % LANES
        parts.append(pltpu.roll(face, turn, 1) if turn else face)
    return jnp.concatenate(parts, axis=0)


def pick_faces(faces, mine, out, offset, stride):
    for entry in range(FACES):
        face = mine[SEND + entry]
        out[(entry // 2) * stride + entry % 2 + offset] = faces[jnp.maximum(face, 0)] * (face >= 0).astype(
            jnp.float32
        )


def place_faces(arrived, mine, ghost, offset, stride):
    ghost[...] = jnp.zeros(ghost.shape, jnp.float32)
    for entry in range(FACES):
        face = mine[RECV + entry]
        ghost[jnp.where(face >= 0, face, FACES)] = arrived[(entry // 2) * stride + entry % 2 + offset]


class Lists:
    def __init__(self, lists, side):
        self.lists, self.side = lists, side

    def at(self, i):
        return self.lists[self.side, i]

    def neighbour(self, slot, direction):
        return self.at(4 * slot + direction)

    def send(self, entry):
        return self.at(SEND + entry)

    def recv(self, entry):
        return self.at(RECV + entry)


def lists_tile(mine):
    sub, lane = iotas(TILE)
    tile = jnp.zeros(TILE, jnp.float32)
    for i in range(LISTS):
        tile = jnp.where(lane == i, mine[i].astype(jnp.float32), tile)
    return jnp.where(sub == 0, tile, 0.0)


def list_copies(ie, io, held, sems):
    return [
        pltpu.make_async_copy(source.at[KINDS * SLOTS], held.at[k], sems.at[k]) for k, source in enumerate((ie, io))
    ]


def read_lists(even, held, lists):
    for side in range(2):
        source = jnp.where(even, 1 - side, side)
        for i in range(LISTS):
            lists[side, i] = held[source, 0, i].astype(jnp.int32)
    return [Lists(lists, side) for side in range(2)]


def sheet_of(even, from_even, from_odd, kind, side):
    rows = slice(kind * SLOTS, (kind + 1) * SLOTS)
    pair = (from_even[rows], from_odd[rows])
    return jnp.where(even, *(pair if side else pair[::-1]))


def own_end(even, to_even, to_odd, kind, side):
    return sheet_of(even, to_even, to_odd, kind, side)


def fill_sheet(store, value):
    store[:SLOTS] = value
    store[SLOTS] = jnp.zeros(TILE, jnp.float32)


def pack_lines(sheets, lists, out, tile, stride):
    sub, lane = iotas(TILE)
    for peer in range(SLOTS):
        totals = []
        row = 0
        for side in range(2):
            for i in range(2):
                face = lists[side].send(2 * peer + i)
                slot = jnp.where(face >= 0, jnp.maximum(face, 0) // 2, SLOTS)
                high = jnp.maximum(face, 0) % 2 == 1
                for store in sheets[side]:
                    line = store[slot]
                    low_line = line[0:1, :]
                    high_line = pltpu.roll(line, EDGE, 1)[7:8, :]
                    if row % 8 == 0:
                        totals.append(jnp.zeros(TILE, jnp.float32))
                    totals[-1] = jnp.where(sub == row % 8, jnp.where(high, high_line, low_line), totals[-1])
                    row += 1
        total = totals[0]
        for group, part in enumerate(totals[1:], 1):
            total = jnp.where(lane // EDGE == group, pltpu.roll(part, EDGE * group, 1), total)
        out[peer * stride + tile] = total


def place_lines(arrived, lists, edges, tile, stride):
    for stores in edges:
        for store in stores:
            store[...] = jnp.zeros(store.shape, jnp.float32)
    sub, lane = iotas(TILE)
    first = (sub == 0) & (lane < EDGE)
    final = (sub == 7) & (lane >= LANES - EDGE)
    groups = (4 * len(edges[0]) + 7) // 8
    for peer in range(SLOTS):
        got = arrived[peer * stride + tile]
        turned = [got] + [pltpu.roll(got, LANES - EDGE * g, 1) for g in range(1, groups + 1)]
        row = 0
        for side in range(2):
            for i in range(2):
                ghost = lists[side].recv(2 * peer + i)
                slot = jnp.where(ghost >= 0, jnp.maximum(ghost, 0) // 2, SLOTS)
                high = jnp.maximum(ghost, 0) % 2 == 1
                for store in edges[side]:
                    group, at = row // 8, row % 8
                    low_part = jnp.where(first, turned[group][at : at + 1, :], 0.0)
                    high_part = jnp.where(final, turned[group + 1][at : at + 1, :], 0.0)
                    store[slot] = store[slot] + jnp.where(high, high_part, low_part)
                    row += 1


def beyond(ends, lists, side, gathered):
    for slot in range(SLOTS):
        entry = lists.neighbour(slot, 2 if side else 3)
        gathered[slot] = ends[slot_or(entry, 0)] * (entry >= 0).astype(jnp.float32)
    return gathered[...]


def sheet_around(store, inner, outer, edge, lists, side, gathered):
    shape = (SLOTS,) + TILE
    sub, lane = iotas(shape)
    x = lane % EDGE
    minus, plus = gathered
    for slot in range(SLOTS):
        minus[slot] = store[slot_or(lists.neighbour(slot, 0), SLOTS)]
        plus[slot] = store[slot_or(lists.neighbour(slot, 1), SLOTS)]
    value = store[:SLOTS]
    edges = edge[:SLOTS]
    forth = pltpu.roll(value, EDGE, 2)
    back = pltpu.roll(value, LANES - EDGE, 2)
    before = jnp.where(lane < EDGE, pltpu.roll(forth, 1, 1), forth)
    after = jnp.where(lane >= LANES - EDGE, pltpu.roll(back, 7, 1), back)
    return (
        jnp.where(x == 0, pltpu.roll(minus[...], LANES - EDGE + 1, 2), pltpu.roll(value, 1, 2)),
        jnp.where(x == EDGE - 1, pltpu.roll(plus[...], EDGE - 1, 2), pltpu.roll(value, LANES - 1, 2)),
        jnp.where((lane < EDGE) & (sub == 0), edges, before),
        jnp.where((lane >= LANES - EDGE) & (sub == 7), edges, after),
        outer if side else inner,
        inner if side else outer,
    )


def layers(ref, index):
    return ref[index * SLOTS : (index + 1) * SLOTS]


def keep_layers(ref, index, value):
    ref[index * SLOTS : (index + 1) * SLOTS] = value


def swept(value, forced, scaled, around):
    total = forced + (1.0 - OMEGA) * value
    for d in range(6):
        total = total + scaled[d] * around[d]
    return total


def kept_index(side, depth):
    return 7 * (2 * side + depth)


def sweep_sheets(sheets, ends, kept, depths, stores, edges, lists, gathered):
    minus, plus, touching = gathered
    for side in range(2):
        old = [layers(sheets, side * (depths + 1) + depth) for depth in range(depths + 1)]
        for depth in range(depths):
            fill_sheet(stores[side][depth], old[depth])
        outer = beyond(ends.at[pl.ds(side * SLOTS, SLOTS)], lists[side], side, touching)
        fresh = []
        for depth in range(depths):
            around = sheet_around(
                stores[side][depth], old[depth + 1], outer, edges[side][depth], lists[side], side, (minus, plus)
            )
            at = kept_index(side, depth)
            scaled = [layers(kept, at + d) for d in range(6)]
            fresh.append(swept(old[depth], layers(kept, at + 6), scaled, around))
            outer = old[depth]
        for depth in range(depths):
            fill_sheet(stores[side][depth], fresh[depth])


def own_ends(v, out):
    for j in range(SLOTS):
        layer_tile(v, j * EDGE, out, j)
        layer_tile(v, j * EDGE + EDGE - 1, out, SLOTS + j)


def weights(k, around):
    faces = [k + other for other in around]
    total = (faces[0] + faces[1]) + (faces[2] + faces[3]) + (faces[4] + faces[5])
    inverse = pl.reciprocal(total, approx=True)
    inverse = inverse * (2.0 - total * inverse)
    factor = jnp.where(k > 0.0, OMEGA * inverse, 0.0)
    return [factor * face for face in faces], 2.0 * factor, total * (0.5 / OMEGA)


def filled(other, own):
    return jnp.where(other > 0.0, other, own)


def six_turned(field, forth, back, j, mine, ghost, below, above, fill=False):
    _, lane = iotas((EDGE, LANES))
    x = lane % EDGE
    xm, xp, zm, zp = [slot_or(mine[4 * j + side], SLOTS) for side in range(4)]
    under_face, over_face = below[zm], above[zp]
    own, minus_rows, plus_rows = block_rows(j), block_rows(xm), block_rows(xp)
    for c in range(COLS):
        v = field[own, column(c)]
        before = forth[own, column(c - 1)] if c else unpack_face(ghost[2 * j], 0)
        after = back[own, column(c + 1)] if c < COLS - 1 else unpack_face(ghost[2 * j + 1], 1)
        under, over = under_face[c : c + 1, :], over_face[c : c + 1, :]
        around = [
            pltpu.roll(jnp.where(x == EDGE - 1, back[minus_rows, column(c)], v), 1, 1),
            pltpu.roll(jnp.where(x == 0, forth[plus_rows, column(c)], v), LANES - 1, 1),
            jnp.where(lane < EDGE, before, forth[own, column(c)]),
            jnp.where(lane >= LANES - EDGE, after, back[own, column(c)]),
        ]
        if fill:
            ends = (True, True, c == 0, c == COLS - 1)
            around = [filled(other, v) if end else other for other, end in zip(around, ends)]
            under, over = filled(under, v[:1]), filled(over, v[EDGE - 1 :])
        around.append(jnp.concatenate([under, v[: EDGE - 1]], axis=0))
        around.append(jnp.concatenate([v[1:], over], axis=0))
        yield c, v, around


def store_swept(total, n, j, u, forth, back, faces):
    rows = block_rows(j)
    ahead, behind = pltpu.roll(total, EDGE, 1), pltpu.roll(total, LANES - EDGE, 1)
    u[rows, column(n)] = total
    forth[rows, column(n)] = ahead
    back[rows, column(n)] = behind
    if n in (0, COLS - 1):
        side = n // (COLS - 1)
        faces[2 * j + side] = face_of(total, side, ahead, behind)


def turn_block(field, j, forth, back):
    rows = block_rows(j)
    for c in range(COLS):
        cells = field[rows, column(c)]
        forth[rows, column(c)] = pltpu.roll(cells, EDGE, 1)
        back[rows, column(c)] = pltpu.roll(cells, LANES - EDGE, 1)


def end_turned(forth, back):
    for turned in (forth, back):
        turned[ROWS:, :] = jnp.zeros((EDGE, PLANE), jnp.float32)


def sweep_blocks(turned, mine, ghost, below, above, wk, wf, u, forth, back, faces):
    def one(j, carry):
        rows = block_rows(j)
        ready = []
        for n, centre, around in six_turned(*turned, j, mine, ghost, below, above):
            total = wf[rows, column(n)] + (1.0 - OMEGA) * centre
            for d in range(6):
                total = total + wk[d, rows, column(n)] * around[d]
            ready.append((total, n))
            if len(ready) == GROUP:
                for total, n in ready:
                    store_swept(total, n, j, u, forth, back, faces)
                ready = []
        return carry

    lax.fori_loop(0, SLOTS, one, 0)
    end_turned(forth, back)


def pair_slot(pairs, owner, bit):
    return pairs[0, owner[0] ^ (1 << bit)]


def block_tiles(v, f, c, row, out):
    for end in range(2):
        for kind, field, count in ((V, v, 4), (C, c, 4), (F, f, 3)):
            for depth in range(count):
                layer_tile(field, row + (depth if end else EDGE - 1 - depth), out, end * KINDS + kind + depth)
    for k, field in enumerate((v, c)):
        for side in range(2):
            out[2 * KINDS + 2 * k + side] = face_tile(field, row, side)


def swap_pack_kernel(bits, pairs, owner, occupied, guess, rhs, coef, *refs):
    bulk, sems = refs[: len(bits)], refs[len(bits)]
    slots = [jnp.maximum(pair_slot(pairs, owner, bit), 0) for bit in bits]

    def copies(n):
        return [
            pltpu.make_async_copy(
                source.at[block_rows(slots[n])], bulk[n].at[pl.ds(k * EDGE, EDGE)], sems.at[n, k]
            )
            for k, source in enumerate((guess, rhs, coef))
        ]

    for n in range(len(bits)):
        for copy in copies(n):
            copy.start()
    for n in range(len(bits)):
        for copy in copies(n):
            copy.wait()

        @pl.when(occupied[slots[n]] == 0)
        def _(n=n):
            bulk[n][...] = jnp.zeros((3 * EDGE, PLANE), jnp.float32)


def swap_pack(fields, occupied, pairs, owner, bits):
    return pl.pallas_call(
        lambda *refs: swap_pack_kernel(bits, *refs),
        in_specs=[SMEM] * 3 + [HBM] * 3,
        out_specs=[VMEM] * len(bits),
        out_shape=[f32(3 * EDGE, PLANE)] * len(bits),
        scratch_shapes=[pltpu.SemaphoreType.DMA((len(bits), 3))],
        compiler_params=params(8),
        cost_estimate=cost(1 << 19, len(bits) * (768 << 10)),
        name="swap_pack",
    )(pairs, owner, occupied, *fields)


def local_kernel(
    occupied, neighbours, send_list, recv_list, guess, rhs, coef, top, bottom, faces, mine, v, f, c, forth_v, back_v, forth_c, back_c, sems
):
    copies = [
        pltpu.make_async_copy(source, target, sems.at[k])
        for k, (source, target) in enumerate(((guess, v), (coef, c), (rhs, f)))
    ]
    for copy in copies:
        copy.start()
    for slot in range(SLOTS):
        for side in range(4):
            mine[4 * slot + side] = neighbours[slot, side]
    for entry in range(FACES):
        mine[SEND + entry] = send_list[0, entry]
        mine[RECV + entry] = recv_list[0, entry]
    for k, (field, kinds) in enumerate(((v, range(V, C)), (c, range(C, F)), (f, range(F, KINDS)))):
        copies[k].wait()
        for j in range(SLOTS):

            @pl.when(occupied[j] == 0)
            def _(field=field, j=j):
                field[j * EDGE : (j + 1) * EDGE, :] = jnp.zeros((EDGE, PLANE), jnp.float32)

        for j in range(SLOTS):
            for depth, kind in enumerate(kinds):
                for end, out in enumerate((top, bottom)):
                    row = j * EDGE + (depth if end else EDGE - 1 - depth)
                    layer_tile(field, row, out, kind * SLOTS + j)
            if k < 2:
                for side in range(2):
                    faces[k * FACES + 2 * j + side] = face_tile(field, j * EDGE, side)
    for field, forth, back in ((v, forth_v, back_v), (c, forth_c, back_c)):

        def one(j, carry, field=field, forth=forth, back=back):
            turn_block(field, j, forth, back)
            return carry

        lax.fori_loop(0, SLOTS, one, 0)
        end_turned(forth, back)


def local(fields, occupied, neighbours, send_list, recv_list):
    return pl.pallas_call(
        local_kernel,
        in_specs=[SMEM] * 4 + [HBM] * 3,
        out_specs=[VMEM] * 3 + [SMEM] + [VMEM] * 7,
        out_shape=[tiles(KINDS * SLOTS)] * 2
        + [tiles(2 * FACES), jax.ShapeDtypeStruct((LISTS,), jnp.int32)]
        + [f32(*FIELD)] * 3
        + [f32(*TURNED)] * 4,
        scratch_shapes=[pltpu.SemaphoreType.DMA((3,))],
        compiler_params=params(8),
        cost_estimate=cost(1 << 20, 4 << 20),
        name="local",
    )(occupied, neighbours, send_list, recv_list, *fields)


def soon_kernel(pairs, owner, *refs):
    bulk = dict(zip(SOON, refs))
    top, bottom, faces, v, f, c, forth_v, back_v, forth_c, back_c, fresh, sems = refs[len(SOON) + 3 + len(MERGED) :]

    def merges(bit, slot):
        return [
            pltpu.make_async_copy(bulk[bit].at[pl.ds(k * EDGE, EDGE)], field.at[block_rows(slot)], sems.at[bit, k])
            for k, field in enumerate((v, f, c))
        ]

    for bit in SOON:
        slot = pair_slot(pairs, owner, bit)

        @pl.when(slot >= 0)
        def _(bit=bit, slot=jnp.maximum(slot, 0)):
            for copy in merges(bit, slot):
                copy.start()
            block_tiles(*(bulk[bit].at[pl.ds(k * EDGE, EDGE)] for k in range(3)), 0, fresh)
            for kind in range(KINDS):
                top[kind * SLOTS + slot] = fresh[kind]
                bottom[kind * SLOTS + slot] = fresh[KINDS + kind]
            for k in range(2):
                for side in range(2):
                    faces[k * FACES + 2 * slot + side] = fresh[2 * KINDS + 2 * k + side]
            for copy in merges(bit, slot):
                copy.wait()
            turn_block(v, slot, forth_v, back_v)
            turn_block(c, slot, forth_c, back_c)


def soon(tops, merged, bulk, pairs, owner):
    count = 3 + len(MERGED)
    outs = pl.pallas_call(
        soon_kernel,
        in_specs=[SMEM] * 2 + [VMEM] * (len(SOON) + count),
        out_specs=[VMEM] * count,
        out_shape=[tiles(KINDS * SLOTS)] * 2 + [tiles(2 * FACES)] + MERGED,
        input_output_aliases={2 + len(SOON) + k: k for k in range(count)},
        scratch_shapes=[scratch(2 * KINDS + 4, *TILE), pltpu.SemaphoreType.DMA((BITS, 3))],
        compiler_params=params(8),
        cost_estimate=cost(1 << 18, 2 << 20),
        name="soon",
    )(pairs, owner, *bulk, *tops, *merged)
    return outs[:3], outs[3:]


def ends_kernel(pairs, owner, mine, parity, top, bottom, faces, *refs):
    bulk = dict(zip(LATE, refs))
    ze, zo, ys, held, fresh = refs[len(LATE) :]
    even = parity[0] == 0
    ze[: KINDS * SLOTS] = jnp.where(even, top[...], bottom[...])
    zo[: KINDS * SLOTS] = jnp.where(even, bottom[...], top[...])
    ze[KINDS * SLOTS] = zo[KINDS * SLOTS] = lists_tile(mine)
    held[...] = faces[...]
    for bit in LATE:
        slot = pair_slot(pairs, owner, bit)

        @pl.when(slot >= 0)
        def _(bit=bit, slot=jnp.maximum(slot, 0)):
            block_tiles(*(bulk[bit].at[pl.ds(k * EDGE, EDGE)] for k in range(3)), 0, fresh)
            for kind in range(KINDS):
                high, low = fresh[kind], fresh[KINDS + kind]
                ze[kind * SLOTS + slot] = jnp.where(even, high, low)
                zo[kind * SLOTS + slot] = jnp.where(even, low, high)
            for k in range(2):
                for side in range(2):
                    held[k * FACES + 2 * slot + side] = fresh[2 * KINDS + 2 * k + side]

    for k in range(2):
        pick_faces(held.at[pl.ds(k * FACES, FACES)], mine, ys, 2 * k, 4)

def ends(top, bottom, faces, bulk, pairs, owner, mine, parity):
    return pl.pallas_call(
        ends_kernel,
        in_specs=[SMEM] * 4 + [VMEM] * (3 + len(LATE)),
        out_specs=[VMEM] * 3,
        out_shape=[tiles(KINDS * SLOTS + 1)] * 2 + [tiles(2 * FACES)],
        scratch_shapes=[scratch(2 * FACES, *TILE), scratch(2 * KINDS + 4, *TILE)],
        compiler_params=params(8),
        cost_estimate=cost(1 << 18, 1 << 20),
        name="ends",
    )(pairs, owner, mine, parity, top, bottom, faces, *bulk)


def first_kernel(pairs, owner, mine, parity, ie, io, ya, *refs):
    bulk, refs = dict(zip(LATE, refs)), refs[len(LATE) + len(MERGED) :]
    v, f, c, forth_v, back_v, forth_c, back_c = refs[: len(MERGED)]
    wk, wf, dg, u, forth, back, ys, lists_out = refs[len(MERGED) : len(MERGED) + 8]
    ghost, ghost_c, faces, held, list_sems, sems, *sheet_refs = refs[len(MERGED) + 8 :]
    even = parity[0] == 0
    slots = {bit: pair_slot(pairs, owner, bit) for bit in LATE}

    def merges(k):
        for bit in LATE:
            copy = pltpu.make_async_copy(
                bulk[bit].at[pl.ds(k * EDGE, EDGE)],
                (v, f, c)[k].at[block_rows(jnp.maximum(slots[bit], 0))],
                sems.at[bit, k],
            )
            yield slots[bit], copy

    def start(k):
        for slot, copy in merges(k):

            @pl.when(slot >= 0)
            def _(copy=copy):
                copy.start()

    def settle(k, field=None, forth=None, back=None):
        for slot, copy in merges(k):

            @pl.when(slot >= 0)
            def _(slot=jnp.maximum(slot, 0), copy=copy):
                copy.wait()
                if field is not None:
                    turn_block(field, slot, forth, back)

    copies = list_copies(ie, io, held, list_sems)
    for copy in copies:
        copy.start()
    for k in (2, 1, 0):
        start(k)
    sheets = sheet_refs[:6], sheet_refs[6:]
    for side in range(2):
        for store, kind in zip(sheets[side], (V, V + 1, V + 2, C, C + 1, C + 2)):
            fill_sheet(store, sheet_of(even, ie, io, kind, side))
    (below, _, _, below_c, _, _), (above, _, _, above_c, _, _) = sheets
    place_faces(ya, mine, ghost, 0, 4)
    place_faces(ya, mine, ghost_c, 2, 4)
    for copy in copies:
        copy.wait()
    lists = read_lists(even, held, lists_out)
    pack_lines(sheets, lists, ys, 2, 3)
    settle(2, c, forth_c, back_c)
    settle(1)
    settle(0, v, forth_v, back_v)

    def one(j, carry):
        rows = block_rows(j)
        conduct = six_turned(c, forth_c, back_c, j, mine, ghost_c, below_c, above_c, fill=True)
        iterate = six_turned(v, forth_v, back_v, j, mine, ghost, below, above)
        for (n, k, around_k), (_, centre, around) in zip(conduct, iterate):
            scaled, weight, inverse = weights(k, around_k)
            forced = weight * f[rows, column(n)]
            wf[rows, column(n)] = forced
            dg[rows, column(n)] = inverse
            total = forced + (1.0 - OMEGA) * centre
            for d in range(6):
                wk[d, rows, column(n)] = scaled[d]
                total = total + scaled[d] * around[d]
            store_swept(total, n, j, u, forth, back, faces)
        return carry

    lax.fori_loop(0, SLOTS, one, 0)
    end_turned(forth, back)
    pick_faces(faces, mine, ys, 0, 3)


SHEET = scratch(SLOTS + 1, *TILE)
GHOSTS = scratch(FACES + 1, *TILE)
GATHERED = [scratch(SLOTS, *TILE)] * 3


MERGED = [f32(*FIELD)] * 3 + [f32(*TURNED)] * 4


def first(merged, bulk, ends_in, ya, pairs, owner, mine, parity):
    outs = pl.pallas_call(
        first_kernel,
        in_specs=[SMEM] * 4 + [VMEM] * (3 + len(LATE) + len(MERGED)),
        out_specs=[VMEM] * (len(MERGED) + 7) + [SMEM],
        out_shape=MERGED
        + [f32(6, *FIELD)]
        + [f32(*FIELD)] * 3
        + [f32(*TURNED)] * 2
        + [tiles(3 * SLOTS), jax.ShapeDtypeStruct((2, LISTS), jnp.int32)],
        input_output_aliases={7 + len(LATE) + k: k for k in range(len(MERGED))},
        scratch_shapes=[GHOSTS] * 2
        + [scratch(FACES, *TILE), pltpu.SMEM((2,) + TILE, jnp.float32), pltpu.SemaphoreType.DMA((2,))]
        + [pltpu.SemaphoreType.DMA((BITS, 3))]
        + [SHEET] * 12,
        compiler_params=params(20),
        cost_estimate=cost(1 << 24, 12 << 20),
        name="first",
    )(pairs, owner, mine, parity, *ends_in, ya, *bulk, *merged)
    return outs[len(MERGED) :]


def second_kernel(
    mine, parity, lists_in,
    v, forth_in, back_in, wk, wf, ye, yo, ie, io, ya,
    u, forth, back, ys, kept, sheets, ends,
    ghost, faces, ends_out, minus, plus, touching, *sheet_refs,
):
    even = parity[0] == 0
    lists = [Lists(lists_in, side) for side in range(2)]
    place_faces(ya, mine, ghost, 0, 3)
    own_ends(v, ends)
    depths = DEPTHS[0]
    stores, edges = (sheet_refs[:6], sheet_refs[6:12]), (sheet_refs[12:18], sheet_refs[18:])
    place_lines(ya, lists, edges, 2, 3)
    for side in range(2):
        iterate = [sheet_of(even, ie, io, V + depth, side) for depth in range(depths + 1)]
        conduct = [sheet_of(even, ie, io, C + depth, side) for depth in range(depths + 1)]
        for depth in range(depths):
            fill_sheet(stores[side][depth], iterate[depth])
            fill_sheet(stores[side][3 + depth], conduct[depth])
        ends_out[...] = own_end(even, ye, yo, V, side)
        outer = beyond(ends_out, lists[side], side, touching)
        ends_out[...] = own_end(even, ye, yo, C, side)
        outer_c = beyond(ends_out, lists[side], side, touching)
        fresh = []
        for depth in range(depths):
            around_c = sheet_around(
                stores[side][3 + depth], conduct[depth + 1], outer_c, edges[side][3 + depth], lists[side], side,
                (minus, plus),
            )
            scaled, weight, _ = weights(conduct[depth], [filled(other, conduct[depth]) for other in around_c])
            forced = weight * sheet_of(even, ie, io, F + depth, side)
            if depth < DEPTHS[1]:
                for d in range(6):
                    keep_layers(kept, kept_index(side, depth) + d, scaled[d])
                keep_layers(kept, kept_index(side, depth) + 6, forced)
            around = sheet_around(
                stores[side][depth], iterate[depth + 1], outer, edges[side][depth], lists[side], side, (minus, plus)
            )
            fresh.append(swept(iterate[depth], forced, scaled, around))
            outer, outer_c = iterate[depth], conduct[depth]
        for depth in range(depths):
            fill_sheet(stores[side][depth], fresh[depth])
            keep_layers(sheets, side * depths + depth, fresh[depth])
    pack_lines([stores[side][: DEPTHS[1]] for side in range(2)], lists, ys, 2, 3)
    below, above = stores[0][0], stores[1][0]
    sweep_blocks((v, forth_in, back_in), mine, ghost, below, above, wk, wf, u, forth, back, faces)
    pick_faces(faces, mine, ys, 0, 3)


def second(turned, wk, wf, sent, got, ya, mine, parity, lists):
    return pl.pallas_call(
        second_kernel,
        in_specs=[SMEM] * 3 + [VMEM] * 10,
        out_specs=[VMEM] * 7,
        out_shape=[f32(*FIELD), f32(*TURNED), f32(*TURNED), tiles(3 * SLOTS)]
        + [tiles(28 * SLOTS), tiles(2 * DEPTHS[0] * SLOTS), tiles(2 * SLOTS)],
        scratch_shapes=[GHOSTS, scratch(FACES, *TILE), scratch(SLOTS, *TILE)] + GATHERED + [SHEET] * 24,
        compiler_params=params(16),
        cost_estimate=cost(1 << 22, 9 << 20),
        name="second",
    )(mine, parity, lists, *turned, wk, wf, *sent, *got, ya)


def third_kernel(
    mine, lists_in,
    v, forth_in, back_in, wk, wf, kept, sheets_in, ends_in, ya,
    u, forth, back, ys, sheets, ends,
    ghost, faces, minus, plus, touching, *sheet_refs,
):
    lists = [Lists(lists_in, side) for side in range(2)]
    place_faces(ya, mine, ghost, 0, 3)
    own_ends(v, ends)
    depths = DEPTHS[1]
    stores, edges = (sheet_refs[:2], sheet_refs[2:4]), (sheet_refs[4:6], sheet_refs[6:])
    place_lines(ya, lists, edges, 2, 3)
    sweep_sheets(sheets_in, ends_in, kept, depths, stores, edges, lists, (minus, plus, touching))
    for side in range(2):
        for depth in range(depths):
            keep_layers(sheets, side * depths + depth, stores[side][depth][:SLOTS])
    pack_lines([stores[side][: DEPTHS[2]] for side in range(2)], lists, ys, 2, 3)
    below, above = stores[0][0], stores[1][0]
    sweep_blocks((v, forth_in, back_in), mine, ghost, below, above, wk, wf, u, forth, back, faces)
    pick_faces(faces, mine, ys, 0, 3)


def third(turned, wk, wf, kept, sheets, ends, ya, mine, lists):
    return pl.pallas_call(
        third_kernel,
        in_specs=[SMEM] * 2 + [VMEM] * 9,
        out_specs=[VMEM] * 6,
        out_shape=[f32(*FIELD), f32(*TURNED), f32(*TURNED), tiles(3 * SLOTS)]
        + [tiles(2 * DEPTHS[1] * SLOTS), tiles(2 * SLOTS)],
        scratch_shapes=[GHOSTS, scratch(FACES, *TILE)] + GATHERED + [SHEET] * 8,
        compiler_params=params(16),
        cost_estimate=cost(1 << 22, 9 << 20),
        name="third",
    )(mine, lists, *turned, wk, wf, kept, sheets, ends, ya)


def last_kernel(
    mine, lists_in,
    v, forth_in, back_in, wk, wf, dg, kept, sheets_in, ends_in, ya,
    out, coarse,
    ghost, below, above, edge_b, edge_a, minus, plus, touching, residual, sem,
):
    write = pltpu.make_async_copy(v, out, sem)
    write.start()
    lists = [Lists(lists_in, side) for side in range(2)]
    place_faces(ya, mine, ghost, 0, 3)
    edges = ((edge_b,), (edge_a,))
    place_lines(ya, lists, edges, 2, 3)
    sweep_sheets(
        sheets_in, ends_in, kept, DEPTHS[2], ((below,), (above,)), edges, lists, (minus, plus, touching)
    )

    def one(j, carry):
        rows = block_rows(j)
        for n, centre, around in six_turned(v, forth_in, back_in, j, mine, ghost, below, above):
            total = wf[rows, column(n)] - OMEGA * centre
            for d in range(6):
                total = total + wk[d, rows, column(n)] * around[d]
            residual[n, rows, :] = total * dg[rows, column(n)]
        return carry

    lax.fori_loop(0, SLOTS, one, 0)
    lane = lax.broadcasted_iota(jnp.int32, (LANES, LANES), 0)
    target = lax.broadcasted_iota(jnp.int32, (LANES, LANES), 1)
    place = (lane // (2 * EDGE)) * (EDGE // 2) + (lane % EDGE) // 2
    half = ROWS // 2
    for part in range(2):
        total = jnp.zeros((half, LANES), jnp.float32)
        for n in range(4):
            column_sum = (
                residual[part * 4 + n, pl.ds(0, half, stride=2), :]
                + residual[part * 4 + n, pl.ds(1, half, stride=2), :]
            )
            gather = jnp.where(place + EDGE * n == target, 0.125, 0.0)
            total = total + jnp.dot(
                column_sum, gather, precision=lax.Precision.HIGHEST, preferred_element_type=jnp.float32
            )
        coarse[:, part * LANES : (part + 1) * LANES] = total
    write.wait()


def last(turned, wk, wf, dg, kept, sheets, ends, ya, mine, lists):
    return pl.pallas_call(
        last_kernel,
        in_specs=[SMEM] * 2 + [VMEM] * 10,
        out_specs=[HBM, VMEM],
        out_shape=[f32(*FIELD), f32(ROWS // 2, PLANE // 4)],
        scratch_shapes=[GHOSTS]
        + [SHEET] * 4
        + GATHERED
        + [scratch(COLS, ROWS, LANES), pltpu.SemaphoreType.DMA],
        compiler_params=params(16),
        cost_estimate=cost(1 << 24, 10 << 20),
        name="last",
    )(mine, lists, *turned, wk, wf, dg, kept, sheets, ends, ya)


def pair_swap(values, stride):
    count = lax.axis_size("owner")
    return lax.ppermute(values, "owner", [(i, i ^ stride) for i in range(count)])


def odd_pair_swap(values):
    count = lax.axis_size("owner")
    return lax.ppermute(values, "owner", [(i, ((i - 1) ^ 1) + 1) for i in range(1, count - 1)])


def in_hbm(values):
    return pltpu.with_memory_space_constraint(values, pltpu.HBM)


def segment_swap(ys):
    return lax.all_to_all(ys, "sub", split_axis=0, concat_axis=0, tiled=True)


def body(guess, rhs, coef, occupied, neighbours, swap_slot, send_list, recv_list):
    my_owner = lax.axis_index("owner").astype(jnp.int32)
    owner = my_owner.reshape(1)
    parity = (my_owner % 2).reshape(1)
    fields = tuple(values.reshape(FIELD) for values in (guess, rhs, coef))
    fields = tuple(in_hbm(x) for x in fields)
    occupied, swap_slot = in_hbm(occupied), in_hbm(swap_slot)
    bulk = swap_pack(fields, occupied, swap_slot, owner, ORDER)
    bulk = [pair_swap(block, 1 << bit) for bit, block in zip(ORDER, bulk)]
    top, bottom, faces, mine, *merged = local(fields, occupied, neighbours, in_hbm(send_list), in_hbm(recv_list))
    (top, bottom, faces), merged = soon((top, bottom, faces), merged, bulk[:2], swap_slot, owner)
    ze, zo, ys = ends(top, bottom, faces, bulk[2:], swap_slot, owner, mine, parity)
    sent, got, ya = (ze, zo), (pair_swap(ze, 1), odd_pair_swap(zo)), segment_swap(ys)
    wk, wf, dg, v, forth, back, ys, lists = first(merged, bulk[2:], got, ya, swap_slot, owner, mine, parity)
    turned = v, forth, back
    *turned, ys, kept, sheets, ends_of = second(turned, wk, wf, sent, got, segment_swap(ys), mine, parity, lists)
    *turned, ys, sheets, ends_of = third(turned, wk, wf, kept, sheets, ends_of, segment_swap(ys), mine, lists)
    v, coarse = last(turned, wk, wf, dg, kept, sheets, ends_of, segment_swap(ys), mine, lists)
    return v.reshape(SLOTS, EDGE, PLANE), coarse.reshape(SLOTS, EDGE // 2, PLANE // 4)


def solution(mesh):
    wide, flat, single = P(("owner", "sub"), None, None), P(("owner", "sub"), None), P(("owner", "sub"))
    return jax.shard_map(
        body,
        mesh=mesh,
        in_specs=(wide, wide, wide, single, flat, flat, flat, flat),
        out_specs=(wide, wide),
        check_vma=False,
    )
```

```python
import jax
import jax.numpy as jnp
from jax import lax
from jax.experimental import pallas as pl
from jax.experimental.pallas import tpu as pltpu
from jax.sharding import PartitionSpec as P

OMEGA = 0.8
SLOTS = 8
EDGE = 32
PLANE = EDGE * EDGE
ROWS = SLOTS * EDGE
LANES = 128
COLS = PLANE // LANES
FIELD = (ROWS, PLANE)
TURNED = (ROWS + EDGE, PLANE)
FACES = 2 * SLOTS
TILE = (8, LANES)
BITS = 4
GROUP = 8
ORDER = (2, 0, 3, 1)
SOON, LATE = ORDER[:2], ORDER[2:]
V, C, F = 0, 4, 8
KINDS = 11
DEPTHS = (3, 2, 1)
SEND = 4 * SLOTS
RECV = SEND + FACES
LISTS = RECV + FACES
SMEM = pl.BlockSpec(memory_space=pltpu.SMEM)
VMEM = pl.BlockSpec(memory_space=pltpu.VMEM)
HBM = pl.BlockSpec(memory_space=pltpu.HBM)


def f32(*shape):
    return jax.ShapeDtypeStruct(shape, jnp.float32)


def tiles(count):
    return f32(count, *TILE)


def scratch(*shape):
    return pltpu.VMEM(shape, jnp.float32)


def params(mib):
    return pltpu.CompilerParams(vmem_limit_bytes=mib << 20)


def cost(flops, bytes_accessed):
    return pl.CostEstimate(flops=flops, bytes_accessed=bytes_accessed, transcendentals=0)


def column(c):
    return slice(c * LANES, (c + 1) * LANES)


def block_rows(j):
    return pl.ds(pl.multiple_of(j * EDGE, EDGE), EDGE)


def iotas(shape):
    rank = len(shape)
    sub = lax.broadcasted_iota(jnp.int32, shape, rank - 2)
    lane = lax.broadcasted_iota(jnp.int32, shape, rank - 1)
    return sub, lane


def slot_or(entry, none):
    return jnp.where(entry >= 0, jnp.maximum(entry, 0) % SLOTS, none)


def layer_tile(field, row, out, index):
    for c in range(COLS):
        out[index, c : c + 1, :] = field[row : row + 1, column(c)]


def face_of(cells, side, forth=None, back=None):
    group = lax.broadcasted_iota(jnp.int32, TILE, 1) // EDGE
    turned = {0: cells, EDGE: forth, LANES - EDGE: back}
    face = None
    for g in range(4):
        turn = (EDGE * g + EDGE * side) % LANES
        rows = slice(8 * g, 8 * g + 8)
        done = turned.get(turn)
        part = pltpu.roll(cells[rows], turn, 1) if done is None else done[rows]
        face = part if face is None else jnp.where(group == g, part, face)
    return face


def face_tile(field, first_row, side):
    return face_of(field[first_row : first_row + EDGE, column(COLS - 1 if side else 0)], side)


def unpack_face(face, side):
    parts = []
    for g in range(4):
        turn = (-EDGE * g - EDGE * side) % LANES
        parts.append(pltpu.roll(face, turn, 1) if turn else face)
    return jnp.concatenate(parts, axis=0)


def pick_faces(faces, mine, out, offset, stride):
    for entry in range(FACES):
        face = mine[SEND + entry]
        out[(entry // 2) * stride + entry % 2 + offset] = faces[jnp.maximum(face, 0)] * (face >= 0).astype(
            jnp.float32
        )


def place_faces(arrived, mine, ghost, offset, stride):
    ghost[...] = jnp.zeros(ghost.shape, jnp.float32)
    for entry in range(FACES):
        face = mine[RECV + entry]
        ghost[jnp.where(face >= 0, face, FACES)] = arrived[(entry // 2) * stride + entry % 2 + offset]


class Lists:
    def __init__(self, lists, side):
        self.lists, self.side = lists, side

    def at(self, i):
        return self.lists[self.side, i]

    def neighbour(self, slot, direction):
        return self.at(4 * slot + direction)

    def send(self, entry):
        return self.at(SEND + entry)

    def recv(self, entry):
        return self.at(RECV + entry)


def lists_tile(mine):
    sub, lane = iotas(TILE)
    tile = jnp.zeros(TILE, jnp.float32)
    for i in range(LISTS):
        tile = jnp.where(lane == i, mine[i].astype(jnp.float32), tile)
    return jnp.where(sub == 0, tile, 0.0)


def list_copies(ie, io, held, sems):
    return [
        pltpu.make_async_copy(source.at[KINDS * SLOTS], held.at[k], sems.at[k]) for k, source in enumerate((ie, io))
    ]


def read_lists(even, held, lists):
    for side in range(2):
        source = jnp.where(even, 1 - side, side)
        for i in range(LISTS):
            lists[side, i] = held[source, 0, i].astype(jnp.int32)
    return [Lists(lists, side) for side in range(2)]


def sheet_of(even, from_even, from_odd, kind, side):
    rows = slice(kind * SLOTS, (kind + 1) * SLOTS)
    pair = (from_even[rows], from_odd[rows])
    return jnp.where(even, *(pair if side else pair[::-1]))


def own_end(even, to_even, to_odd, kind, side):
    return sheet_of(even, to_even, to_odd, kind, side)


def fill_sheet(store, value):
    store[:SLOTS] = value
    store[SLOTS] = jnp.zeros(TILE, jnp.float32)


def pack_lines(sheets, lists, out, tile, stride):
    sub, lane = iotas(TILE)
    for peer in range(SLOTS):
        totals = []
        row = 0
        for side in range(2):
            for i in range(2):
                face = lists[side].send(2 * peer + i)
                slot = jnp.where(face >= 0, jnp.maximum(face, 0) // 2, SLOTS)
                high = jnp.maximum(face, 0) % 2 == 1
                for store in sheets[side]:
                    line = store[slot]
                    low_line = line[0:1, :]
                    high_line = pltpu.roll(line, EDGE, 1)[7:8, :]
                    if row % 8 == 0:
                        totals.append(jnp.zeros(TILE, jnp.float32))
                    totals[-1] = jnp.where(sub == row % 8, jnp.where(high, high_line, low_line), totals[-1])
                    row += 1
        total = totals[0]
        for group, part in enumerate(totals[1:], 1):
            total = jnp.where(lane // EDGE == group, pltpu.roll(part, EDGE * group, 1), total)
        out[peer * stride + tile] = total


def place_lines(arrived, lists, edges, tile, stride):
    for stores in edges:
        for store in stores:
            store[...] = jnp.zeros(store.shape, jnp.float32)
    sub, lane = iotas(TILE)
    first = (sub == 0) & (lane < EDGE)
    final = (sub == 7) & (lane >= LANES - EDGE)
    groups = (4 * len(edges[0]) + 7) // 8
    for peer in range(SLOTS):
        got = arrived[peer * stride + tile]
        turned = [got] + [pltpu.roll(got, LANES - EDGE * g, 1) for g in range(1, groups + 1)]
        row = 0
        for side in range(2):
            for i in range(2):
                ghost = lists[side].recv(2 * peer + i)
                slot = jnp.where(ghost >= 0, jnp.maximum(ghost, 0) // 2, SLOTS)
                high = jnp.maximum(ghost, 0) % 2 == 1
                for store in edges[side]:
                    group, at = row // 8, row % 8
                    low_part = jnp.where(first, turned[group][at : at + 1, :], 0.0)
                    high_part = jnp.where(final, turned[group + 1][at : at + 1, :], 0.0)
                    store[slot] = store[slot] + jnp.where(high, high_part, low_part)
                    row += 1


def beyond(ends, lists, side, gathered):
    for slot in range(SLOTS):
        entry = lists.neighbour(slot, 2 if side else 3)
        gathered[slot] = ends[slot_or(entry, 0)] * (entry >= 0).astype(jnp.float32)
    return gathered[...]


def sheet_around(store, inner, outer, edge, lists, side, gathered):
    shape = (SLOTS,) + TILE
    sub, lane = iotas(shape)
    x = lane % EDGE
    minus, plus = gathered
    for slot in range(SLOTS):
        minus[slot] = store[slot_or(lists.neighbour(slot, 0), SLOTS)]
        plus[slot] = store[slot_or(lists.neighbour(slot, 1), SLOTS)]
    value = store[:SLOTS]
    edges = edge[:SLOTS]
    forth = pltpu.roll(value, EDGE, 2)
    back = pltpu.roll(value, LANES - EDGE, 2)
    before = jnp.where(lane < EDGE, pltpu.roll(forth, 1, 1), forth)
    after = jnp.where(lane >= LANES - EDGE, pltpu.roll(back, 7, 1), back)
    return (
        jnp.where(x == 0, pltpu.roll(minus[...], LANES - EDGE + 1, 2), pltpu.roll(value, 1, 2)),
        jnp.where(x == EDGE - 1, pltpu.roll(plus[...], EDGE - 1, 2), pltpu.roll(value, LANES - 1, 2)),
        jnp.where((lane < EDGE) & (sub == 0), edges, before),
        jnp.where((lane >= LANES - EDGE) & (sub == 7), edges, after),
        outer if side else inner,
        inner if side else outer,
    )


def layers(ref, index):
    return ref[index * SLOTS : (index + 1) * SLOTS]


def keep_layers(ref, index, value):
    ref[index * SLOTS : (index + 1) * SLOTS] = value


def swept(value, forced, scaled, around):
    total = forced + (1.0 - OMEGA) * value
    for d in range(6):
        total = total + scaled[d] * around[d]
    return total


def kept_index(side, depth):
    return 7 * (2 * side + depth)


def sweep_sheets(sheets, ends, kept, depths, stores, edges, lists, gathered):
    minus, plus, touching = gathered
    for side in range(2):
        old = [layers(sheets, side * (depths + 1) + depth) for depth in range(depths + 1)]
        for depth in range(depths):
            fill_sheet(stores[side][depth], old[depth])
        outer = beyond(ends.at[pl.ds(side * SLOTS, SLOTS)], lists[side], side, touching)
        fresh = []
        for depth in range(depths):
            around = sheet_around(
                stores[side][depth], old[depth + 1], outer, edges[side][depth], lists[side], side, (minus, plus)
            )
            at = kept_index(side, depth)
            scaled = [layers(kept, at + d) for d in range(6)]
            fresh.append(swept(old[depth], layers(kept, at + 6), scaled, around))
            outer = old[depth]
        for depth in range(depths):
            fill_sheet(stores[side][depth], fresh[depth])


def own_ends(v, out):
    for j in range(SLOTS):
        layer_tile(v, j * EDGE, out, j)
        layer_tile(v, j * EDGE + EDGE - 1, out, SLOTS + j)


def weights(k, around):
    faces = [k + other for other in around]
    total = (faces[0] + faces[1]) + (faces[2] + faces[3]) + (faces[4] + faces[5])
    inverse = pl.reciprocal(total, approx=True)
    inverse = inverse * (2.0 - total * inverse)
    factor = jnp.where(k > 0.0, OMEGA * inverse, 0.0)
    return [factor * face for face in faces], 2.0 * factor, total * (0.5 / OMEGA)


def filled(other, own):
    return jnp.where(other > 0.0, other, own)


def six_turned(field, forth, back, j, mine, ghost, below, above, fill=False):
    _, lane = iotas((EDGE, LANES))
    x = lane % EDGE
    xm, xp, zm, zp = [slot_or(mine[4 * j + side], SLOTS) for side in range(4)]
    under_face, over_face = below[zm], above[zp]
    own, minus_rows, plus_rows = block_rows(j), block_rows(xm), block_rows(xp)
    for c in range(COLS):
        v = field[own, column(c)]
        before = forth[own, column(c - 1)] if c else unpack_face(ghost[2 * j], 0)
        after = back[own, column(c + 1)] if c < COLS - 1 else unpack_face(ghost[2 * j + 1], 1)
        under, over = under_face[c : c + 1, :], over_face[c : c + 1, :]
        around = [
            pltpu.roll(jnp.where(x == EDGE - 1, back[minus_rows, column(c)], v), 1, 1),
            pltpu.roll(jnp.where(x == 0, forth[plus_rows, column(c)], v), LANES - 1, 1),
            jnp.where(lane < EDGE, before, forth[own, column(c)]),
            jnp.where(lane >= LANES - EDGE, after, back[own, column(c)]),
        ]
        if fill:
            ends = (True, True, c == 0, c == COLS - 1)
            around = [filled(other, v) if end else other for other, end in zip(around, ends)]
            under, over = filled(under, v[:1]), filled(over, v[EDGE - 1 :])
        around.append(jnp.concatenate([under, v[: EDGE - 1]], axis=0))
        around.append(jnp.concatenate([v[1:], over], axis=0))
        yield c, v, around


def store_swept(total, n, j, u, forth, back, faces):
    rows = block_rows(j)
    ahead, behind = pltpu.roll(total, EDGE, 1), pltpu.roll(total, LANES - EDGE, 1)
    u[rows, column(n)] = total
    forth[rows, column(n)] = ahead
    back[rows, column(n)] = behind
    if n in (0, COLS - 1):
        side = n // (COLS - 1)
        faces[2 * j + side] = face_of(total, side, ahead, behind)


def turn_block(field, j, forth, back):
    rows = block_rows(j)
    for c in range(COLS):
        cells = field[rows, column(c)]
        forth[rows, column(c)] = pltpu.roll(cells, EDGE, 1)
        back[rows, column(c)] = pltpu.roll(cells, LANES - EDGE, 1)


def end_turned(forth, back):
    for turned in (forth, back):
        turned[ROWS:, :] = jnp.zeros((EDGE, PLANE), jnp.float32)


def sweep_blocks(turned, mine, ghost, below, above, wk, wf, u, forth, back, faces):
    def one(j, carry):
        rows = block_rows(j)
        ready = []
        for n, centre, around in six_turned(*turned, j, mine, ghost, below, above):
            total = wf[rows, column(n)] + (1.0 - OMEGA) * centre
            for d in range(6):
                total = total + wk[d, rows, column(n)] * around[d]
            ready.append((total, n))
            if len(ready) == GROUP:
                for total, n in ready:
                    store_swept(total, n, j, u, forth, back, faces)
                ready = []
        return carry

    lax.fori_loop(0, SLOTS, one, 0)
    end_turned(forth, back)


def pair_slot(pairs, owner, bit):
    return pairs[0, owner[0] ^ (1 << bit)]


def block_tiles(v, f, c, row, out):
    for end in range(2):
        for kind, field, count in ((V, v, 4), (C, c, 4), (F, f, 3)):
            for depth in range(count):
                layer_tile(field, row + (depth if end else EDGE - 1 - depth), out, end * KINDS + kind + depth)
    for k, field in enumerate((v, c)):
        for side in range(2):
            out[2 * KINDS + 2 * k + side] = face_tile(field, row, side)


def swap_pack_kernel(bits, pairs, owner, occupied, guess, rhs, coef, *refs):
    bulk, sems = refs[: len(bits)], refs[len(bits)]
    slots = [jnp.maximum(pair_slot(pairs, owner, bit), 0) for bit in bits]

    def copies(n):
        return [
            pltpu.make_async_copy(
                source.at[block_rows(slots[n])], bulk[n].at[pl.ds(k * EDGE, EDGE)], sems.at[n, k]
            )
            for k, source in enumerate((guess, rhs, coef))
        ]

    for n in range(len(bits)):
        for copy in copies(n):
            copy.start()
    for n in range(len(bits)):
        for copy in copies(n):
            copy.wait()

        @pl.when(occupied[slots[n]] == 0)
        def _(n=n):
            bulk[n][...] = jnp.zeros((3 * EDGE, PLANE), jnp.float32)


def swap_pack(fields, occupied, pairs, owner, bits):
    return pl.pallas_call(
        lambda *refs: swap_pack_kernel(bits, *refs),
        in_specs=[SMEM] * 3 + [HBM] * 3,
        out_specs=[VMEM] * len(bits),
        out_shape=[f32(3 * EDGE, PLANE)] * len(bits),
        scratch_shapes=[pltpu.SemaphoreType.DMA((len(bits), 3))],
        compiler_params=params(8),
        cost_estimate=cost(1 << 19, len(bits) * (768 << 10)),
        name="swap_pack",
    )(pairs, owner, occupied, *fields)


def local_kernel(
    occupied, neighbours, send_list, recv_list, guess, rhs, coef, top, bottom, faces, mine, v, f, c, forth_v, back_v, forth_c, back_c, sems
):
    copies = [
        pltpu.make_async_copy(source, target, sems.at[k])
        for k, (source, target) in enumerate(((guess, v), (coef, c), (rhs, f)))
    ]
    for copy in copies:
        copy.start()
    for slot in range(SLOTS):
        for side in range(4):
            mine[4 * slot + side] = neighbours[slot, side]
    for entry in range(FACES):
        mine[SEND + entry] = send_list[0, entry]
        mine[RECV + entry] = recv_list[0, entry]
    for k, (field, kinds) in enumerate(((v, range(V, C)), (c, range(C, F)), (f, range(F, KINDS)))):
        copies[k].wait()
        for j in range(SLOTS):

            @pl.when(occupied[j] == 0)
            def _(field=field, j=j):
                field[j * EDGE : (j + 1) * EDGE, :] = jnp.zeros((EDGE, PLANE), jnp.float32)

        for j in range(SLOTS):
            for depth, kind in enumerate(kinds):
                for end, out in enumerate((top, bottom)):
                    row = j * EDGE + (depth if end else EDGE - 1 - depth)
                    layer_tile(field, row, out, kind * SLOTS + j)
            if k < 2:
                for side in range(2):
                    faces[k * FACES + 2 * j + side] = face_tile(field, j * EDGE, side)
    for field, forth, back in ((v, forth_v, back_v), (c, forth_c, back_c)):

        def one(j, carry, field=field, forth=forth, back=back):
            turn_block(field, j, forth, back)
            return carry

        lax.fori_loop(0, SLOTS, one, 0)
        end_turned(forth, back)


def local(fields, occupied, neighbours, send_list, recv_list):
    return pl.pallas_call(
        local_kernel,
        in_specs=[SMEM] * 4 + [HBM] * 3,
        out_specs=[VMEM] * 3 + [SMEM] + [VMEM] * 7,
        out_shape=[tiles(KINDS * SLOTS)] * 2
        + [tiles(2 * FACES), jax.ShapeDtypeStruct((LISTS,), jnp.int32)]
        + [f32(*FIELD)] * 3
        + [f32(*TURNED)] * 4,
        scratch_shapes=[pltpu.SemaphoreType.DMA((3,))],
        compiler_params=params(8),
        cost_estimate=cost(1 << 20, 4 << 20),
        name="local",
    )(occupied, neighbours, send_list, recv_list, *fields)


def soon_kernel(pairs, owner, *refs):
    bulk = dict(zip(SOON, refs))
    top, bottom, faces, v, f, c, forth_v, back_v, forth_c, back_c, fresh, sems = refs[len(SOON) + 3 + len(MERGED) :]

    def merges(bit, slot):
        return [
            pltpu.make_async_copy(bulk[bit].at[pl.ds(k * EDGE, EDGE)], field.at[block_rows(slot)], sems.at[bit, k])
            for k, field in enumerate((v, f, c))
        ]

    for bit in SOON:
        slot = pair_slot(pairs, owner, bit)

        @pl.when(slot >= 0)
        def _(bit=bit, slot=jnp.maximum(slot, 0)):
            for copy in merges(bit, slot):
                copy.start()
            block_tiles(*(bulk[bit].at[pl.ds(k * EDGE, EDGE)] for k in range(3)), 0, fresh)
            for kind in range(KINDS):
                top[kind * SLOTS + slot] = fresh[kind]
                bottom[kind * SLOTS + slot] = fresh[KINDS + kind]
            for k in range(2):
                for side in range(2):
                    faces[k * FACES + 2 * slot + side] = fresh[2 * KINDS + 2 * k + side]
            for copy in merges(bit, slot):
                copy.wait()
            turn_block(v, slot, forth_v, back_v)
            turn_block(c, slot, forth_c, back_c)


def soon(tops, merged, bulk, pairs, owner):
    count = 3 + len(MERGED)
    outs = pl.pallas_call(
        soon_kernel,
        in_specs=[SMEM] * 2 + [VMEM] * (len(SOON) + count),
        out_specs=[VMEM] * count,
        out_shape=[tiles(KINDS * SLOTS)] * 2 + [tiles(2 * FACES)] + MERGED,
        input_output_aliases={2 + len(SOON) + k: k for k in range(count)},
        scratch_shapes=[scratch(2 * KINDS + 4, *TILE), pltpu.SemaphoreType.DMA((BITS, 3))],
        compiler_params=params(8),
        cost_estimate=cost(1 << 18, 2 << 20),
        name="soon",
    )(pairs, owner, *bulk, *tops, *merged)
    return outs[:3], outs[3:]


def ends_kernel(pairs, owner, mine, parity, top, bottom, faces, *refs):
    bulk = dict(zip(LATE, refs))
    ze, zo, ys, held, fresh = refs[len(LATE) :]
    even = parity[0] == 0
    ze[: KINDS * SLOTS] = jnp.where(even, top[...], bottom[...])
    zo[: KINDS * SLOTS] = jnp.where(even, bottom[...], top[...])
    ze[KINDS * SLOTS] = zo[KINDS * SLOTS] = lists_tile(mine)
    held[...] = faces[...]
    for bit in LATE:
        slot = pair_slot(pairs, owner, bit)

        @pl.when(slot >= 0)
        def _(bit=bit, slot=jnp.maximum(slot, 0)):
            block_tiles(*(bulk[bit].at[pl.ds(k * EDGE, EDGE)] for k in range(3)), 0, fresh)
            for kind in range(KINDS):
                high, low = fresh[kind], fresh[KINDS + kind]
                ze[kind * SLOTS + slot] = jnp.where(even, high, low)
                zo[kind * SLOTS + slot] = jnp.where(even, low, high)
            for k in range(2):
                for side in range(2):
                    held[k * FACES + 2 * slot + side] = fresh[2 * KINDS + 2 * k + side]

    for k in range(2):
        pick_faces(held.at[pl.ds(k * FACES, FACES)], mine, ys, 2 * k, 4)

def ends(top, bottom, faces, bulk, pairs, owner, mine, parity):
    return pl.pallas_call(
        ends_kernel,
        in_specs=[SMEM] * 4 + [VMEM] * (3 + len(LATE)),
        out_specs=[VMEM] * 3,
        out_shape=[tiles(KINDS * SLOTS + 1)] * 2 + [tiles(2 * FACES)],
        scratch_shapes=[scratch(2 * FACES, *TILE), scratch(2 * KINDS + 4, *TILE)],
        compiler_params=params(8),
        cost_estimate=cost(1 << 18, 1 << 20),
        name="ends",
    )(pairs, owner, mine, parity, top, bottom, faces, *bulk)


def first_kernel(pairs, owner, mine, parity, ie, io, ya, *refs):
    bulk, refs = dict(zip(LATE, refs)), refs[len(LATE) + len(MERGED) :]
    v, f, c, forth_v, back_v, forth_c, back_c = refs[: len(MERGED)]
    wk, wf, dg, u, forth, back, ys, lists_out = refs[len(MERGED) : len(MERGED) + 8]
    ghost, ghost_c, faces, held, list_sems, sems, *sheet_refs = refs[len(MERGED) + 8 :]
    even = parity[0] == 0
    slots = {bit: pair_slot(pairs, owner, bit) for bit in LATE}

    def merges(k):
        for bit in LATE:
            copy = pltpu.make_async_copy(
                bulk[bit].at[pl.ds(k * EDGE, EDGE)],
                (v, f, c)[k].at[block_rows(jnp.maximum(slots[bit], 0))],
                sems.at[bit, k],
            )
            yield slots[bit], copy

    def start(k):
        for slot, copy in merges(k):

            @pl.when(slot >= 0)
            def _(copy=copy):
                copy.start()

    def settle(k, field=None, forth=None, back=None):
        for slot, copy in merges(k):

            @pl.when(slot >= 0)
            def _(slot=jnp.maximum(slot, 0), copy=copy):
                copy.wait()
                if field is not None:
                    turn_block(field, slot, forth, back)

    copies = list_copies(ie, io, held, list_sems)
    for copy in copies:
        copy.start()
    for k in (2, 1, 0):
        start(k)
    sheets = sheet_refs[:6], sheet_refs[6:]
    for side in range(2):
        for store, kind in zip(sheets[side], (V, V + 1, V + 2, C, C + 1, C + 2)):
            fill_sheet(store, sheet_of(even, ie, io, kind, side))
    (below, _, _, below_c, _, _), (above, _, _, above_c, _, _) = sheets
    place_faces(ya, mine, ghost, 0, 4)
    place_faces(ya, mine, ghost_c, 2, 4)
    for copy in copies:
        copy.wait()
    lists = read_lists(even, held, lists_out)
    pack_lines(sheets, lists, ys, 2, 3)
    settle(2, c, forth_c, back_c)
    settle(1)
    settle(0, v, forth_v, back_v)

    def one(j, carry):
        rows = block_rows(j)
        conduct = six_turned(c, forth_c, back_c, j, mine, ghost_c, below_c, above_c, fill=True)
        iterate = six_turned(v, forth_v, back_v, j, mine, ghost, below, above)
        ready = []
        for (n, k, around_k), (_, centre, around) in zip(conduct, iterate):
            scaled, weight, inverse = weights(k, around_k)
            forced = weight * f[rows, column(n)]
            wf[rows, column(n)] = forced
            dg[rows, column(n)] = inverse
            total = forced + (1.0 - OMEGA) * centre
            for d in range(6):
                wk[d, rows, column(n)] = scaled[d]
                total = total + scaled[d] * around[d]
            ready.append((total, n))
        for total, n in ready:
            store_swept(total, n, j, u, forth, back, faces)
        return carry

    lax.fori_loop(0, SLOTS, one, 0)
    end_turned(forth, back)
    pick_faces(faces, mine, ys, 0, 3)


SHEET = scratch(SLOTS + 1, *TILE)
GHOSTS = scratch(FACES + 1, *TILE)
GATHERED = [scratch(SLOTS, *TILE)] * 3


MERGED = [f32(*FIELD)] * 3 + [f32(*TURNED)] * 4


def first(merged, bulk, ends_in, ya, pairs, owner, mine, parity):
    outs = pl.pallas_call(
        first_kernel,
        in_specs=[SMEM] * 4 + [VMEM] * (3 + len(LATE) + len(MERGED)),
        out_specs=[VMEM] * (len(MERGED) + 7) + [SMEM],
        out_shape=MERGED
        + [f32(6, *FIELD)]
        + [f32(*FIELD)] * 3
        + [f32(*TURNED)] * 2
        + [tiles(3 * SLOTS), jax.ShapeDtypeStruct((2, LISTS), jnp.int32)],
        input_output_aliases={7 + len(LATE) + k: k for k in range(len(MERGED))},
        scratch_shapes=[GHOSTS] * 2
        + [scratch(FACES, *TILE), pltpu.SMEM((2,) + TILE, jnp.float32), pltpu.SemaphoreType.DMA((2,))]
        + [pltpu.SemaphoreType.DMA((BITS, 3))]
        + [SHEET] * 12,
        compiler_params=params(20),
        cost_estimate=cost(1 << 24, 12 << 20),
        name="first",
    )(pairs, owner, mine, parity, *ends_in, ya, *bulk, *merged)
    return outs[len(MERGED) :]


def second_kernel(
    mine, parity, lists_in,
    v, forth_in, back_in, wk, wf, ye, yo, ie, io, ya,
    u, forth, back, ys, kept, sheets, ends,
    ghost, faces, ends_out, minus, plus, touching, *sheet_refs,
):
    even = parity[0] == 0
    lists = [Lists(lists_in, side) for side in range(2)]
    place_faces(ya, mine, ghost, 0, 3)
    own_ends(v, ends)
    depths = DEPTHS[0]
    stores, edges = (sheet_refs[:6], sheet_refs[6:12]), (sheet_refs[12:18], sheet_refs[18:])
    place_lines(ya, lists, edges, 2, 3)
    for side in range(2):
        iterate = [sheet_of(even, ie, io, V + depth, side) for depth in range(depths + 1)]
        conduct = [sheet_of(even, ie, io, C + depth, side) for depth in range(depths + 1)]
        for depth in range(depths):
            fill_sheet(stores[side][depth], iterate[depth])
            fill_sheet(stores[side][3 + depth], conduct[depth])
        ends_out[...] = own_end(even, ye, yo, V, side)
        outer = beyond(ends_out, lists[side], side, touching)
        ends_out[...] = own_end(even, ye, yo, C, side)
        outer_c = beyond(ends_out, lists[side], side, touching)
        fresh = []
        for depth in range(depths):
            around_c = sheet_around(
                stores[side][3 + depth], conduct[depth + 1], outer_c, edges[side][3 + depth], lists[side], side,
                (minus, plus),
            )
            scaled, weight, _ = weights(conduct[depth], [filled(other, conduct[depth]) for other in around_c])
            forced = weight * sheet_of(even, ie, io, F + depth, side)
            if depth < DEPTHS[1]:
                for d in range(6):
                    keep_layers(kept, kept_index(side, depth) + d, scaled[d])
                keep_layers(kept, kept_index(side, depth) + 6, forced)
            around = sheet_around(
                stores[side][depth], iterate[depth + 1], outer, edges[side][depth], lists[side], side, (minus, plus)
            )
            fresh.append(swept(iterate[depth], forced, scaled, around))
            outer, outer_c = iterate[depth], conduct[depth]
        for depth in range(depths):
            fill_sheet(stores[side][depth], fresh[depth])
            keep_layers(sheets, side * depths + depth, fresh[depth])
    pack_lines([stores[side][: DEPTHS[1]] for side in range(2)], lists, ys, 2, 3)
    below, above = stores[0][0], stores[1][0]
    sweep_blocks((v, forth_in, back_in), mine, ghost, below, above, wk, wf, u, forth, back, faces)
    pick_faces(faces, mine, ys, 0, 3)


def second(turned, wk, wf, sent, got, ya, mine, parity, lists):
    return pl.pallas_call(
        second_kernel,
        in_specs=[SMEM] * 3 + [VMEM] * 10,
        out_specs=[VMEM] * 7,
        out_shape=[f32(*FIELD), f32(*TURNED), f32(*TURNED), tiles(3 * SLOTS)]
        + [tiles(28 * SLOTS), tiles(2 * DEPTHS[0] * SLOTS), tiles(2 * SLOTS)],
        scratch_shapes=[GHOSTS, scratch(FACES, *TILE), scratch(SLOTS, *TILE)] + GATHERED + [SHEET] * 24,
        compiler_params=params(16),
        cost_estimate=cost(1 << 22, 9 << 20),
        name="second",
    )(mine, parity, lists, *turned, wk, wf, *sent, *got, ya)


def third_kernel(
    mine, lists_in,
    v, forth_in, back_in, wk, wf, kept, sheets_in, ends_in, ya,
    u, forth, back, ys, sheets, ends,
    ghost, faces, minus, plus, touching, *sheet_refs,
):
    lists = [Lists(lists_in, side) for side in range(2)]
    place_faces(ya, mine, ghost, 0, 3)
    own_ends(v, ends)
    depths = DEPTHS[1]
    stores, edges = (sheet_refs[:2], sheet_refs[2:4]), (sheet_refs[4:6], sheet_refs[6:])
    place_lines(ya, lists, edges, 2, 3)
    sweep_sheets(sheets_in, ends_in, kept, depths, stores, edges, lists, (minus, plus, touching))
    for side in range(2):
        for depth in range(depths):
            keep_layers(sheets, side * depths + depth, stores[side][depth][:SLOTS])
    pack_lines([stores[side][: DEPTHS[2]] for side in range(2)], lists, ys, 2, 3)
    below, above = stores[0][0], stores[1][0]
    sweep_blocks((v, forth_in, back_in), mine, ghost, below, above, wk, wf, u, forth, back, faces)
    pick_faces(faces, mine, ys, 0, 3)


def third(turned, wk, wf, kept, sheets, ends, ya, mine, lists):
    return pl.pallas_call(
        third_kernel,
        in_specs=[SMEM] * 2 + [VMEM] * 9,
        out_specs=[VMEM] * 6,
        out_shape=[f32(*FIELD), f32(*TURNED), f32(*TURNED), tiles(3 * SLOTS)]
        + [tiles(2 * DEPTHS[1] * SLOTS), tiles(2 * SLOTS)],
        scratch_shapes=[GHOSTS, scratch(FACES, *TILE)] + GATHERED + [SHEET] * 8,
        compiler_params=params(16),
        cost_estimate=cost(1 << 22, 9 << 20),
        name="third",
    )(mine, lists, *turned, wk, wf, kept, sheets, ends, ya)


def last_kernel(
    mine, lists_in,
    v, forth_in, back_in, wk, wf, dg, kept, sheets_in, ends_in, ya,
    out, coarse,
    ghost, below, above, edge_b, edge_a, minus, plus, touching, residual, sem,
):
    write = pltpu.make_async_copy(v, out, sem)
    write.start()
    lists = [Lists(lists_in, side) for side in range(2)]
    place_faces(ya, mine, ghost, 0, 3)
    edges = ((edge_b,), (edge_a,))
    place_lines(ya, lists, edges, 2, 3)
    sweep_sheets(
        sheets_in, ends_in, kept, DEPTHS[2], ((below,), (above,)), edges, lists, (minus, plus, touching)
    )

    def one(j, carry):
        rows = block_rows(j)
        for n, centre, around in six_turned(v, forth_in, back_in, j, mine, ghost, below, above):
            total = wf[rows, column(n)] - OMEGA * centre
            for d in range(6):
                total = total + wk[d, rows, column(n)] * around[d]
            residual[n, rows, :] = total * dg[rows, column(n)]
        return carry

    lax.fori_loop(0, SLOTS, one, 0)
    lane = lax.broadcasted_iota(jnp.int32, (LANES, LANES), 0)
    target = lax.broadcasted_iota(jnp.int32, (LANES, LANES), 1)
    place = (lane // (2 * EDGE)) * (EDGE // 2) + (lane % EDGE) // 2
    half = ROWS // 2
    for part in range(2):
        total = jnp.zeros((half, LANES), jnp.float32)
        for n in range(4):
            column_sum = (
                residual[part * 4 + n, pl.ds(0, half, stride=2), :]
                + residual[part * 4 + n, pl.ds(1, half, stride=2), :]
            )
            gather = jnp.where(place + EDGE * n == target, 0.125, 0.0).astype(jnp.bfloat16)
            high = column_sum.astype(jnp.bfloat16)
            low = (column_sum - high.astype(jnp.float32)).astype(jnp.bfloat16)
            total = total + (
                jnp.dot(high, gather, preferred_element_type=jnp.float32)
                + jnp.dot(low, gather, preferred_element_type=jnp.float32)
            )
        coarse[:, part * LANES : (part + 1) * LANES] = total
    write.wait()


def last(turned, wk, wf, dg, kept, sheets, ends, ya, mine, lists):
    return pl.pallas_call(
        last_kernel,
        in_specs=[SMEM] * 2 + [VMEM] * 10,
        out_specs=[HBM, VMEM],
        out_shape=[f32(*FIELD), f32(ROWS // 2, PLANE // 4)],
        scratch_shapes=[GHOSTS]
        + [SHEET] * 4
        + GATHERED
        + [scratch(COLS, ROWS, LANES), pltpu.SemaphoreType.DMA],
        compiler_params=params(16),
        cost_estimate=cost(1 << 24, 10 << 20),
        name="last",
    )(mine, lists, *turned, wk, wf, dg, kept, sheets, ends, ya)


def pair_swap(values, stride):
    count = lax.axis_size("owner")
    return lax.ppermute(values, "owner", [(i, i ^ stride) for i in range(count)])


def odd_pair_swap(values):
    count = lax.axis_size("owner")
    return lax.ppermute(values, "owner", [(i, ((i - 1) ^ 1) + 1) for i in range(1, count - 1)])


def in_hbm(values):
    return pltpu.with_memory_space_constraint(values, pltpu.HBM)


def segment_swap(ys):
    return lax.all_to_all(ys, "sub", split_axis=0, concat_axis=0, tiled=True)


def body(guess, rhs, coef, occupied, neighbours, swap_slot, send_list, recv_list):
    my_owner = lax.axis_index("owner").astype(jnp.int32)
    owner = my_owner.reshape(1)
    parity = (my_owner % 2).reshape(1)
    fields = tuple(values.reshape(FIELD) for values in (guess, rhs, coef))
    fields = tuple(in_hbm(x) for x in fields)
    occupied, swap_slot = in_hbm(occupied), in_hbm(swap_slot)
    bulk = [
        pair_swap(block, 1 << bit)
        for bits in (SOON, LATE)
        for bit, block in zip(bits, swap_pack(fields, occupied, swap_slot, owner, bits))
    ]
    top, bottom, faces, mine, *merged = local(fields, occupied, neighbours, in_hbm(send_list), in_hbm(recv_list))
    (top, bottom, faces), merged = soon((top, bottom, faces), merged, bulk[:2], swap_slot, owner)
    ze, zo, ys = ends(top, bottom, faces, bulk[2:], swap_slot, owner, mine, parity)
    sent, got, ya = (ze, zo), (pair_swap(ze, 1), odd_pair_swap(zo)), segment_swap(ys)
    wk, wf, dg, v, forth, back, ys, lists = first(merged, bulk[2:], got, ya, swap_slot, owner, mine, parity)
    turned = v, forth, back
    *turned, ys, kept, sheets, ends_of = second(turned, wk, wf, sent, got, segment_swap(ys), mine, parity, lists)
    *turned, ys, sheets, ends_of = third(turned, wk, wf, kept, sheets, ends_of, segment_swap(ys), mine, lists)
    v, coarse = last(turned, wk, wf, dg, kept, sheets, ends_of, segment_swap(ys), mine, lists)
    return v.reshape(SLOTS, EDGE, PLANE), coarse.reshape(SLOTS, EDGE // 2, PLANE // 4)


def solution(mesh):
    wide, flat, single = P(("owner", "sub"), None, None), P(("owner", "sub"), None), P(("owner", "sub"))
    return jax.shard_map(
        body,
        mesh=mesh,
        in_specs=(wide, wide, wide, single, flat, flat, flat, flat),
        out_specs=(wide, wide),
        check_vma=False,
    )
```

```python
import jax
import jax.numpy as jnp
from jax import lax
from jax.experimental import pallas as pl
from jax.experimental.pallas import tpu as pltpu
from jax.sharding import PartitionSpec as P

OMEGA = 0.8
SLOTS = 8
EDGE = 32
PLANE = EDGE * EDGE
ROWS = SLOTS * EDGE
LANES = 128
COLS = PLANE // LANES
FIELD = (ROWS, PLANE)
TURNED = (ROWS + EDGE, PLANE)
FACES = 2 * SLOTS
TILE = (8, LANES)
BITS = 4
GROUP = 8
ORDER = (2, 0, 3, 1)
SOON, LATE = ORDER[:2], ORDER[2:]
V, C, F = 0, 4, 8
KINDS = 11
DEPTHS = (3, 2, 1)
SEND = 4 * SLOTS
RECV = SEND + FACES
LISTS = RECV + FACES
SMEM = pl.BlockSpec(memory_space=pltpu.SMEM)
VMEM = pl.BlockSpec(memory_space=pltpu.VMEM)
HBM = pl.BlockSpec(memory_space=pltpu.HBM)


def f32(*shape):
    return jax.ShapeDtypeStruct(shape, jnp.float32)


def tiles(count):
    return f32(count, *TILE)


def scratch(*shape):
    return pltpu.VMEM(shape, jnp.float32)


def params(mib):
    return pltpu.CompilerParams(vmem_limit_bytes=mib << 20)


def cost(flops, bytes_accessed):
    return pl.CostEstimate(flops=flops, bytes_accessed=bytes_accessed, transcendentals=0)


def column(c):
    return slice(c * LANES, (c + 1) * LANES)


def block_rows(j):
    return pl.ds(pl.multiple_of(j * EDGE, EDGE), EDGE)


def iotas(shape):
    rank = len(shape)
    sub = lax.broadcasted_iota(jnp.int32, shape, rank - 2)
    lane = lax.broadcasted_iota(jnp.int32, shape, rank - 1)
    return sub, lane


def slot_or(entry, none):
    return jnp.where(entry >= 0, jnp.maximum(entry, 0) % SLOTS, none)


def layer_tile(field, row, out, index):
    for c in range(COLS):
        out[index, c : c + 1, :] = field[row : row + 1, column(c)]


def face_of(cells, side, forth=None, back=None):
    group = lax.broadcasted_iota(jnp.int32, TILE, 1) // EDGE
    turned = {0: cells, EDGE: forth, LANES - EDGE: back}
    face = None
    for g in range(4):
        turn = (EDGE * g + EDGE * side) % LANES
        rows = slice(8 * g, 8 * g + 8)
        done = turned.get(turn)
        part = pltpu.roll(cells[rows], turn, 1) if done is None else done[rows]
        face = part if face is None else jnp.where(group == g, part, face)
    return face


def face_tile(field, first_row, side):
    return face_of(field[first_row : first_row + EDGE, column(COLS - 1 if side else 0)], side)


def unpack_face(face, side):
    parts = []
    for g in range(4):
        turn = (-EDGE * g - EDGE * side) % LANES
        parts.append(pltpu.roll(face, turn, 1) if turn else face)
    return jnp.concatenate(parts, axis=0)


def pick_faces(faces, mine, out, offset, stride):
    for entry in range(FACES):
        face = mine[SEND + entry]
        out[(entry // 2) * stride + entry % 2 + offset] = faces[jnp.maximum(face, 0)] * (face >= 0).astype(
            jnp.float32
        )


def place_faces(arrived, mine, ghost, offset, stride):
    ghost[...] = jnp.zeros(ghost.shape, jnp.float32)
    for entry in range(FACES):
        face = mine[RECV + entry]
        ghost[jnp.where(face >= 0, face, FACES)] = arrived[(entry // 2) * stride + entry % 2 + offset]


class Lists:
    def __init__(self, lists, side):
        self.lists, self.side = lists, side

    def at(self, i):
        return self.lists[self.side, i]

    def neighbour(self, slot, direction):
        return self.at(4 * slot + direction)

    def send(self, entry):
        return self.at(SEND + entry)

    def recv(self, entry):
        return self.at(RECV + entry)


def lists_tile(mine):
    sub, lane = iotas(TILE)
    tile = jnp.zeros(TILE, jnp.float32)
    for i in range(LISTS):
        tile = jnp.where(lane == i, mine[i].astype(jnp.float32), tile)
    return jnp.where(sub == 0, tile, 0.0)


def list_copies(ie, io, held, sems):
    return [
        pltpu.make_async_copy(source.at[KINDS * SLOTS], held.at[k], sems.at[k]) for k, source in enumerate((ie, io))
    ]


def read_lists(even, held, lists):
    for side in range(2):
        source = jnp.where(even, 1 - side, side)
        for i in range(LISTS):
            lists[side, i] = held[source, 0, i].astype(jnp.int32)
    return [Lists(lists, side) for side in range(2)]


def sheet_of(even, from_even, from_odd, kind, side):
    rows = slice(kind * SLOTS, (kind + 1) * SLOTS)
    pair = (from_even[rows], from_odd[rows])
    return jnp.where(even, *(pair if side else pair[::-1]))


def own_end(even, to_even, to_odd, kind, side):
    return sheet_of(even, to_even, to_odd, kind, side)


def fill_sheet(store, value):
    store[:SLOTS] = value
    store[SLOTS] = jnp.zeros(TILE, jnp.float32)


def pack_lines(sheets, lists, out, tile, stride):
    sub, lane = iotas(TILE)
    for peer in range(SLOTS):
        totals = []
        row = 0
        for side in range(2):
            for i in range(2):
                face = lists[side].send(2 * peer + i)
                slot = jnp.where(face >= 0, jnp.maximum(face, 0) // 2, SLOTS)
                high = jnp.maximum(face, 0) % 2 == 1
                for store in sheets[side]:
                    line = store[slot]
                    low_line = line[0:1, :]
                    high_line = pltpu.roll(line, EDGE, 1)[7:8, :]
                    if row % 8 == 0:
                        totals.append(jnp.zeros(TILE, jnp.float32))
                    totals[-1] = jnp.where(sub == row % 8, jnp.where(high, high_line, low_line), totals[-1])
                    row += 1
        total = totals[0]
        for group, part in enumerate(totals[1:], 1):
            total = jnp.where(lane // EDGE == group, pltpu.roll(part, EDGE * group, 1), total)
        out[peer * stride + tile] = total


def place_lines(arrived, lists, edges, tile, stride):
    for stores in edges:
        for store in stores:
            store[...] = jnp.zeros(store.shape, jnp.float32)
    sub, lane = iotas(TILE)
    first = (sub == 0) & (lane < EDGE)
    final = (sub == 7) & (lane >= LANES - EDGE)
    groups = (4 * len(edges[0]) + 7) // 8
    for peer in range(SLOTS):
        got = arrived[peer * stride + tile]
        turned = [got] + [pltpu.roll(got, LANES - EDGE * g, 1) for g in range(1, groups + 1)]
        row = 0
        for side in range(2):
            for i in range(2):
                ghost = lists[side].recv(2 * peer + i)
                slot = jnp.where(ghost >= 0, jnp.maximum(ghost, 0) // 2, SLOTS)
                high = jnp.maximum(ghost, 0) % 2 == 1
                for store in edges[side]:
                    group, at = row // 8, row % 8
                    low_part = jnp.where(first, turned[group][at : at + 1, :], 0.0)
                    high_part = jnp.where(final, turned[group + 1][at : at + 1, :], 0.0)
                    store[slot] = store[slot] + jnp.where(high, high_part, low_part)
                    row += 1


def beyond(ends, lists, side, gathered):
    for slot in range(SLOTS):
        entry = lists.neighbour(slot, 2 if side else 3)
        gathered[slot] = ends[slot_or(entry, 0)] * (entry >= 0).astype(jnp.float32)
    return gathered[...]


def sheet_around(store, inner, outer, edge, lists, side, gathered):
    shape = (SLOTS,) + TILE
    sub, lane = iotas(shape)
    x = lane % EDGE
    minus, plus = gathered
    for slot in range(SLOTS):
        minus[slot] = store[slot_or(lists.neighbour(slot, 0), SLOTS)]
        plus[slot] = store[slot_or(lists.neighbour(slot, 1), SLOTS)]
    value = store[:SLOTS]
    edges = edge[:SLOTS]
    forth = pltpu.roll(value, EDGE, 2)
    back = pltpu.roll(value, LANES - EDGE, 2)
    before = jnp.where(lane < EDGE, pltpu.roll(forth, 1, 1), forth)
    after = jnp.where(lane >= LANES - EDGE, pltpu.roll(back, 7, 1), back)
    return (
        jnp.where(x == 0, pltpu.roll(minus[...], LANES - EDGE + 1, 2), pltpu.roll(value, 1, 2)),
        jnp.where(x == EDGE - 1, pltpu.roll(plus[...], EDGE - 1, 2), pltpu.roll(value, LANES - 1, 2)),
        jnp.where((lane < EDGE) & (sub == 0), edges, before),
        jnp.where((lane >= LANES - EDGE) & (sub == 7), edges, after),
        outer if side else inner,
        inner if side else outer,
    )


def layers(ref, index):
    return ref[index * SLOTS : (index + 1) * SLOTS]


def keep_layers(ref, index, value):
    ref[index * SLOTS : (index + 1) * SLOTS] = value


def swept(value, forced, scaled, around):
    total = forced + (1.0 - OMEGA) * value
    for d in range(6):
        total = total + scaled[d] * around[d]
    return total


def kept_index(side, depth):
    return 7 * (2 * side + depth)


def sweep_sheets(sheets, ends, kept, depths, stores, edges, lists, gathered):
    minus, plus, touching = gathered
    for side in range(2):
        old = [layers(sheets, side * (depths + 1) + depth) for depth in range(depths + 1)]
        for depth in range(depths):
            fill_sheet(stores[side][depth], old[depth])
        outer = beyond(ends.at[pl.ds(side * SLOTS, SLOTS)], lists[side], side, touching)
        fresh = []
        for depth in range(depths):
            around = sheet_around(
                stores[side][depth], old[depth + 1], outer, edges[side][depth], lists[side], side, (minus, plus)
            )
            at = kept_index(side, depth)
            scaled = [layers(kept, at + d) for d in range(6)]
            fresh.append(swept(old[depth], layers(kept, at + 6), scaled, around))
            outer = old[depth]
        for depth in range(depths):
            fill_sheet(stores[side][depth], fresh[depth])


def own_ends(v, out):
    for j in range(SLOTS):
        layer_tile(v, j * EDGE, out, j)
        layer_tile(v, j * EDGE + EDGE - 1, out, SLOTS + j)


def weights(k, around):
    faces = [k + other for other in around]
    total = (faces[0] + faces[1]) + (faces[2] + faces[3]) + (faces[4] + faces[5])
    inverse = pl.reciprocal(total, approx=True)
    inverse = inverse * (2.0 - total * inverse)
    factor = jnp.where(k > 0.0, OMEGA * inverse, 0.0)
    return [factor * face for face in faces], 2.0 * factor, total * (0.5 / OMEGA)


def filled(other, own):
    return jnp.where(other > 0.0, other, own)


def six_turned(field, forth, back, j, mine, ghost, below, above, fill=False):
    _, lane = iotas((EDGE, LANES))
    x = lane % EDGE
    xm, xp, zm, zp = [slot_or(mine[4 * j + side], SLOTS) for side in range(4)]
    under_face, over_face = below[zm], above[zp]
    own, minus_rows, plus_rows = block_rows(j), block_rows(xm), block_rows(xp)
    for c in range(COLS):
        v = field[own, column(c)]
        before = forth[own, column(c - 1)] if c else unpack_face(ghost[2 * j], 0)
        after = back[own, column(c + 1)] if c < COLS - 1 else unpack_face(ghost[2 * j + 1], 1)
        under, over = under_face[c : c + 1, :], over_face[c : c + 1, :]
        around = [
            pltpu.roll(jnp.where(x == EDGE - 1, back[minus_rows, column(c)], v), 1, 1),
            pltpu.roll(jnp.where(x == 0, forth[plus_rows, column(c)], v), LANES - 1, 1),
            jnp.where(lane < EDGE, before, forth[own, column(c)]),
            jnp.where(lane >= LANES - EDGE, after, back[own, column(c)]),
        ]
        if fill:
            ends = (True, True, c == 0, c == COLS - 1)
            around = [filled(other, v) if end else other for other, end in zip(around, ends)]
            under, over = filled(under, v[:1]), filled(over, v[EDGE - 1 :])
        around.append(jnp.concatenate([under, v[: EDGE - 1]], axis=0))
        around.append(jnp.concatenate([v[1:], over], axis=0))
        yield c, v, around


def store_swept(total, n, j, u, forth, back, faces):
    rows = block_rows(j)
    ahead, behind = pltpu.roll(total, EDGE, 1), pltpu.roll(total, LANES - EDGE, 1)
    u[rows, column(n)] = total
    forth[rows, column(n)] = ahead
    back[rows, column(n)] = behind
    if n in (0, COLS - 1):
        side = n // (COLS - 1)
        faces[2 * j + side] = face_of(total, side, ahead, behind)


def turn_block(field, j, forth, back):
    rows = block_rows(j)
    for c in range(COLS):
        cells = field[rows, column(c)]
        forth[rows, column(c)] = pltpu.roll(cells, EDGE, 1)
        back[rows, column(c)] = pltpu.roll(cells, LANES - EDGE, 1)


def end_turned(forth, back):
    for turned in (forth, back):
        turned[ROWS:, :] = jnp.zeros((EDGE, PLANE), jnp.float32)


def sweep_blocks(turned, mine, ghost, below, above, wk, wf, u, forth, back, faces):
    def one(j, carry):
        rows = block_rows(j)
        ready = []
        for n, centre, around in six_turned(*turned, j, mine, ghost, below, above):
            total = wf[rows, column(n)] + (1.0 - OMEGA) * centre
            for d in range(6):
                total = total + wk[d, rows, column(n)] * around[d]
            ready.append((total, n))
            if len(ready) == GROUP:
                for total, n in ready:
                    store_swept(total, n, j, u, forth, back, faces)
                ready = []
        return carry

    lax.fori_loop(0, SLOTS, one, 0)
    end_turned(forth, back)


def pair_slot(pairs, owner, bit):
    return pairs[0, owner[0] ^ (1 << bit)]


def block_tiles(v, f, c, row, out):
    for end in range(2):
        for kind, field, count in ((V, v, 4), (C, c, 4), (F, f, 3)):
            for depth in range(count):
                layer_tile(field, row + (depth if end else EDGE - 1 - depth), out, end * KINDS + kind + depth)
    for k, field in enumerate((v, c)):
        for side in range(2):
            out[2 * KINDS + 2 * k + side] = face_tile(field, row, side)


def swap_pack_kernel(bits, pairs, owner, occupied, guess, rhs, coef, *refs):
    bulk, sems = refs[: len(bits)], refs[len(bits)]
    slots = [jnp.maximum(pair_slot(pairs, owner, bit), 0) for bit in bits]

    def copies(n):
        return [
            pltpu.make_async_copy(
                source.at[block_rows(slots[n])], bulk[n].at[pl.ds(k * EDGE, EDGE)], sems.at[n, k]
            )
            for k, source in enumerate((guess, rhs, coef))
        ]

    for n in range(len(bits)):
        for copy in copies(n):
            copy.start()
    for n in range(len(bits)):
        for copy in copies(n):
            copy.wait()

        @pl.when(occupied[slots[n]] == 0)
        def _(n=n):
            bulk[n][...] = jnp.zeros((3 * EDGE, PLANE), jnp.float32)


def swap_pack(fields, occupied, pairs, owner, bits):
    return pl.pallas_call(
        lambda *refs: swap_pack_kernel(bits, *refs),
        in_specs=[SMEM] * 3 + [HBM] * 3,
        out_specs=[VMEM] * len(bits),
        out_shape=[f32(3 * EDGE, PLANE)] * len(bits),
        scratch_shapes=[pltpu.SemaphoreType.DMA((len(bits), 3))],
        compiler_params=params(8),
        cost_estimate=cost(1 << 19, len(bits) * (768 << 10)),
        name="swap_pack",
    )(pairs, owner, occupied, *fields)


def local_kernel(
    occupied, neighbours, send_list, recv_list, guess, rhs, coef, top, bottom, faces, mine, v, f, c, forth_v, back_v, forth_c, back_c, sems
):
    copies = [
        pltpu.make_async_copy(source, target, sems.at[k])
        for k, (source, target) in enumerate(((guess, v), (coef, c), (rhs, f)))
    ]
    for copy in copies:
        copy.start()
    for slot in range(SLOTS):
        for side in range(4):
            mine[4 * slot + side] = neighbours[slot, side]
    for entry in range(FACES):
        mine[SEND + entry] = send_list[0, entry]
        mine[RECV + entry] = recv_list[0, entry]
    for k, (field, kinds) in enumerate(((v, range(V, C)), (c, range(C, F)), (f, range(F, KINDS)))):
        copies[k].wait()
        for j in range(SLOTS):

            @pl.when(occupied[j] == 0)
            def _(field=field, j=j):
                field[j * EDGE : (j + 1) * EDGE, :] = jnp.zeros((EDGE, PLANE), jnp.float32)

        for j in range(SLOTS):
            for depth, kind in enumerate(kinds):
                for end, out in enumerate((top, bottom)):
                    row = j * EDGE + (depth if end else EDGE - 1 - depth)
                    layer_tile(field, row, out, kind * SLOTS + j)
            if k < 2:
                for side in range(2):
                    faces[k * FACES + 2 * j + side] = face_tile(field, j * EDGE, side)
    for field, forth, back in ((v, forth_v, back_v), (c, forth_c, back_c)):

        def one(j, carry, field=field, forth=forth, back=back):
            turn_block(field, j, forth, back)
            return carry

        lax.fori_loop(0, SLOTS, one, 0)
        end_turned(forth, back)


def local(fields, occupied, neighbours, send_list, recv_list):
    return pl.pallas_call(
        local_kernel,
        in_specs=[SMEM] * 4 + [HBM] * 3,
        out_specs=[VMEM] * 3 + [SMEM] + [VMEM] * 7,
        out_shape=[tiles(KINDS * SLOTS)] * 2
        + [tiles(2 * FACES), jax.ShapeDtypeStruct((LISTS,), jnp.int32)]
        + [f32(*FIELD)] * 3
        + [f32(*TURNED)] * 4,
        scratch_shapes=[pltpu.SemaphoreType.DMA((3,))],
        compiler_params=params(8),
        cost_estimate=cost(1 << 20, 4 << 20),
        name="local",
    )(occupied, neighbours, send_list, recv_list, *fields)


def soon_kernel(pairs, owner, *refs):
    bulk = dict(zip(SOON, refs))
    top, bottom, faces, v, f, c, forth_v, back_v, forth_c, back_c, fresh, sems = refs[len(SOON) + 3 + len(MERGED) :]

    def merges(bit, slot):
        return [
            pltpu.make_async_copy(bulk[bit].at[pl.ds(k * EDGE, EDGE)], field.at[block_rows(slot)], sems.at[bit, k])
            for k, field in enumerate((v, f, c))
        ]

    for bit in SOON:
        slot = pair_slot(pairs, owner, bit)

        @pl.when(slot >= 0)
        def _(bit=bit, slot=jnp.maximum(slot, 0)):
            for copy in merges(bit, slot):
                copy.start()
            block_tiles(*(bulk[bit].at[pl.ds(k * EDGE, EDGE)] for k in range(3)), 0, fresh)
            for kind in range(KINDS):
                top[kind * SLOTS + slot] = fresh[kind]
                bottom[kind * SLOTS + slot] = fresh[KINDS + kind]
            for k in range(2):
                for side in range(2):
                    faces[k * FACES + 2 * slot + side] = fresh[2 * KINDS + 2 * k + side]
            for copy in merges(bit, slot):
                copy.wait()
            turn_block(v, slot, forth_v, back_v)
            turn_block(c, slot, forth_c, back_c)


def soon(tops, merged, bulk, pairs, owner):
    count = 3 + len(MERGED)
    outs = pl.pallas_call(
        soon_kernel,
        in_specs=[SMEM] * 2 + [VMEM] * (len(SOON) + count),
        out_specs=[VMEM] * count,
        out_shape=[tiles(KINDS * SLOTS)] * 2 + [tiles(2 * FACES)] + MERGED,
        input_output_aliases={2 + len(SOON) + k: k for k in range(count)},
        scratch_shapes=[scratch(2 * KINDS + 4, *TILE), pltpu.SemaphoreType.DMA((BITS, 3))],
        compiler_params=params(8),
        cost_estimate=cost(1 << 18, 2 << 20),
        name="soon",
    )(pairs, owner, *bulk, *tops, *merged)
    return outs[:3], outs[3:]


def ends_kernel(pairs, owner, mine, parity, top, bottom, faces, *refs):
    bulk = dict(zip(LATE, refs))
    ze, zo, ys, held, fresh = refs[len(LATE) :]
    even = parity[0] == 0
    ze[: KINDS * SLOTS] = jnp.where(even, top[...], bottom[...])
    zo[: KINDS * SLOTS] = jnp.where(even, bottom[...], top[...])
    ze[KINDS * SLOTS] = zo[KINDS * SLOTS] = lists_tile(mine)
    held[...] = faces[...]
    for bit in LATE:
        slot = pair_slot(pairs, owner, bit)

        @pl.when(slot >= 0)
        def _(bit=bit, slot=jnp.maximum(slot, 0)):
            block_tiles(*(bulk[bit].at[pl.ds(k * EDGE, EDGE)] for k in range(3)), 0, fresh)
            for kind in range(KINDS):
                high, low = fresh[kind], fresh[KINDS + kind]
                ze[kind * SLOTS + slot] = jnp.where(even, high, low)
                zo[kind * SLOTS + slot] = jnp.where(even, low, high)
            for k in range(2):
                for side in range(2):
                    held[k * FACES + 2 * slot + side] = fresh[2 * KINDS + 2 * k + side]

    for k in range(2):
        pick_faces(held.at[pl.ds(k * FACES, FACES)], mine, ys, 2 * k, 4)

def ends(top, bottom, faces, bulk, pairs, owner, mine, parity):
    return pl.pallas_call(
        ends_kernel,
        in_specs=[SMEM] * 4 + [VMEM] * (3 + len(LATE)),
        out_specs=[VMEM] * 3,
        out_shape=[tiles(KINDS * SLOTS + 1)] * 2 + [tiles(2 * FACES)],
        scratch_shapes=[scratch(2 * FACES, *TILE), scratch(2 * KINDS + 4, *TILE)],
        compiler_params=params(8),
        cost_estimate=cost(1 << 18, 1 << 20),
        name="ends",
    )(pairs, owner, mine, parity, top, bottom, faces, *bulk)


def first_kernel(pairs, owner, mine, parity, ie, io, ya, *refs):
    bulk, refs = dict(zip(LATE, refs)), refs[len(LATE) + len(MERGED) :]
    v, f, c, forth_v, back_v, forth_c, back_c = refs[: len(MERGED)]
    wk, wf, dg, u, forth, back, ys, lists_out = refs[len(MERGED) : len(MERGED) + 8]
    ghost, ghost_c, faces, held, list_sems, sems, *sheet_refs = refs[len(MERGED) + 8 :]
    even = parity[0] == 0
    slots = {bit: pair_slot(pairs, owner, bit) for bit in LATE}

    def merges(k):
        for bit in LATE:
            copy = pltpu.make_async_copy(
                bulk[bit].at[pl.ds(k * EDGE, EDGE)],
                (v, f, c)[k].at[block_rows(jnp.maximum(slots[bit], 0))],
                sems.at[bit, k],
            )
            yield slots[bit], copy

    def start(k):
        for slot, copy in merges(k):

            @pl.when(slot >= 0)
            def _(copy=copy):
                copy.start()

    def settle(k, field=None, forth=None, back=None):
        for slot, copy in merges(k):

            @pl.when(slot >= 0)
            def _(slot=jnp.maximum(slot, 0), copy=copy):
                copy.wait()
                if field is not None:
                    turn_block(field, slot, forth, back)

    copies = list_copies(ie, io, held, list_sems)
    for copy in copies:
        copy.start()
    for k in (2, 1, 0):
        start(k)
    sheets = sheet_refs[:6], sheet_refs[6:]
    for side in range(2):
        for store, kind in zip(sheets[side], (V, V + 1, V + 2, C, C + 1, C + 2)):
            fill_sheet(store, sheet_of(even, ie, io, kind, side))
    (below, _, _, below_c, _, _), (above, _, _, above_c, _, _) = sheets
    place_faces(ya, mine, ghost, 0, 4)
    place_faces(ya, mine, ghost_c, 2, 4)
    for copy in copies:
        copy.wait()
    lists = read_lists(even, held, lists_out)
    pack_lines(sheets, lists, ys, 2, 3)
    settle(2, c, forth_c, back_c)
    settle(1)
    settle(0, v, forth_v, back_v)

    def one(j, carry):
        rows = block_rows(j)
        conduct = six_turned(c, forth_c, back_c, j, mine, ghost_c, below_c, above_c, fill=True)
        iterate = six_turned(v, forth_v, back_v, j, mine, ghost, below, above)
        ready = []
        for (n, k, around_k), (_, centre, around) in zip(conduct, iterate):
            scaled, weight, inverse = weights(k, around_k)
            forced = weight * f[rows, column(n)]
            wf[rows, column(n)] = forced
            dg[rows, column(n)] = inverse
            total = forced + (1.0 - OMEGA) * centre
            for d in range(6):
                wk[d, rows, column(n)] = scaled[d]
                total = total + scaled[d] * around[d]
            ready.append((total, n))
        for total, n in ready:
            store_swept(total, n, j, u, forth, back, faces)
        return carry

    lax.fori_loop(0, SLOTS, one, 0)
    end_turned(forth, back)
    pick_faces(faces, mine, ys, 0, 3)


SHEET = scratch(SLOTS + 1, *TILE)
GHOSTS = scratch(FACES + 1, *TILE)
GATHERED = [scratch(SLOTS, *TILE)] * 3


MERGED = [f32(*FIELD)] * 3 + [f32(*TURNED)] * 4


def first(merged, bulk, ends_in, ya, pairs, owner, mine, parity):
    outs = pl.pallas_call(
        first_kernel,
        in_specs=[SMEM] * 4 + [VMEM] * (3 + len(LATE) + len(MERGED)),
        out_specs=[VMEM] * (len(MERGED) + 7) + [SMEM],
        out_shape=MERGED
        + [f32(6, *FIELD)]
        + [f32(*FIELD)] * 3
        + [f32(*TURNED)] * 2
        + [tiles(3 * SLOTS), jax.ShapeDtypeStruct((2, LISTS), jnp.int32)],
        input_output_aliases={7 + len(LATE) + k: k for k in range(len(MERGED))},
        scratch_shapes=[GHOSTS] * 2
        + [scratch(FACES, *TILE), pltpu.SMEM((2,) + TILE, jnp.float32), pltpu.SemaphoreType.DMA((2,))]
        + [pltpu.SemaphoreType.DMA((BITS, 3))]
        + [SHEET] * 12,
        compiler_params=params(20),
        cost_estimate=cost(1 << 24, 12 << 20),
        name="first",
    )(pairs, owner, mine, parity, *ends_in, ya, *bulk, *merged)
    return outs[len(MERGED) :]


def second_kernel(
    mine, parity, lists_in,
    v, forth_in, back_in, wk, wf, ye, yo, ie, io, ya,
    u, forth, back, ys, kept, sheets, ends,
    ghost, faces, ends_out, minus, plus, touching, *sheet_refs,
):
    even = parity[0] == 0
    lists = [Lists(lists_in, side) for side in range(2)]
    place_faces(ya, mine, ghost, 0, 3)
    own_ends(v, ends)
    depths = DEPTHS[0]
    stores, edges = (sheet_refs[:6], sheet_refs[6:12]), (sheet_refs[12:18], sheet_refs[18:])
    place_lines(ya, lists, edges, 2, 3)
    for side in range(2):
        iterate = [sheet_of(even, ie, io, V + depth, side) for depth in range(depths + 1)]
        conduct = [sheet_of(even, ie, io, C + depth, side) for depth in range(depths + 1)]
        for depth in range(depths):
            fill_sheet(stores[side][depth], iterate[depth])
            fill_sheet(stores[side][3 + depth], conduct[depth])
        ends_out[...] = own_end(even, ye, yo, V, side)
        outer = beyond(ends_out, lists[side], side, touching)
        ends_out[...] = own_end(even, ye, yo, C, side)
        outer_c = beyond(ends_out, lists[side], side, touching)
        fresh = []
        for depth in range(depths):
            around_c = sheet_around(
                stores[side][3 + depth], conduct[depth + 1], outer_c, edges[side][3 + depth], lists[side], side,
                (minus, plus),
            )
            scaled, weight, _ = weights(conduct[depth], [filled(other, conduct[depth]) for other in around_c])
            forced = weight * sheet_of(even, ie, io, F + depth, side)
            if depth < DEPTHS[1]:
                for d in range(6):
                    keep_layers(kept, kept_index(side, depth) + d, scaled[d])
                keep_layers(kept, kept_index(side, depth) + 6, forced)
            around = sheet_around(
                stores[side][depth], iterate[depth + 1], outer, edges[side][depth], lists[side], side, (minus, plus)
            )
            fresh.append(swept(iterate[depth], forced, scaled, around))
            outer, outer_c = iterate[depth], conduct[depth]
        for depth in range(depths):
            fill_sheet(stores[side][depth], fresh[depth])
            keep_layers(sheets, side * depths + depth, fresh[depth])
    pack_lines([stores[side][: DEPTHS[1]] for side in range(2)], lists, ys, 2, 3)
    below, above = stores[0][0], stores[1][0]
    sweep_blocks((v, forth_in, back_in), mine, ghost, below, above, wk, wf, u, forth, back, faces)
    pick_faces(faces, mine, ys, 0, 3)


def second(turned, wk, wf, sent, got, ya, mine, parity, lists):
    return pl.pallas_call(
        second_kernel,
        in_specs=[SMEM] * 3 + [VMEM] * 10,
        out_specs=[VMEM] * 7,
        out_shape=[f32(*FIELD), f32(*TURNED), f32(*TURNED), tiles(3 * SLOTS)]
        + [tiles(28 * SLOTS), tiles(2 * DEPTHS[0] * SLOTS), tiles(2 * SLOTS)],
        scratch_shapes=[GHOSTS, scratch(FACES, *TILE), scratch(SLOTS, *TILE)] + GATHERED + [SHEET] * 24,
        compiler_params=params(16),
        cost_estimate=cost(1 << 22, 9 << 20),
        name="second",
    )(mine, parity, lists, *turned, wk, wf, *sent, *got, ya)


def third_kernel(
    mine, lists_in,
    v, forth_in, back_in, wk, wf, kept, sheets_in, ends_in, ya,
    u, forth, back, ys, sheets, ends,
    ghost, faces, minus, plus, touching, *sheet_refs,
):
    lists = [Lists(lists_in, side) for side in range(2)]
    place_faces(ya, mine, ghost, 0, 3)
    own_ends(v, ends)
    depths = DEPTHS[1]
    stores, edges = (sheet_refs[:2], sheet_refs[2:4]), (sheet_refs[4:6], sheet_refs[6:])
    place_lines(ya, lists, edges, 2, 3)
    sweep_sheets(sheets_in, ends_in, kept, depths, stores, edges, lists, (minus, plus, touching))
    for side in range(2):
        for depth in range(depths):
            keep_layers(sheets, side * depths + depth, stores[side][depth][:SLOTS])
    pack_lines([stores[side][: DEPTHS[2]] for side in range(2)], lists, ys, 2, 3)
    below, above = stores[0][0], stores[1][0]
    sweep_blocks((v, forth_in, back_in), mine, ghost, below, above, wk, wf, u, forth, back, faces)
    pick_faces(faces, mine, ys, 0, 3)


def third(turned, wk, wf, kept, sheets, ends, ya, mine, lists):
    return pl.pallas_call(
        third_kernel,
        in_specs=[SMEM] * 2 + [VMEM] * 9,
        out_specs=[VMEM] * 6,
        out_shape=[f32(*FIELD), f32(*TURNED), f32(*TURNED), tiles(3 * SLOTS)]
        + [tiles(2 * DEPTHS[1] * SLOTS), tiles(2 * SLOTS)],
        scratch_shapes=[GHOSTS, scratch(FACES, *TILE)] + GATHERED + [SHEET] * 8,
        compiler_params=params(16),
        cost_estimate=cost(1 << 22, 9 << 20),
        name="third",
    )(mine, lists, *turned, wk, wf, kept, sheets, ends, ya)


def last_kernel(
    mine, lists_in,
    v, forth_in, back_in, wk, wf, dg, kept, sheets_in, ends_in, ya,
    out, coarse,
    ghost, below, above, edge_b, edge_a, minus, plus, touching, residual, sem,
):
    write = pltpu.make_async_copy(v, out, sem)
    write.start()
    lists = [Lists(lists_in, side) for side in range(2)]
    place_faces(ya, mine, ghost, 0, 3)
    edges = ((edge_b,), (edge_a,))
    place_lines(ya, lists, edges, 2, 3)
    sweep_sheets(
        sheets_in, ends_in, kept, DEPTHS[2], ((below,), (above,)), edges, lists, (minus, plus, touching)
    )

    def one(j, carry):
        rows = block_rows(j)
        for n, centre, around in six_turned(v, forth_in, back_in, j, mine, ghost, below, above):
            total = wf[rows, column(n)] - OMEGA * centre
            for d in range(6):
                total = total + wk[d, rows, column(n)] * around[d]
            residual[n, rows, :] = total * dg[rows, column(n)]
        return carry

    lax.fori_loop(0, SLOTS, one, 0)
    lane = lax.broadcasted_iota(jnp.int32, (LANES, LANES), 0)
    target = lax.broadcasted_iota(jnp.int32, (LANES, LANES), 1)
    place = (lane // (2 * EDGE)) * (EDGE // 2) + (lane % EDGE) // 2
    half = ROWS // 2
    for part in range(2):
        total = jnp.zeros((half, LANES), jnp.float32)
        for n in range(4):
            column_sum = (
                residual[part * 4 + n, pl.ds(0, half, stride=2), :]
                + residual[part * 4 + n, pl.ds(1, half, stride=2), :]
            )
            gather = jnp.where(place + EDGE * n == target, 0.125, 0.0).astype(jnp.bfloat16)
            high = column_sum.astype(jnp.bfloat16)
            low = (column_sum - high.astype(jnp.float32)).astype(jnp.bfloat16)
            total = total + jnp.dot(
                jnp.concatenate([high, low], axis=1),
                jnp.concatenate([gather, gather], axis=0),
                preferred_element_type=jnp.float32,
            )
        coarse[:, part * LANES : (part + 1) * LANES] = total
    write.wait()


def last(turned, wk, wf, dg, kept, sheets, ends, ya, mine, lists):
    return pl.pallas_call(
        last_kernel,
        in_specs=[SMEM] * 2 + [VMEM] * 10,
        out_specs=[HBM, VMEM],
        out_shape=[f32(*FIELD), f32(ROWS // 2, PLANE // 4)],
        scratch_shapes=[GHOSTS]
        + [SHEET] * 4
        + GATHERED
        + [scratch(COLS, ROWS, LANES), pltpu.SemaphoreType.DMA],
        compiler_params=params(16),
        cost_estimate=cost(1 << 24, 10 << 20),
        name="last",
    )(mine, lists, *turned, wk, wf, dg, kept, sheets, ends, ya)


def pair_swap(values, stride):
    count = lax.axis_size("owner")
    return lax.ppermute(values, "owner", [(i, i ^ stride) for i in range(count)])


def odd_pair_swap(values):
    count = lax.axis_size("owner")
    return lax.ppermute(values, "owner", [(i, ((i - 1) ^ 1) + 1) for i in range(1, count - 1)])


def in_hbm(values):
    return pltpu.with_memory_space_constraint(values, pltpu.HBM)


def segment_swap(ys):
    return lax.all_to_all(ys, "sub", split_axis=0, concat_axis=0, tiled=True)


def body(guess, rhs, coef, occupied, neighbours, swap_slot, send_list, recv_list):
    my_owner = lax.axis_index("owner").astype(jnp.int32)
    owner = my_owner.reshape(1)
    parity = (my_owner % 2).reshape(1)
    fields = tuple(values.reshape(FIELD) for values in (guess, rhs, coef))
    fields = tuple(in_hbm(x) for x in fields)
    occupied, swap_slot = in_hbm(occupied), in_hbm(swap_slot)
    bulk = [
        pair_swap(block, 1 << bit)
        for bits in (SOON, LATE)
        for bit, block in zip(bits, swap_pack(fields, occupied, swap_slot, owner, bits))
    ]
    top, bottom, faces, mine, *merged = local(fields, occupied, neighbours, in_hbm(send_list), in_hbm(recv_list))
    (top, bottom, faces), merged = soon((top, bottom, faces), merged, bulk[:2], swap_slot, owner)
    ze, zo, ys = ends(top, bottom, faces, bulk[2:], swap_slot, owner, mine, parity)
    sent, got, ya = (ze, zo), (pair_swap(ze, 1), odd_pair_swap(zo)), segment_swap(ys)
    wk, wf, dg, v, forth, back, ys, lists = first(merged, bulk[2:], got, ya, swap_slot, owner, mine, parity)
    turned = v, forth, back
    *turned, ys, kept, sheets, ends_of = second(turned, wk, wf, sent, got, segment_swap(ys), mine, parity, lists)
    *turned, ys, sheets, ends_of = third(turned, wk, wf, kept, sheets, ends_of, segment_swap(ys), mine, lists)
    v, coarse = last(turned, wk, wf, dg, kept, sheets, ends_of, segment_swap(ys), mine, lists)
    return v.reshape(SLOTS, EDGE, PLANE), coarse.reshape(SLOTS, EDGE // 2, PLANE // 4)


def solution(mesh):
    wide, flat, single = P(("owner", "sub"), None, None), P(("owner", "sub"), None), P(("owner", "sub"))
    return jax.shard_map(
        body,
        mesh=mesh,
        in_specs=(wide, wide, wide, single, flat, flat, flat, flat),
        out_specs=(wide, wide),
        check_vma=False,
    )
```
